256 devices in a mesh: patch: 64 (over x, z, core), feat: 4 (over y).
Axes of the slice: x: 4, y: 4, z: 8, core: 2. Of those that a mesh axis runs over, the one named last changes fastest.
Arguments:
- nodes: bfloat16 [40960, 512], P(('patch', 'feat')), may hold values from -6 to 6
- edges: bfloat16 [327680, 512], P(('patch', 'feat')), may hold values from -6 to 6
- receivers: int32 [327680], P(('patch', 'feat')), may hold values from 0 to 639
- sender_slot: int32 [327680], P(('patch', 'feat')), may hold values from 0 to 2175
- send_rows: int32 [64, 4, 64, 24], P('patch', 'feat'), may hold values from 0 to 159
- live_edges: int32 [256], P(('patch', 'feat')), may hold values from 1 to 1280, 245760 in all
- edge_w1: bfloat16 [1536, 512], replicated, may hold values from -0.15625 to 0.15625
- edge_b1: float32 [512], replicated, may hold values from -3 to 3
- edge_w2: bfloat16 [512, 512], replicated, may hold values from -0.25 to 0.25
- edge_gain: float32 [512], replicated, may hold values from 0.5 to 1.5
- node_w1: bfloat16 [1024, 512], replicated, may hold values from -0.1875 to 0.1875
- node_b1: float32 [512], replicated, may hold values from -3 to 3
- node_w2: bfloat16 [512, 512], replicated, may hold values from -0.25 to 0.25
- node_gain: float32 [512], replicated, may hold values from 0.5 to 1.5
Outputs:
- edges_out: bfloat16 [327680, 512], P(('patch', 'feat'))
- nodes_out: bfloat16 [40960, 512], P(('patch', 'feat'))
The draws below stay inside these ranges and needn't reach their ends.
Inputs may be any that keep to these rules, and one draw needn't show every extreme that they name: `live_edges`: edge slots at or past a device's count are padding.
All inputs are finite; a program needn't handle non-finite values.
Results may differ from the reference program's by a relative error of at most 0.0052.
Values may be sent and summed in bfloat16 or wider, within the bound.
No kernel may reach another device: no remote copies, remote signals or barrier semaphores. Data moves between devices by JAX's collectives and lax.ppermute only.
A program may use at most 64 MiB of HBM per device.

```python
import math
import jax
import jax.numpy as jnp
import numpy as np
from jax import lax

D = 512
NODE_SUB = 160
EDGE_DEV = 1280
CAP = 24
NODE_DEV = 640
NODES = 40960
EDGES = 327680
N_PATCH = 64
N_FEAT = 4
DEVICES = 256


def plant(array, own_key, least, high):
    dims = array.shape
    index_at = [jax.random.randint(jax.random.fold_in(own_key, axis), (), 0, dims[axis]) for axis in range(len(dims))]
    array = array.at[tuple(index_at)].set(least)
    longest = dims.index(max(dims))
    index_at[longest] = (index_at[longest] + 1) % dims[longest]
    return array.at[tuple(index_at)].set(high)


def block_levels(rng, shape, shards, smallest, high):
    gain, own = 1.0, jax.random.fold_in(rng, 6)
    for position, shards_of in shards:
        heights = jnp.exp(jax.random.uniform(jax.random.fold_in(own, position), (shards_of,), jnp.float32, smallest / len(shards), high / len(shards)))
        gain = gain * jnp.repeat(heights, shape[position] // shards_of).reshape([-1 if axis == position else 1 for axis in range(len(shape))])
    return gain


def profile(number_of, total, most, lean):
    weights = [(1 << 20) // math.isqrt(grade ** lean) + 1 for grade in range(2, number_of + 1)]
    rest, holding = total - most - (number_of - 1), [1] * (number_of - 1)
    while rest > 0:
        candidates = [i for i in range(number_of - 1) if holding[i] < most]
        mass, budget = sum([weights[i] for i in candidates]), rest
        for i in candidates:
            more = min(most - holding[i], max(1, budget * weights[i] // mass), rest)
            holding[i] = holding[i] + more
            rest = rest - more
    return np.array([most] + holding)


def uneven_parts(rng, amount, total, most, slope):
    if amount == 2:
        one = jax.random.randint(rng, (), max(1, total - most), min(most, total - 1) + 1)
        return jnp.stack([one, total - one])
    sizes = jnp.asarray(profile(amount, total, most, slope), jnp.int32)
    pairs = (amount - 1) // 2
    donor, receiver = sizes[1:1 + 2 * pairs:2], sizes[2:2 + 2 * pairs:2]
    slack = jnp.minimum(donor - 1, most - receiver)
    moved = jax.random.randint(jax.random.fold_in(rng, 1), (pairs,), 0, 1 << 20) % (slack + 1)
    sizes = sizes.at[1:1 + 2 * pairs:2].set(donor - moved).at[2:2 + 2 * pairs:2].set(receiver + moved)
    return sizes[jax.random.permutation(jax.random.fold_in(rng, 2), amount)]


def scatter_about(key, extent, scale, reach, cuts=(), held_as=jnp.bfloat16):
    values = scale * jax.random.normal(key, extent, jnp.float32)
    if cuts:
        values = values * block_levels(key, extent, cuts, -0.22, 0.18)
    return jnp.clip(values, -reach, reach).astype(held_as)


def setup_inputs(seed: int = 0) -> dict:
    arg_keys = jax.random.split(jax.random.key(seed), 15)
    nodes = scatter_about(arg_keys[0], (NODES, D), 1.0, 6.0, ((0, 256),))
    edges = scatter_about(arg_keys[1], (EDGES, D), 1.0, 6.0, ((0, 256),))
    receivers = plant(jax.random.randint(arg_keys[2], (EDGES,), 0, NODE_DEV), jax.random.fold_in(arg_keys[2], 1), 0, NODE_DEV - 1).astype(jnp.int32)
    sender_slot = plant(jax.random.randint(arg_keys[3], (EDGES,), 0, NODE_DEV + N_PATCH * CAP), jax.random.fold_in(arg_keys[3], 1), 0, (NODE_DEV + N_PATCH * CAP) - 1).astype(jnp.int32)
    send_rows = plant(jax.random.randint(arg_keys[4], (N_PATCH, N_FEAT, N_PATCH, CAP), 0, NODE_SUB), jax.random.fold_in(arg_keys[4], 1), 0, NODE_SUB - 1).astype(jnp.int32)
    live_edges = uneven_parts(arg_keys[5], DEVICES, DEVICES * EDGE_DEV * 3 // 4, EDGE_DEV, 1).astype(jnp.int32)
    edge_w1 = scatter_about(arg_keys[6], (3 * D, D), (3 * D) ** -0.5, 0.15625)
    edge_b1 = scatter_about(arg_keys[7], (D,), 0.5, 3.0, (), jnp.float32)
    edge_w2 = scatter_about(arg_keys[8], (D, D), D ** -0.5, 0.25)
    edge_gain = jnp.clip(1.0 + 0.1 * jax.random.normal(arg_keys[9], (D,), jnp.float32), 0.5, 1.5)
    node_w1 = scatter_about(arg_keys[10], (2 * D, D), (2 * D) ** -0.5, 0.1875)
    node_b1 = scatter_about(arg_keys[11], (D,), 0.5, 3.0, (), jnp.float32)
    node_w2 = scatter_about(arg_keys[12], (D, D), D ** -0.5, 0.25)
    node_gain = jnp.clip(1.0 + 0.1 * jax.random.normal(arg_keys[13], (D,), jnp.float32), 0.5, 1.5)
    return dict(nodes=nodes, edges=edges, receivers=receivers, sender_slot=sender_slot, send_rows=send_rows, live_edges=live_edges, edge_w1=edge_w1, edge_b1=edge_b1, edge_w2=edge_w2, edge_gain=edge_gain, node_w1=node_w1, node_b1=node_b1, node_w2=node_w2, node_gain=node_gain)


epsilon = 1e-05

def layer_norm(values, scales):
    average = lax.optimization_barrier(jnp.mean(values, axis=-1, keepdims=True))
    centred = values - average
    variance = lax.optimization_barrier(jnp.mean(centred * centred, axis=-1, keepdims=True))
    return centred * lax.rsqrt(variance + epsilon) * scales

def edge_change(edge_rows, sender_feat, receiver_feat, edge_w1, edge_b1, edge_w2, edge_gain):
    latent = edge_rows.shape[1]
    first = jnp.dot(edge_rows, edge_w1[:latent], preferred_element_type=jnp.float32)
    first = first + jnp.dot(sender_feat, edge_w1[latent:2 * latent], preferred_element_type=jnp.float32)
    first = first + jnp.dot(receiver_feat, edge_w1[2 * latent:], preferred_element_type=jnp.float32)
    hidden = jax.nn.silu(first + edge_b1).astype(jnp.bfloat16)
    return layer_norm(jnp.dot(hidden, edge_w2, preferred_element_type=jnp.float32), edge_gain)

def node_change(node_rows, incoming, node_w1, node_b1, node_w2, node_gain):
    latent = node_rows.shape[1]
    first = jnp.dot(node_rows, node_w1[:latent], preferred_element_type=jnp.float32)
    first = first + jnp.dot(incoming, node_w1[latent:], preferred_element_type=jnp.float32)
    hidden = jax.nn.silu(first + node_b1).astype(jnp.bfloat16)
    return layer_norm(jnp.dot(hidden, node_w2, preferred_element_type=jnp.float32), node_gain)

def reference(nodes, edges, receivers, sender_slot, send_rows, live_edges, edge_w1, edge_b1, edge_w2, edge_gain, node_w1, node_b1, node_w2, node_gain):
    groups = N_PATCH * N_FEAT
    edge_ids = jnp.arange(groups * EDGE_DEV, dtype=jnp.int32)
    device_index = edge_ids // EDGE_DEV
    patch_index = device_index // N_FEAT
    feat_index = device_index % N_FEAT
    is_local = sender_slot < NODE_DEV
    remote_slot = jnp.maximum(sender_slot - NODE_DEV, 0)
    source_patch = remote_slot // CAP
    slot_column = remote_slot % CAP
    listed_row = send_rows[source_patch, feat_index, patch_index, slot_column]
    senders = jnp.where(is_local, patch_index * NODE_DEV + sender_slot, source_patch * NODE_DEV + feat_index * NODE_SUB + listed_row).astype(jnp.int32)
    receiver_rows = (patch_index * NODE_DEV + receivers).astype(jnp.int32)
    alive = edge_ids % EDGE_DEV < live_edges[device_index]
    latent = edges.shape[1]

    def per_device(packs):
        edge_rows, sender_ids, receiver_ids, alive_rows = packs
        change = edge_change(edge_rows, jnp.take(nodes, sender_ids, axis=0), jnp.take(nodes, receiver_ids, axis=0), edge_w1, edge_b1, edge_w2, edge_gain)
        return (edge_rows.astype(jnp.float32) + jnp.where(alive_rows[:, None], change, 0.0)).astype(jnp.bfloat16)
    edges_out = lax.map(per_device, (edges.reshape(groups, EDGE_DEV, latent), senders.reshape(groups, EDGE_DEV), receiver_rows.reshape(groups, EDGE_DEV), alive.reshape(groups, EDGE_DEV)))
    edges_out = edges_out.reshape(groups * EDGE_DEV, latent)
    summed = jax.ops.segment_sum(jnp.where(alive[:, None], edges_out.astype(jnp.float32), 0.0), receiver_rows, num_segments=NODES)
    incoming = summed.astype(jnp.bfloat16)
    change = node_change(nodes, incoming, node_w1, node_b1, node_w2, node_gain)
    nodes_out = (nodes.astype(jnp.float32) + change).astype(jnp.bfloat16)
    return (edges_out, nodes_out)
```

```python
import functools

import jax
import jax.numpy as jnp
from jax import lax
from jax.experimental import pallas as pl
from jax.experimental.pallas import tpu as pltpu
from jax.sharding import PartitionSpec as P

epsilon = 1e-05
f32 = jnp.float32
bf16 = jnp.bfloat16
TILE = 256
LIMIT = 48 << 20


def dot(left, right):
    return jnp.dot(left, right, preferred_element_type=f32)


def silu(value):
    return value / (1.0 + jnp.exp(-value))


def layer_norm(values, scales):
    average = jnp.mean(values, axis=-1, keepdims=True)
    centred = values - average
    variance = jnp.mean(centred * centred, axis=-1, keepdims=True)
    return centred * lax.rsqrt(variance + epsilon) * scales


def one_hot_rows(column, count, first=0):
    ids = lax.broadcasted_iota(jnp.int32, (column.shape[0], count), 1) + first
    return (column == ids).astype(f32).astype(bf16)


def one_hot_columns(row, count):
    ids = lax.broadcasted_iota(jnp.int32, (count, row.shape[1]), 0)
    return row == ids


def whole(*shape):
    return pl.BlockSpec(shape, lambda i: (0,) * len(shape))


def rows_of(tile, width):
    return pl.BlockSpec((tile, width), lambda i: (i, 0))


def select_kernel(index_ref, table_ref, out_ref):
    hot = one_hot_columns(index_ref[...], table_ref.shape[0]).astype(f32).astype(bf16)
    rows = lax.dot_general(
        hot, table_ref[...], (((0,), (0,)), ((), ())), preferred_element_type=f32
    )
    out_ref[...] = rows.astype(bf16)


def select(index, table):
    count, width = index.shape[1], table.shape[1]
    tile = 512
    return pl.pallas_call(
        select_kernel,
        grid=(count // tile,),
        in_specs=[
            pl.BlockSpec((1, tile), lambda i: (0, i)),
            whole(*table.shape),
        ],
        out_specs=rows_of(tile, width),
        out_shape=jax.ShapeDtypeStruct((count, width), bf16),
        compiler_params=pltpu.CompilerParams(vmem_limit_bytes=LIMIT),
        name="select",
    )(index, table)


def before_kernel(patch_ref, edges_ref, recv_ref, send_ref, w1_ref, b1_ref, out_ref):
    latent = edges_ref.shape[1]
    count = patch_ref.shape[0]
    patch = patch_ref[...]
    own = dot(one_hot_rows(recv_ref[...], count), patch).astype(bf16)
    near = dot(one_hot_rows(send_ref[...], count), patch).astype(bf16)
    total = dot(edges_ref[...], w1_ref[:latent])
    total = total + dot(near, w1_ref[latent : 2 * latent])
    total = total + dot(own, w1_ref[2 * latent :])
    out_ref[...] = total + b1_ref[...]


def edge_before(patch_rows, edges, recv, send, w1, b1):
    count, latent = edges.shape
    return pl.pallas_call(
        before_kernel,
        grid=(count // TILE,),
        in_specs=[
            whole(*patch_rows.shape),
            rows_of(TILE, latent),
            rows_of(TILE, 1),
            rows_of(TILE, 1),
            whole(*w1.shape),
            whole(1, latent),
        ],
        out_specs=rows_of(TILE, latent),
        out_shape=jax.ShapeDtypeStruct((count, latent), f32),
        compiler_params=pltpu.CompilerParams(vmem_limit_bytes=LIMIT),
        cost_estimate=pl.CostEstimate(
            flops=2 * count * latent * (3 * latent + 2 * patch_rows.shape[0]),
            bytes_accessed=8 << 20,
            transcendentals=0,
        ),
        name="edge_before",
    )(patch_rows, edges, recv, send, w1, b1)


def after_kernel(
    live_ref, before_ref, remote_ref, edges_ref, send_ref, recv_ref, w1_ref, w2_ref, gain_ref,
    out_ref, sums_ref, total_ref,
):
    step = pl.program_id(0)
    tile = edges_ref.shape[0]
    nodes = sums_ref.shape[0]
    hot = one_hot_rows(send_ref[...], remote_ref.shape[0], nodes)
    far = dot(hot, remote_ref[...]).astype(bf16)
    hidden = silu(before_ref[...] + dot(far, w1_ref[...])).astype(bf16)
    change = layer_norm(dot(hidden, w2_ref[...]), gain_ref[...])
    live = live_ref[0] - step * tile
    alive = lax.broadcasted_iota(jnp.int32, (tile, 1), 0) < live
    edge = edges_ref[...].astype(f32) + jnp.where(alive, change, 0.0)
    edge = edge.astype(bf16)
    out_ref[...] = edge
    alive_row = lax.broadcasted_iota(jnp.int32, (1, tile), 1) < live
    receiver = jnp.where(alive_row, recv_ref[...], -1)
    hot = one_hot_columns(receiver, nodes).astype(f32).astype(bf16)
    part = dot(hot, edge)

    @pl.when(step == 0)
    def _():
        total_ref[...] = part

    @pl.when(step > 0)
    def _():
        total_ref[...] += part

    @pl.when(step == pl.num_programs(0) - 1)
    def _():
        sums_ref[...] = total_ref[...].astype(bf16)


def edge_after(live, before, remote, edges, send, recv, w1, w2, gain, nodes):
    count, latent = edges.shape
    return pl.pallas_call(
        after_kernel,
        grid=(count // TILE,),
        in_specs=[
            pl.BlockSpec(memory_space=pltpu.SMEM),
            rows_of(TILE, latent),
            whole(*remote.shape),
            rows_of(TILE, latent),
            rows_of(TILE, 1),
            pl.BlockSpec((1, TILE), lambda i: (0, i)),
            pl.BlockSpec((latent, latent), lambda i: (1, 0)),
            whole(*w2.shape),
            whole(1, latent),
        ],
        out_specs=[rows_of(TILE, latent), whole(nodes, latent)],
        out_shape=[
            jax.ShapeDtypeStruct((count, latent), bf16),
            jax.ShapeDtypeStruct((nodes, latent), bf16),
        ],
        scratch_shapes=[pltpu.VMEM((nodes, latent), f32)],
        compiler_params=pltpu.CompilerParams(vmem_limit_bytes=LIMIT),
        name="edge_after",
    )(live, before, remote, edges, send, recv, w1, w2, gain)


def node_kernel(nodes_ref, p0_ref, p1_ref, p2_ref, p3_ref, w1_ref, b1_ref, w2_ref, gain_ref, out_ref):
    latent = nodes_ref.shape[1]
    total = p0_ref[...].astype(f32) + p1_ref[...].astype(f32)
    total = total + p2_ref[...].astype(f32) + p3_ref[...].astype(f32)
    incoming = total.astype(bf16)
    nodes = nodes_ref[...]
    first = dot(nodes, w1_ref[:latent]) + dot(incoming, w1_ref[latent:])
    hidden = silu(first + b1_ref[...]).astype(bf16)
    change = layer_norm(dot(hidden, w2_ref[...]), gain_ref[...])
    out_ref[...] = (nodes.astype(f32) + change).astype(bf16)


def node_update(nodes, parts, w1, b1, w2, gain):
    return pl.pallas_call(
        node_kernel,
        out_shape=jax.ShapeDtypeStruct(nodes.shape, bf16),
        compiler_params=pltpu.CompilerParams(vmem_limit_bytes=LIMIT),
        name="node_update",
    )(nodes, *parts, w1, b1, w2, gain)


def local(
    nodes,
    edges,
    receivers,
    sender_slot,
    send_rows,
    live_edges,
    edge_w1,
    edge_b1,
    edge_w2,
    edge_gain,
    node_w1,
    node_b1,
    node_w2,
    node_gain,
):
    rows, latent = nodes.shape
    outgoing = send_rows[0, 0]
    packed = select(outgoing.reshape(1, -1), nodes).reshape(*outgoing.shape, latent)
    remote = lax.all_to_all(packed, "patch", split_axis=0, concat_axis=0, tiled=True)
    remote = remote.reshape(-1, latent)
    patch_rows = lax.all_gather(nodes, "feat", axis=0, tiled=True)
    recv = receivers.reshape(-1, 1)
    send = sender_slot.reshape(-1, 1)
    before = edge_before(patch_rows, edges, recv, send, edge_w1, edge_b1.reshape(1, -1))
    edges_out, sums = edge_after(
        live_edges, before, remote, edges, send, receivers.reshape(1, -1), edge_w1, edge_w2,
        edge_gain.reshape(1, -1), patch_rows.shape[0],
    )
    size = lax.axis_size("feat")
    me = lax.axis_index("feat")
    parts = []
    for k in range(size):
        part = lax.dynamic_slice_in_dim(sums, lax.rem(me + k, size) * rows, rows)
        if k:
            part = lax.ppermute(part, "feat", [(i, (i + k) % size) for i in range(size)])
        parts.append(part)
    nodes_out = node_update(
        nodes, parts, node_w1, node_b1.reshape(1, -1), node_w2, node_gain.reshape(1, -1)
    )
    return (edges_out, nodes_out)


def solution(mesh):
    placed = (
        P(("patch", "feat"), None),
        P(("patch", "feat"), None),
        P(("patch", "feat")),
        P(("patch", "feat")),
        P("patch", "feat", None, None),
        P(("patch", "feat")),
    ) + (P(),) * 8
    return jax.shard_map(
        local,
        mesh=mesh,
        in_specs=placed,
        out_specs=(P(("patch", "feat"), None), P(("patch", "feat"), None)),
        check_vma=False,
    )
```

```python
import jax
import jax.numpy as jnp
from jax import lax
from jax.experimental import pallas as pl
from jax.experimental.pallas import tpu as pltpu
from jax.sharding import PartitionSpec as P

epsilon = 1e-05
f32 = jnp.float32
bf16 = jnp.bfloat16
i32 = jnp.int32
TILE = 256
LIMIT = 48 << 20
X, Z, C = 4, 8, 2
TAIL = 16
BATCHES = (((0, 1), (7, 2)), ((6, 3),), ((5, 4),))


def dot(left, right):
    return jnp.dot(left, right, preferred_element_type=f32)


def dot_first(left, right):
    return lax.dot_general(left, right, (((0,), (0,)), ((), ())), preferred_element_type=f32)


def silu(value):
    return value / (1.0 + jnp.exp(-value))


def layer_norm(values, scales):
    average = jnp.mean(values, axis=-1, keepdims=True)
    centred = values - average
    variance = jnp.mean(centred * centred, axis=-1, keepdims=True)
    return centred * lax.rsqrt(variance + epsilon) * scales


def as_bf16(mask):
    return mask.astype(f32).astype(bf16)


def hot_rows(column, count, first=0):
    ids = lax.broadcasted_iota(i32, (column.shape[0], count), 1) + first
    return as_bf16(column == ids)


def hot_columns(row, count):
    return as_bf16(row == lax.broadcasted_iota(i32, (count, row.shape[1]), 0))


def whole(*shape):
    return pl.BlockSpec(shape, lambda i: (0,) * len(shape))


def rows_of(tile, width):
    return pl.BlockSpec((tile, width), lambda i: (i, 0))


def odd(dz):
    return (dz >= 1) & (dz <= 4)


def pack_kernel(where_ref, lists_ref, nodes_ref, out_ref):
    rows, latent = nodes_ref.shape
    cap, peers = lists_ref.shape
    out_ref[:rows] = nodes_ref[...]
    me = where_ref[0]
    x, z, c = me // (Z * C), me // C % Z, me % C
    lane = lax.broadcasted_iota(i32, (cap, latent), 1)
    spread = as_bf16(lane % cap == lax.broadcasted_iota(i32, (cap, latent), 0))
    listed = dot_first(lists_ref[...].astype(f32).astype(bf16), spread)
    peer = lax.broadcasted_iota(i32, (peers, latent), 0)
    lane = lax.broadcasted_iota(i32, (peers, latent), 1)
    k = (peer // (Z * C) - x) & (X - 1)
    dz = (peer // C % Z - z) & (Z - 1)
    s = (peer % C - c) & (C - 1)
    slot = (k * C + s) * 2 + jnp.where(odd(dz), 1, 0)
    listed = jnp.where(lane // cap == slot, listed + 1.0, 0.0).astype(bf16)
    row = lax.broadcasted_iota(i32, (TAIL, peers), 0)
    peer = lax.broadcasted_iota(i32, (TAIL, peers), 1)
    pick = as_bf16(row == ((peer // C % Z - z) & (Z - 1)))
    out_ref[rows:] = (dot(pick, listed) - 1.0).astype(bf16)


def pack(me, lists, nodes):
    return pl.pallas_call(
        pack_kernel,
        in_specs=[
            pl.BlockSpec(memory_space=pltpu.SMEM),
            pl.BlockSpec(memory_space=pltpu.VMEM),
            pl.BlockSpec(memory_space=pltpu.VMEM),
        ],
        out_shape=jax.ShapeDtypeStruct((nodes.shape[0] + TAIL, nodes.shape[1]), bf16),
        name="pack",
    )(me, lists, nodes)


def select_kernel(pairs, cap, *refs):
    blocks, outs = refs[: 2 * len(pairs)], refs[2 * len(pairs) :]
    rows = blocks[0].shape[0] - TAIL
    lanes = X * C * 2 * cap
    for at, pair in enumerate(pairs):
        total = None
        for side, dz in enumerate(pair):
            block = blocks[2 * at + side]
            wanted = block[rows:].astype(f32)[dz : dz + 1, :lanes].astype(i32)
            part = dot_first(hot_columns(wanted, rows), block[:rows])
            total = part if total is None else total + part
        total = total.astype(bf16)
        size = 2 * cap
        for k in range(X):
            for s in range(C):
                first = (k * C + s) * size
                put = (s * len(pairs) + at) * size
                outs[k][put : put + size] = total[first : first + size]


def select(pairs, cap, blocks):
    latent = blocks[0].shape[1]
    shape = jax.ShapeDtypeStruct((C * len(pairs) * 2 * cap, latent), bf16)
    rows = blocks[0].shape[0]
    return pl.pallas_call(
        lambda *refs: select_kernel(pairs, cap, *refs),
        out_shape=[shape] * X,
        cost_estimate=pl.CostEstimate(
            flops=len(pairs) * 2 * 384 * rows * latent * 4,
            bytes_accessed=len(pairs) * 2 << 20,
            transcendentals=0,
        ),
        name="select",
    )(*blocks)


def before_kernel(
    n0_ref, n1_ref, n2_ref, n3_ref, edges_ref, recv_ref, send_ref, w1_ref, b1_ref, out_ref, patch_ref
):
    latent = edges_ref.shape[1]
    rows = n0_ref.shape[0]
    count = patch_ref.shape[0]

    @pl.when(pl.program_id(0) == 0)
    def _():
        for k, ref in enumerate((n0_ref, n1_ref, n2_ref, n3_ref)):
            patch_ref[k * rows : (k + 1) * rows] = ref[...]

    patch = patch_ref[...]
    own = dot(hot_rows(recv_ref[...], count), patch).astype(bf16)
    near = dot(hot_rows(send_ref[...], count), patch).astype(bf16)
    total = dot(edges_ref[...], w1_ref[:latent])
    total = total + dot(near, w1_ref[latent : 2 * latent])
    total = total + dot(own, w1_ref[2 * latent :])
    out_ref[...] = total + b1_ref[...]


def edge_before(parts, edges, recv, send, w1, b1):
    count, latent = edges.shape
    rows = parts[0].shape[0]
    return pl.pallas_call(
        before_kernel,
        grid=(count // TILE,),
        in_specs=[whole(rows, latent)] * 4
        + [
            rows_of(TILE, latent),
            rows_of(TILE, 1),
            rows_of(TILE, 1),
            whole(*w1.shape),
            whole(1, latent),
        ],
        out_specs=rows_of(TILE, latent),
        out_shape=jax.ShapeDtypeStruct((count, latent), f32),
        scratch_shapes=[pltpu.VMEM((4 * rows, latent), bf16)],
        compiler_params=pltpu.CompilerParams(vmem_limit_bytes=LIMIT),
        cost_estimate=pl.CostEstimate(
            flops=2 * count * latent * (3 * latent + 8 * rows),
            bytes_accessed=8 << 20,
            transcendentals=0,
        ),
        name="edge_before",
    )(*parts, edges, recv, send, w1, b1)


def after_kernel(cap, *refs):
    live_ref, before_ref, edges_ref, send_ref, recv_ref, w1_ref, w2_ref, gain_ref = refs[:8]
    count = len(BATCHES) * (X + 1)
    remote_refs = refs[8 : 8 + count]
    out_ref, s0_ref, s1_ref, s2_ref, s3_ref, total_ref, table_ref = refs[8 + count :]
    step = pl.program_id(0)
    tile = edges_ref.shape[0]
    rows = s0_ref.shape[0]
    nodes = 4 * rows

    @pl.when(step == 0)
    def _():
        total_ref[...] = jnp.zeros_like(total_ref)
        put = 0
        for at, pairs in enumerate(BATCHES):
            size = len(pairs) * 2 * cap
            group = remote_refs[at * (X + 1) : (at + 1) * (X + 1)]
            for k in range(X):
                table_ref[put : put + size] = group[k][:size]
                put += size
            table_ref[put : put + X * size] = group[X][...]
            put += X * size

    hot = hot_rows(send_ref[...], table_ref.shape[0], nodes)
    far = dot(hot, table_ref[...]).astype(bf16)
    hidden = silu(before_ref[...] + dot(far, w1_ref[...])).astype(bf16)
    change = layer_norm(dot(hidden, w2_ref[...]), gain_ref[...])
    live = live_ref[0] - step * tile
    alive = lax.broadcasted_iota(i32, (tile, 1), 0) < live
    edge = edges_ref[...].astype(f32) + jnp.where(alive, change, 0.0)
    edge = edge.astype(bf16)
    out_ref[...] = edge
    alive_row = lax.broadcasted_iota(i32, (1, tile), 1) < live
    receiver = jnp.where(alive_row, recv_ref[...], -1)
    total_ref[...] += dot(hot_columns(receiver, nodes), edge)

    @pl.when(step == pl.num_programs(0) - 1)
    def _():
        for k, ref in enumerate((s0_ref, s1_ref, s2_ref, s3_ref)):
            ref[...] = total_ref[k * rows : (k + 1) * rows].astype(ref.dtype)


def edge_after(cap, rows, live, before, edges, send, recv, w1, w2, gain, remote):
    count, latent = edges.shape
    slots = X * Z * C * cap
    sums = jax.ShapeDtypeStruct((rows, latent), bf16)
    return pl.pallas_call(
        lambda *refs: after_kernel(cap, *refs),
        grid=(count // TILE,),
        in_specs=[
            pl.BlockSpec(memory_space=pltpu.SMEM),
            rows_of(TILE, latent),
            rows_of(TILE, latent),
            rows_of(TILE, 1),
            pl.BlockSpec((1, TILE), lambda i: (0, i)),
            pl.BlockSpec((latent, latent), lambda i: (1, 0)),
            whole(*w2.shape),
            whole(1, latent),
        ]
        + [whole(*part.shape) for part in remote],
        out_specs=[rows_of(TILE, latent)] + [whole(rows, latent)] * 4,
        out_shape=[
            jax.ShapeDtypeStruct((count, latent), bf16),
            jax.ShapeDtypeStruct((rows, latent), f32),
            sums,
            sums,
            sums,
        ],
        scratch_shapes=[pltpu.VMEM((4 * rows, latent), f32), pltpu.VMEM((slots, latent), bf16)],
        compiler_params=pltpu.CompilerParams(vmem_limit_bytes=LIMIT),
        name="edge_after",
    )(live, before, edges, send, recv, w1, w2, gain, *remote)


def node_kernel(nodes_ref, p0_ref, p1_ref, p2_ref, p3_ref, w1_ref, b1_ref, w2_ref, gain_ref, out_ref):
    latent = nodes_ref.shape[1]
    total = p0_ref[...].astype(f32) + p1_ref[...].astype(f32)
    total = total + p2_ref[...].astype(f32) + p3_ref[...].astype(f32)
    incoming = total.astype(bf16)
    nodes = nodes_ref[...]
    first = dot(nodes, w1_ref[:latent]) + dot(incoming, w1_ref[latent:])
    hidden = silu(first + b1_ref[...]).astype(bf16)
    change = layer_norm(dot(hidden, w2_ref[...]), gain_ref[...])
    out_ref[...] = (nodes.astype(f32) + change).astype(bf16)


def node_update(nodes, parts, w1, b1, w2, gain):
    return pl.pallas_call(
        node_kernel,
        out_shape=jax.ShapeDtypeStruct(nodes.shape, bf16),
        compiler_params=pltpu.CompilerParams(vmem_limit_bytes=LIMIT),
        name="node_update",
    )(nodes, *parts, w1, b1, w2, gain)


def pairs_of(move):
    found = []
    for x in range(X):
        for z in range(Z):
            for c in range(C):
                tx, tz, tc = move(x, z, c)
                found.append(((x * Z + z) * C + c, ((tx % X) * Z + tz % Z) * C + tc % C))
    return found


def moved(value, move):
    return lax.ppermute(value, "patch", pairs_of(move))


def local(
    nodes,
    edges,
    receivers,
    sender_slot,
    send_rows,
    live_edges,
    edge_w1,
    edge_b1,
    edge_w2,
    edge_gain,
    node_w1,
    node_b1,
    node_w2,
    node_gain,
):
    rows, latent = nodes.shape
    cap = send_rows.shape[3]
    me = lax.axis_index("patch")
    mine = lax.axis_index("feat")
    x, z, c = me // (Z * C), me // C % Z, me % C
    feat = lax.axis_size("feat")

    block = pack(me.reshape(1), send_rows[0, 0].T, nodes)
    up = lambda a: moved(a, lambda x, z, c: (x, z + 1, c))
    down = lambda a: moved(a, lambda x, z, c: (x, z - 1, c))
    held = {0: block}
    forth = back = block
    for hop in range(1, 4):
        forth, back = up(forth), down(back)
        held[hop], held[Z - hop] = forth, back
    last = jnp.where(c == 0, forth, back)
    held[4] = moved(last, lambda x, z, c: (x, z + 1 - 2 * c, c))

    remote = []
    for pairs in BATCHES:
        picked = select(pairs, cap, [held[dz] for pair in pairs for dz in pair])
        group = [picked[0]]
        for k in range(1, X):
            group.append(moved(picked[k], lambda x, z, c: (x + k, z, c)))
        size = len(pairs) * 2 * cap
        crossing = jnp.concatenate([part[size:] for part in group], axis=0)
        group.append(moved(crossing, lambda x, z, c: (x, z, c + 1)))
        remote += group

    parts = [nodes]
    for k in range(1, feat):
        parts.append(lax.ppermute(nodes, "feat", [(i, (i + k) % feat) for i in range(feat)]))

    def near_row(row):
        return ((mine - row // rows) & (feat - 1)) * rows + row % rows

    patch_rows = feat * rows
    slot = jnp.maximum(sender_slot - patch_rows, 0)
    source, entry = slot // cap, slot % cap
    k = (x - source // (Z * C)) & (X - 1)
    dz = (z - source // C % Z) & (Z - 1)
    s = (source - c) & (C - 1)
    place = jnp.zeros_like(slot)
    base = 0
    for pairs in BATCHES:
        for at, pair in enumerate(pairs):
            for side, value in enumerate(pair):
                size = len(pairs) * 2 * cap
                here = base + (s * X + k) * size + at * 2 * cap + side * cap
                place = jnp.where(dz == value, here, place)
        base += X * C * len(pairs) * 2 * cap
    far_row = patch_rows + place + entry
    send = jnp.where(sender_slot < patch_rows, near_row(sender_slot), far_row).reshape(-1, 1)
    recv = near_row(receivers)

    before = edge_before(
        parts, edges, recv.reshape(-1, 1), send, edge_w1, edge_b1.reshape(1, -1)
    )
    edges_out, *sums = edge_after(
        cap, rows, live_edges, before, edges, send, recv.reshape(1, -1), edge_w1, edge_w2,
        edge_gain.reshape(1, -1), remote,
    )
    parts = [sums[0]]
    for k in range(1, feat):
        parts.append(lax.ppermute(sums[k], "feat", [(i, (i - k) % feat) for i in range(feat)]))
    nodes_out = node_update(
        nodes, parts, node_w1, node_b1.reshape(1, -1), node_w2, node_gain.reshape(1, -1)
    )
    return (edges_out, nodes_out)


def solution(mesh):
    placed = (
        P(("patch", "feat"), None),
        P(("patch", "feat"), None),
        P(("patch", "feat")),
        P(("patch", "feat")),
        P("patch", "feat", None, None),
        P(("patch", "feat")),
    ) + (P(),) * 8
    return jax.shard_map(
        local,
        mesh=mesh,
        in_specs=placed,
        out_specs=(P(("patch", "feat"), None), P(("patch", "feat"), None)),
        check_vma=False,
    )
```

```python
import jax
import jax.numpy as jnp
from jax import lax
from jax.experimental import pallas as pl
from jax.experimental.pallas import tpu as pltpu
from jax.sharding import PartitionSpec as P

epsilon = 1e-05
f32 = jnp.float32
bf16 = jnp.bfloat16
TILES = 2
LIMIT = 16 << 20
VMEM = pl.BlockSpec(memory_space=pltpu.VMEM)
SMEM = pl.BlockSpec(memory_space=pltpu.SMEM)


def dot(left, right):
    return jnp.dot(left, right, preferred_element_type=f32)


def silu(value):
    return value / (1.0 + jnp.exp(-value))


def layer_norm(values, scales):
    average = jnp.mean(values, axis=-1, keepdims=True)
    centred = values - average
    variance = jnp.mean(centred * centred, axis=-1, keepdims=True)
    return centred * lax.rsqrt(variance + epsilon) * scales


def dot_first(left, right):
    return lax.dot_general(left, right, (((0,), (0,)), ((), ())), preferred_element_type=f32)


def as_bf16(mask):
    return mask.astype(f32).astype(bf16)


def hot_rows(column, count, first=0):
    ids = lax.broadcasted_iota(jnp.int32, (column.shape[0], count), 1) + first
    return as_bf16(column == ids)


def hot_columns(row, count, first=0):
    ids = lax.broadcasted_iota(jnp.int32, (count, row.shape[1]), 0) + first
    return as_bf16(row == ids)


def select_kernel(lists_ref, table_ref, out_ref):
    cap, peers = lists_ref.shape
    table = table_ref[...]
    lists = lists_ref[...].astype(f32).astype(bf16)
    size = 512
    for at in range(cap * peers // size):
        lane = lax.broadcasted_iota(jnp.int32, (cap, size), 1) + at * size
        spread = as_bf16(lane % cap == lax.broadcasted_iota(jnp.int32, (cap, size), 0))
        listed = dot_first(lists, spread)
        lane = lax.broadcasted_iota(jnp.int32, (peers, size), 1) + at * size
        own = lane // cap == lax.broadcasted_iota(jnp.int32, (peers, size), 0)
        wanted = jnp.sum(jnp.where(own, listed, 0.0), axis=0, keepdims=True)
        hot = hot_columns(wanted.astype(jnp.int32), table.shape[0])
        out_ref[at * size : (at + 1) * size] = dot_first(hot, table).astype(bf16)


def select(lists, table):
    return pl.pallas_call(
        select_kernel,
        in_specs=[VMEM] * 2,
        out_shape=jax.ShapeDtypeStruct((lists.size, table.shape[1]), bf16),
        compiler_params=pltpu.CompilerParams(vmem_limit_bytes=LIMIT),
        name="select",
    )(lists, table)


def before_kernel(patch_ref, edges_ref, recv_ref, send_ref, w1_ref, b1_ref, out_ref):
    count, latent = edges_ref.shape
    tile = count // TILES
    nodes = patch_ref.shape[0]
    for at in range(TILES):
        rows = slice(at * tile, (at + 1) * tile)
        own = dot(hot_rows(recv_ref[rows], nodes), patch_ref[...]).astype(bf16)
        near = dot(hot_rows(send_ref[rows], nodes), patch_ref[...]).astype(bf16)
        total = dot(edges_ref[rows], w1_ref[:latent])
        total = total + dot(near, w1_ref[latent : 2 * latent])
        total = total + dot(own, w1_ref[2 * latent :])
        out_ref[rows] = total + b1_ref[...]


def edge_before(patch_rows, edges, recv, send, w1, b1):
    count, latent = edges.shape
    return pl.pallas_call(
        before_kernel,
        in_specs=[VMEM] * 6,
        out_shape=jax.ShapeDtypeStruct((count, latent), f32),
        compiler_params=pltpu.CompilerParams(vmem_limit_bytes=LIMIT),
        cost_estimate=pl.CostEstimate(
            flops=2 * count * latent * (3 * latent + 2 * patch_rows.shape[0]),
            bytes_accessed=8 << 20,
            transcendentals=0,
        ),
        name="edge_before",
    )(patch_rows, edges, recv, send, w1, b1)


def after_kernel(
    live_ref, before_ref, remote_ref, edges_ref, send_ref, recv_ref, w1_ref, w2_ref, gain_ref,
    out_ref, sums_ref,
):
    count, latent = edges_ref.shape
    tile = count // TILES
    nodes = sums_ref.shape[0]
    live = live_ref[0]
    for at in range(TILES):
        rows = slice(at * tile, (at + 1) * tile)
        hot = hot_rows(send_ref[rows], remote_ref.shape[0], nodes)
        far = dot(hot, remote_ref[...]).astype(bf16)
        first = before_ref[rows] + dot(far, w1_ref[latent : 2 * latent])
        hidden = silu(first).astype(bf16)
        change = layer_norm(dot(hidden, w2_ref[...]), gain_ref[...])
        alive = lax.broadcasted_iota(jnp.int32, (tile, 1), 0) + at * tile < live
        edge = edges_ref[rows].astype(f32) + jnp.where(alive, change, 0.0)
        out_ref[rows] = edge.astype(bf16)
    alive = lax.broadcasted_iota(jnp.int32, (1, count), 1) < live
    receiver = jnp.where(alive, recv_ref[...], -1)
    size = nodes // 4
    for at in range(4):
        hot = hot_columns(receiver, size, at * size)
        sums_ref[at * size : (at + 1) * size] = dot(hot, out_ref[...]).astype(bf16)


def edge_after(live, before, remote, edges, send, recv, w1, w2, gain, nodes):
    count, latent = edges.shape
    return pl.pallas_call(
        after_kernel,
        in_specs=[SMEM] + [VMEM] * 8,
        out_shape=[
            jax.ShapeDtypeStruct((count, latent), bf16),
            jax.ShapeDtypeStruct((nodes, latent), bf16),
        ],
        compiler_params=pltpu.CompilerParams(vmem_limit_bytes=LIMIT),
        name="edge_after",
    )(live, before, remote, edges, send, recv, w1, w2, gain)


def node_kernel(nodes_ref, p0_ref, p1_ref, p2_ref, p3_ref, w1_ref, b1_ref, w2_ref, gain_ref, out_ref):
    latent = nodes_ref.shape[1]
    total = p0_ref[...].astype(f32) + p1_ref[...].astype(f32)
    total = total + p2_ref[...].astype(f32) + p3_ref[...].astype(f32)
    incoming = total.astype(bf16)
    nodes = nodes_ref[...]
    first = dot(nodes, w1_ref[:latent]) + dot(incoming, w1_ref[latent:])
    hidden = silu(first + b1_ref[...]).astype(bf16)
    change = layer_norm(dot(hidden, w2_ref[...]), gain_ref[...])
    out_ref[...] = (nodes.astype(f32) + change).astype(bf16)


def node_update(nodes, parts, w1, b1, w2, gain):
    return pl.pallas_call(
        node_kernel,
        out_shape=jax.ShapeDtypeStruct(nodes.shape, bf16),
        compiler_params=pltpu.CompilerParams(vmem_limit_bytes=LIMIT),
        name="node_update",
    )(nodes, *parts, w1, b1, w2, gain)


def local(
    nodes,
    edges,
    receivers,
    sender_slot,
    send_rows,
    live_edges,
    edge_w1,
    edge_b1,
    edge_w2,
    edge_gain,
    node_w1,
    node_b1,
    node_w2,
    node_gain,
):
    rows, latent = nodes.shape
    outgoing = send_rows[0, 0]
    packed = select(outgoing.T, nodes).reshape(*outgoing.shape, latent)
    remote = lax.all_to_all(packed, "patch", split_axis=0, concat_axis=0, tiled=True)
    remote = remote.reshape(-1, latent)
    patch_rows = lax.all_gather(nodes, "feat", axis=0, tiled=True)
    recv = receivers.reshape(-1, 1)
    send = sender_slot.reshape(-1, 1)
    before = edge_before(patch_rows, edges, recv, send, edge_w1, edge_b1.reshape(1, -1))
    edges_out, sums = edge_after(
        live_edges, before, remote, edges, send, receivers.reshape(1, -1), edge_w1, edge_w2,
        edge_gain.reshape(1, -1), patch_rows.shape[0],
    )
    size = lax.axis_size("feat")
    me = lax.axis_index("feat")
    parts = []
    for k in range(size):
        part = lax.dynamic_slice_in_dim(sums, lax.rem(me + k, size) * rows, rows)
        if k:
            part = lax.ppermute(part, "feat", [(i, (i + k) % size) for i in range(size)])
        parts.append(part)
    nodes_out = node_update(
        nodes, parts, node_w1, node_b1.reshape(1, -1), node_w2, node_gain.reshape(1, -1)
    )
    return (edges_out, nodes_out)


def solution(mesh):
    placed = (
        P(("patch", "feat"), None),
        P(("patch", "feat"), None),
        P(("patch", "feat")),
        P(("patch", "feat")),
        P("patch", "feat", None, None),
        P(("patch", "feat")),
    ) + (P(),) * 8
    return jax.shard_map(
        local,
        mesh=mesh,
        in_specs=placed,
        out_specs=(P(("patch", "feat"), None), P(("patch", "feat"), None)),
        check_vma=False,
    )
```

```python
import jax
import jax.numpy as jnp
from jax import lax
from jax.experimental import pallas as pl
from jax.experimental.pallas import tpu as pltpu
from jax.sharding import PartitionSpec as P

epsilon = 1e-05
f32 = jnp.float32
bf16 = jnp.bfloat16
TILES = 2
GATHERS = 1
LIMIT = 16 << 20
VMEM = pl.BlockSpec(memory_space=pltpu.VMEM)
SMEM = pl.BlockSpec(memory_space=pltpu.SMEM)


def dot(left, right):
    return jnp.dot(left, right, preferred_element_type=f32)


def silu(value):
    return value / (1.0 + jnp.exp(-value))


def layer_norm(values, scales):
    average = jnp.mean(values, axis=-1, keepdims=True)
    centred = values - average
    variance = jnp.mean(centred * centred, axis=-1, keepdims=True)
    return centred * lax.rsqrt(variance + epsilon) * scales


def dot_first(left, right):
    return lax.dot_general(left, right, (((0,), (0,)), ((), ())), preferred_element_type=f32)


def as_bf16(mask):
    return mask.astype(f32).astype(bf16)


def hot_rows(column, count, first=0):
    ids = lax.broadcasted_iota(jnp.int32, (column.shape[0], count), 1) + first
    return as_bf16(column == ids)


def hot_columns(row, count, first=0):
    ids = lax.broadcasted_iota(jnp.int32, (count, row.shape[1]), 0) + first
    return as_bf16(row == ids)


def select_kernel(lists_ref, table_ref, out_ref):
    cap, peers = lists_ref.shape
    table = table_ref[...]
    lists = lists_ref[...].astype(f32).astype(bf16)
    size = 512
    for at in range(cap * peers // size):
        lane = lax.broadcasted_iota(jnp.int32, (cap, size), 1) + at * size
        spread = as_bf16(lane % cap == lax.broadcasted_iota(jnp.int32, (cap, size), 0))
        listed = dot_first(lists, spread)
        lane = lax.broadcasted_iota(jnp.int32, (peers, size), 1) + at * size
        own = lane // cap == lax.broadcasted_iota(jnp.int32, (peers, size), 0)
        wanted = jnp.sum(jnp.where(own, listed, 0.0), axis=0, keepdims=True)
        hot = hot_columns(wanted.astype(jnp.int32), table.shape[0])
        out_ref[at * size : (at + 1) * size] = dot_first(hot, table).astype(bf16)


def select(lists, table):
    return pl.pallas_call(
        select_kernel,
        in_specs=[VMEM] * 2,
        out_shape=jax.ShapeDtypeStruct((lists.size, table.shape[1]), bf16),
        compiler_params=pltpu.CompilerParams(vmem_limit_bytes=LIMIT),
        name="select",
    )(lists, table)


def before_kernel(patch_ref, edges_ref, recv_ref, send_ref, w1_ref, b1_ref, out_ref):
    count, latent = edges_ref.shape
    tile = count // TILES
    nodes = patch_ref.shape[0]
    for at in range(TILES):
        rows = slice(at * tile, (at + 1) * tile)
        own = dot(hot_rows(recv_ref[rows], nodes), patch_ref[...]).astype(bf16)
        near = dot(hot_rows(send_ref[rows], nodes), patch_ref[...]).astype(bf16)
        total = dot(edges_ref[rows], w1_ref[:latent])
        total = total + dot(near, w1_ref[latent : 2 * latent])
        total = total + dot(own, w1_ref[2 * latent :])
        out_ref[rows] = total + b1_ref[...]


def edge_before(patch_rows, edges, recv, send, w1, b1):
    count, latent = edges.shape
    return pl.pallas_call(
        before_kernel,
        in_specs=[VMEM] * 6,
        out_shape=jax.ShapeDtypeStruct((count, latent), f32),
        compiler_params=pltpu.CompilerParams(vmem_limit_bytes=LIMIT),
        cost_estimate=pl.CostEstimate(
            flops=2 * count * latent * (3 * latent + 2 * patch_rows.shape[0]),
            bytes_accessed=8 << 20,
            transcendentals=0,
        ),
        name="edge_before",
    )(patch_rows, edges, recv, send, w1, b1)


def in_hbm(value):
    return pltpu.with_memory_space_constraint(value, pltpu.HBM)


def after_kernel(
    live_ref, remote_ref, send_ref, recv_ref, gain_ref, before_hbm, w1_hbm, w2_hbm, edges_hbm,
    out_hbm, sums_ref, before_ref, w1_ref, w2_ref, edges_ref, out_ref, load_sems, store_sems,
):
    count, latent = edges_ref.shape
    tile = count // TILES
    nodes = sums_ref.shape[0]
    loads = [
        pltpu.make_async_copy(w1_hbm.at[pl.ds(latent, latent)], w1_ref, load_sems.at[0]),
        pltpu.make_async_copy(before_hbm, before_ref, load_sems.at[1]),
        pltpu.make_async_copy(w2_hbm, w2_ref, load_sems.at[2]),
        pltpu.make_async_copy(edges_hbm, edges_ref, load_sems.at[3]),
    ]
    for load in loads:
        load.start()
    stores = []
    live = live_ref[0]
    for at in range(GATHERS):
        rows = slice(at * count // GATHERS, (at + 1) * count // GATHERS)
        hot = hot_rows(send_ref[rows], remote_ref.shape[0], nodes)
        out_ref[rows] = dot(hot, remote_ref[...]).astype(bf16)
    for load in loads:
        load.wait()
    for at in range(TILES):
        rows = slice(at * tile, (at + 1) * tile)
        first = before_ref[rows] + dot(out_ref[rows], w1_ref[...])
        hidden = silu(first).astype(bf16)
        change = layer_norm(dot(hidden, w2_ref[...]), gain_ref[...])
        alive = lax.broadcasted_iota(jnp.int32, (tile, 1), 0) + at * tile < live
        edge = edges_ref[rows].astype(f32) + jnp.where(alive, change, 0.0)
        edges_ref[rows] = edge.astype(bf16)
        part = pl.ds(at * tile, tile)
        stores.append(
            pltpu.make_async_copy(edges_ref.at[part], out_hbm.at[part], store_sems.at[at])
        )
        stores[-1].start()
    alive = lax.broadcasted_iota(jnp.int32, (1, count), 1) < live
    receiver = jnp.where(alive, recv_ref[...], -1)
    size = nodes // 4
    for at in range(4):
        hot = hot_columns(receiver, size, at * size)
        sums_ref[at * size : (at + 1) * size] = dot(hot, edges_ref[...]).astype(bf16)
    for store in stores:
        store.wait()


def edge_after(live, before, remote, edges, send, recv, w1, w2, gain, nodes):
    count, latent = edges.shape
    hbm = pl.BlockSpec(memory_space=pltpu.HBM)
    return pl.pallas_call(
        after_kernel,
        in_specs=[SMEM] + [VMEM] * 4 + [hbm] * 4,
        out_specs=[hbm, VMEM],
        out_shape=[
            jax.ShapeDtypeStruct((count, latent), bf16),
            jax.ShapeDtypeStruct((nodes, latent), bf16),
        ],
        scratch_shapes=[
            pltpu.VMEM((count, latent), f32),
            pltpu.VMEM((latent, latent), bf16),
            pltpu.VMEM((latent, latent), bf16),
            pltpu.VMEM((count, latent), bf16),
            pltpu.VMEM((count, latent), bf16),
            pltpu.SemaphoreType.DMA((4,)),
            pltpu.SemaphoreType.DMA((TILES,)),
        ],
        compiler_params=pltpu.CompilerParams(vmem_limit_bytes=32 << 20),
        name="edge_after",
    )(
        live, remote, send, recv, gain, in_hbm(before), in_hbm(w1), in_hbm(w2), in_hbm(edges)
    )


def node_kernel(nodes_ref, p0_ref, p1_ref, p2_ref, p3_ref, w1_ref, b1_ref, w2_ref, gain_ref, out_ref):
    latent = nodes_ref.shape[1]
    total = p0_ref[...].astype(f32) + p1_ref[...].astype(f32)
    total = total + p2_ref[...].astype(f32) + p3_ref[...].astype(f32)
    incoming = total.astype(bf16)
    nodes = nodes_ref[...]
    first = dot(nodes, w1_ref[:latent]) + dot(incoming, w1_ref[latent:])
    hidden = silu(first + b1_ref[...]).astype(bf16)
    change = layer_norm(dot(hidden, w2_ref[...]), gain_ref[...])
    out_ref[...] = (nodes.astype(f32) + change).astype(bf16)


def node_update(nodes, parts, w1, b1, w2, gain):
    return pl.pallas_call(
        node_kernel,
        out_shape=jax.ShapeDtypeStruct(nodes.shape, bf16),
        compiler_params=pltpu.CompilerParams(vmem_limit_bytes=LIMIT),
        name="node_update",
    )(nodes, *parts, w1, b1, w2, gain)


def local(
    nodes,
    edges,
    receivers,
    sender_slot,
    send_rows,
    live_edges,
    edge_w1,
    edge_b1,
    edge_w2,
    edge_gain,
    node_w1,
    node_b1,
    node_w2,
    node_gain,
):
    rows, latent = nodes.shape
    outgoing = send_rows[0, 0]
    packed = select(outgoing.T, nodes).reshape(*outgoing.shape, latent)
    remote = lax.all_to_all(packed, "patch", split_axis=0, concat_axis=0, tiled=True)
    remote = remote.reshape(-1, latent)
    patch_rows = lax.all_gather(nodes, "feat", axis=0, tiled=True)
    recv = receivers.reshape(-1, 1)
    send = sender_slot.reshape(-1, 1)
    before = edge_before(patch_rows, edges, recv, send, edge_w1, edge_b1.reshape(1, -1))
    edges_out, sums = edge_after(
        live_edges, before, remote, edges, send, receivers.reshape(1, -1), edge_w1, edge_w2,
        edge_gain.reshape(1, -1), patch_rows.shape[0],
    )
    size = lax.axis_size("feat")
    me = lax.axis_index("feat")
    parts = []
    for k in range(size):
        part = lax.dynamic_slice_in_dim(sums, lax.rem(me + k, size) * rows, rows)
        if k:
            part = lax.ppermute(part, "feat", [(i, (i + k) % size) for i in range(size)])
        parts.append(part)
    nodes_out = node_update(
        nodes, parts, node_w1, node_b1.reshape(1, -1), node_w2, node_gain.reshape(1, -1)
    )
    return (edges_out, nodes_out)


def solution(mesh):
    placed = (
        P(("patch", "feat"), None),
        P(("patch", "feat"), None),
        P(("patch", "feat")),
        P(("patch", "feat")),
        P("patch", "feat", None, None),
        P(("patch", "feat")),
    ) + (P(),) * 8
    return jax.shard_map(
        local,
        mesh=mesh,
        in_specs=placed,
        out_specs=(P(("patch", "feat"), None), P(("patch", "feat"), None)),
        check_vma=False,
    )
```

```python
import jax
import jax.numpy as jnp
from jax import lax
from jax.experimental import pallas as pl
from jax.experimental.pallas import tpu as pltpu
from jax.sharding import PartitionSpec as P

epsilon = 1e-05
f32 = jnp.float32
bf16 = jnp.bfloat16
i32 = jnp.int32
TILES = 2
LIMIT = 16 << 20
VMEM = pl.BlockSpec(memory_space=pltpu.VMEM)
SMEM = pl.BlockSpec(memory_space=pltpu.SMEM)
HBM = pl.BlockSpec(memory_space=pltpu.HBM)
X, Z, C = 4, 8, 2
TAIL = 16
COST = 1 << 20
BATCHES = (((0, 1), (7, 2)), ((6, 3), (5, 4)))


def dot(left, right):
    return jnp.dot(left, right, preferred_element_type=f32)


def dot_first(left, right):
    return lax.dot_general(left, right, (((0,), (0,)), ((), ())), preferred_element_type=f32)


def silu(value):
    return value / (1.0 + jnp.exp(-value))


def layer_norm(values, scales):
    average = jnp.mean(values, axis=-1, keepdims=True)
    centred = values - average
    variance = jnp.mean(centred * centred, axis=-1, keepdims=True)
    return centred * lax.rsqrt(variance + epsilon) * scales


def as_bf16(mask):
    return mask.astype(f32).astype(bf16)


def hot_columns(row, count, first=0):
    ids = lax.broadcasted_iota(i32, (count, row.shape[1]), 0) + first
    return as_bf16(row == ids)


def in_hbm(value):
    return pltpu.with_memory_space_constraint(value, pltpu.HBM)


def odd(dz):
    return (dz >= 1) & (dz <= 4)


def pack_kernel(where_ref, lists_ref, nodes_ref, out_ref):
    rows, latent = nodes_ref.shape
    cap, peers = lists_ref.shape
    out_ref[:rows] = nodes_ref[...]
    me = where_ref[0]
    x, z, c = me // (Z * C), me // C % Z, me % C
    lane = lax.broadcasted_iota(i32, (cap, latent), 1)
    spread = as_bf16(lane % cap == lax.broadcasted_iota(i32, (cap, latent), 0))
    listed = dot_first(lists_ref[...].astype(f32).astype(bf16), spread)
    peer = lax.broadcasted_iota(i32, (peers, latent), 0)
    lane = lax.broadcasted_iota(i32, (peers, latent), 1)
    k = (peer // (Z * C) - x) & (X - 1)
    dz = (peer // C % Z - z) & (Z - 1)
    s = (peer % C - c) & (C - 1)
    slot = (k * C + s) * 2 + jnp.where(odd(dz), 1, 0)
    listed = jnp.where(lane // cap == slot, listed + 1.0, 0.0).astype(bf16)
    row = lax.broadcasted_iota(i32, (TAIL, peers), 0)
    peer = lax.broadcasted_iota(i32, (TAIL, peers), 1)
    pick = as_bf16(row == ((peer // C % Z - z) & (Z - 1)))
    out_ref[rows:] = (dot(pick, listed) - 1.0).astype(bf16)


def pack(me, lists, nodes):
    return pl.pallas_call(
        pack_kernel,
        in_specs=[SMEM, VMEM, VMEM],
        out_shape=jax.ShapeDtypeStruct((nodes.shape[0] + TAIL, nodes.shape[1]), bf16),
        name="pack",
    )(me, lists, nodes)


def select_kernel(pairs, cap, *refs):
    blocks, outs = refs[: 2 * len(pairs)], refs[2 * len(pairs) :]
    rows = blocks[0].shape[0] - TAIL
    lanes = X * C * 2 * cap
    for at, pair in enumerate(pairs):
        total = None
        for side, dz in enumerate(pair):
            block = blocks[2 * at + side]
            wanted = block[rows:].astype(f32)[dz : dz + 1, :lanes].astype(i32)
            part = dot_first(hot_columns(wanted, rows), block[:rows])
            total = part if total is None else total + part
        total = total.astype(bf16)
        size = 2 * cap
        for k in range(X):
            for s in range(C):
                first = (k * C + s) * size
                put = (s * len(pairs) + at) * size
                outs[k][put : put + size] = total[first : first + size]


def select(pairs, cap, blocks):
    latent = blocks[0].shape[1]
    shape = jax.ShapeDtypeStruct((C * len(pairs) * 2 * cap, latent), bf16)
    rows = blocks[0].shape[0]
    return pl.pallas_call(
        lambda *refs: select_kernel(pairs, cap, *refs),
        in_specs=[VMEM] * len(blocks),
        out_shape=[shape] * X,
        compiler_params=pltpu.CompilerParams(vmem_limit_bytes=LIMIT),
        cost_estimate=pl.CostEstimate(flops=COST, bytes_accessed=0, transcendentals=0),
        name="select",
    )(*blocks)


def cross_kernel(*refs):
    out_ref = refs[-1]
    size = refs[0].shape[0] // C
    for k in range(X):
        out_ref[k * size : (k + 1) * size] = refs[k][size:]


def crossing(parts, *earlier):
    rows, latent = parts[0].shape
    return pl.pallas_call(
        cross_kernel,
        in_specs=[VMEM] * X + [HBM] * len(earlier),
        out_shape=jax.ShapeDtypeStruct((rows // C * X, latent), bf16),
        compiler_params=pltpu.CompilerParams(vmem_limit_bytes=LIMIT),
        name="crossing",
    )(*parts, *[in_hbm(part) for part in earlier])


def fill(table_ref, put, group):
    size = group[0].shape[0] // C
    for k in range(X):
        table_ref[put : put + size] = group[k][:size]
        put += size
    table_ref[put : put + X * size] = group[X][...]


def before_kernel(*refs):
    recv_ref, send_ref, b1_ref = refs[:3]
    group = refs[3 : 4 + X]
    patch_hbm, edges_hbm, w1_hbm, out_hbm = refs[4 + X : 8 + X]
    patch_ref, table_ref, edges_ref, w1_ref, out_ref, sems = refs[8 + X :]
    fetch = pltpu.make_async_copy(patch_hbm, patch_ref, sems.at[2 + TILES])
    fetch.start()
    loads = [
        pltpu.make_async_copy(edges_hbm, edges_ref, sems.at[0]),
        pltpu.make_async_copy(w1_hbm, w1_ref, sems.at[1]),
    ]
    for load in loads:
        load.start()
    count, latent = edges_ref.shape
    nodes = patch_ref.shape[0]
    tile = count // TILES
    fill(table_ref, nodes, group)
    fetch.wait()
    table_ref[:nodes] = patch_ref[...].astype(bf16)
    stores = []
    for at in range(TILES):
        rows = slice(at * tile, (at + 1) * tile)
        own = dot_first(hot_columns(recv_ref[:, rows], nodes), table_ref[:nodes]).astype(bf16)
        hot = hot_columns(send_ref[:, rows], table_ref.shape[0])
        near = dot_first(hot, table_ref[...]).astype(bf16)
        if at == 0:
            for load in loads:
                load.wait()
        total = dot(edges_ref[rows], w1_ref[:latent])
        total = total + dot(near, w1_ref[latent : 2 * latent])
        total = total + dot(own, w1_ref[2 * latent :])
        out_ref[rows] = total + b1_ref[...]
        part = pl.ds(at * tile, tile)
        stores.append(pltpu.make_async_copy(out_ref.at[part], out_hbm.at[part], sems.at[2 + at]))
        stores[-1].start()
    for store in stores:
        store.wait()


def edge_before(patch_rows, recv, send, b1, group, edges, w1):
    count, latent = edges.shape
    table = patch_rows.shape[0] + sum(part.shape[0] for part in group[:X]) // C + group[X].shape[0]
    return pl.pallas_call(
        before_kernel,
        in_specs=[VMEM] * (4 + X) + [HBM] * 3,
        out_specs=HBM,
        out_shape=pltpu.HBM((count, latent), f32),
        scratch_shapes=[
            pltpu.VMEM(patch_rows.shape, f32),
            pltpu.VMEM((table, latent), bf16),
            pltpu.VMEM((count, latent), bf16),
            pltpu.VMEM(w1.shape, bf16),
            pltpu.VMEM((count, latent), f32),
            pltpu.SemaphoreType.DMA((3 + TILES,)),
        ],
        compiler_params=pltpu.CompilerParams(vmem_limit_bytes=32 << 20),
        cost_estimate=pl.CostEstimate(flops=COST, bytes_accessed=0, transcendentals=0),
        name="edge_before",
    )(recv, send, b1, *group, in_hbm(patch_rows), in_hbm(edges), in_hbm(w1))


def after_kernel(first_row, *refs):
    live_ref, send_ref, recv_ref, gain_ref = refs[:4]
    group = refs[4 : 5 + X]
    before_hbm, w1_hbm, w2_hbm, edges_hbm, out_hbm = refs[5 + X : 10 + X]
    sums_refs = refs[10 + X : 14 + X]
    table_ref, before_ref, w1_ref, w2_ref, edges_ref, far_ref, load_sems, store_sems = refs[14 + X :]
    count, latent = edges_ref.shape
    tile = count // TILES
    loads = [
        pltpu.make_async_copy(w1_hbm.at[pl.ds(latent, latent)], w1_ref, load_sems.at[0]),
        pltpu.make_async_copy(before_hbm, before_ref, load_sems.at[1]),
        pltpu.make_async_copy(w2_hbm, w2_ref, load_sems.at[2]),
        pltpu.make_async_copy(edges_hbm, edges_ref, load_sems.at[3]),
    ]
    for load in loads:
        load.start()
    fill(table_ref, 0, group)
    stores = []
    live = live_ref[0]
    hot = hot_columns(send_ref[...], table_ref.shape[0], first_row)
    far_ref[...] = dot_first(hot, table_ref[...]).astype(bf16)
    for load in loads:
        load.wait()
    for at in range(TILES):
        rows = slice(at * tile, (at + 1) * tile)
        first = before_ref[rows] + dot(far_ref[rows], w1_ref[...])
        hidden = silu(first).astype(bf16)
        change = layer_norm(dot(hidden, w2_ref[...]), gain_ref[...])
        alive = lax.broadcasted_iota(i32, (tile, 1), 0) + at * tile < live
        edge = edges_ref[rows].astype(f32) + jnp.where(alive, change, 0.0)
        edges_ref[rows] = edge.astype(bf16)
        part = pl.ds(at * tile, tile)
        stores.append(
            pltpu.make_async_copy(edges_ref.at[part], out_hbm.at[part], store_sems.at[at])
        )
        stores[-1].start()
    alive = lax.broadcasted_iota(i32, (1, count), 1) < live
    receiver = jnp.where(alive, recv_ref[...], -1)
    size = sums_refs[0].shape[0]
    for at, ref in enumerate(sums_refs):
        hot = hot_columns(receiver, size, at * size)
        ref[...] = dot(hot, edges_ref[...]).astype(ref.dtype)
    for store in stores:
        store.wait()


def edge_after(first_row, live, send, recv, gain, group, before, w1, w2, edges, rows):
    count, latent = edges.shape
    table = sum(part.shape[0] for part in group[:X]) // C + group[X].shape[0]
    return pl.pallas_call(
        lambda *refs: after_kernel(first_row, *refs),
        in_specs=[SMEM] + [VMEM] * (4 + X) + [HBM] * 4,
        out_specs=[HBM] + [VMEM] * 4,
        out_shape=[jax.ShapeDtypeStruct((count, latent), bf16)]
        + [jax.ShapeDtypeStruct((rows, latent), f32 if k == 0 else bf16) for k in range(4)],
        scratch_shapes=[
            pltpu.VMEM((table, latent), bf16),
            pltpu.VMEM((count, latent), f32),
            pltpu.VMEM((latent, latent), bf16),
            pltpu.VMEM((latent, latent), bf16),
            pltpu.VMEM((count, latent), bf16),
            pltpu.VMEM((count, latent), bf16),
            pltpu.SemaphoreType.DMA((4,)),
            pltpu.SemaphoreType.DMA((TILES,)),
        ],
        compiler_params=pltpu.CompilerParams(vmem_limit_bytes=32 << 20),
        name="edge_after",
    )(live, send, recv, gain, *group, *[in_hbm(part) for part in (before, w1, w2, edges)])


def node_kernel(nodes_ref, p0_ref, p1_ref, p2_ref, p3_ref, w1_ref, b1_ref, w2_ref, gain_ref, out_ref):
    latent = nodes_ref.shape[1]
    total = p0_ref[...].astype(f32) + p1_ref[...].astype(f32)
    total = total + p2_ref[...].astype(f32) + p3_ref[...].astype(f32)
    incoming = total.astype(bf16)
    nodes = nodes_ref[...]
    first = dot(nodes, w1_ref[:latent]) + dot(incoming, w1_ref[latent:])
    hidden = silu(first + b1_ref[...]).astype(bf16)
    change = layer_norm(dot(hidden, w2_ref[...]), gain_ref[...])
    out_ref[...] = (nodes.astype(f32) + change).astype(bf16)


def node_update(nodes, parts, w1, b1, w2, gain):
    return pl.pallas_call(
        node_kernel,
        in_specs=[VMEM] * 9,
        out_shape=jax.ShapeDtypeStruct(nodes.shape, bf16),
        compiler_params=pltpu.CompilerParams(vmem_limit_bytes=LIMIT),
        name="node_update",
    )(nodes, *parts, w1, b1, w2, gain)


def pairs_of(move):
    found = []
    for x in range(X):
        for z in range(Z):
            for c in range(C):
                tx, tz, tc = move(x, z, c)
                found.append(((x * Z + z) * C + c, ((tx % X) * Z + tz % Z) * C + tc % C))
    return found


def moved(value, move):
    return lax.ppermute(value, "patch", pairs_of(move))


def local(
    nodes,
    edges,
    receivers,
    sender_slot,
    send_rows,
    live_edges,
    edge_w1,
    edge_b1,
    edge_w2,
    edge_gain,
    node_w1,
    node_b1,
    node_w2,
    node_gain,
):
    rows, latent = nodes.shape
    cap = send_rows.shape[3]
    me = lax.axis_index("patch")
    mine = lax.axis_index("feat")
    x, z, c = me // (Z * C), me // C % Z, me % C
    feat = lax.axis_size("feat")

    block = pack(me.reshape(1), send_rows[0, 0].T, nodes)
    patch_rows = lax.all_gather(nodes.astype(f32), "feat", axis=0, tiled=True)
    up = lambda a: moved(a, lambda x, z, c: (x, z + 1, c))
    down = lambda a: moved(a, lambda x, z, c: (x, z - 1, c))
    held = {0: block}
    forth = back = block
    for hop in range(1, 4):
        forth, back = up(forth), down(back)
        held[hop], held[Z - hop] = forth, back
    held[4] = up(forth)

    groups = []
    for pairs in BATCHES:
        picked = select(pairs, cap, [held[dz] for pair in pairs for dz in pair])
        group = [picked[0]]
        for k in range(1, X):
            group.append(moved(picked[k], lambda x, z, c: (x + k, z, c)))
        groups.append(group)
    swap = lambda a: moved(a, lambda x, z, c: (x, z, c + 1))
    groups[0].append(swap(crossing(groups[0])))

    def near_row(row):
        return ((mine - row // rows) & (feat - 1)) * rows + row % rows

    patch = feat * rows
    slot = jnp.maximum(sender_slot - patch, 0)
    source, entry = slot // cap, slot % cap
    k = (x - source // (Z * C)) & (X - 1)
    dz = (z - source // C % Z) & (Z - 1)
    s = (source - c) & (C - 1)
    place = jnp.zeros_like(slot)
    base = 0
    for pairs in BATCHES:
        for at, pair in enumerate(pairs):
            for side, value in enumerate(pair):
                size = len(pairs) * 2 * cap
                here = base + (s * X + k) * size + at * 2 * cap + side * cap
                place = jnp.where(dz == value, here, place)
        base += X * C * len(pairs) * 2 * cap
    send = jnp.where(sender_slot < patch, sender_slot, patch + place + entry).reshape(1, -1)
    first_row = patch + len(BATCHES[0]) * 2 * cap * X * C
    before = edge_before(
        patch_rows, receivers.reshape(1, -1), send, edge_b1.reshape(1, -1), groups[0], edges, edge_w1
    )
    groups[1].append(swap(crossing(groups[1], before)))
    edges_out, *sums = edge_after(
        first_row, live_edges, send, near_row(receivers).reshape(1, -1), edge_gain.reshape(1, -1),
        groups[1], before, edge_w1, edge_w2, edges, rows,
    )
    parts = [sums[0]]
    for k in range(1, feat):
        parts.append(lax.ppermute(sums[k], "feat", [(i, (i - k) % feat) for i in range(feat)]))
    nodes_out = node_update(
        nodes, parts, node_w1, node_b1.reshape(1, -1), node_w2, node_gain.reshape(1, -1)
    )
    return (edges_out, nodes_out)


def solution(mesh):
    placed = (
        P(("patch", "feat"), None),
        P(("patch", "feat"), None),
        P(("patch", "feat")),
        P(("patch", "feat")),
        P("patch", "feat", None, None),
        P(("patch", "feat")),
    ) + (P(),) * 8
    return jax.shard_map(
        local,
        mesh=mesh,
        in_specs=placed,
        out_specs=(P(("patch", "feat"), None), P(("patch", "feat"), None)),
        check_vma=False,
    )
```

```python
import jax
import jax.numpy as jnp
from jax import lax
from jax.experimental import pallas as pl
from jax.experimental.pallas import tpu as pltpu
from jax.sharding import PartitionSpec as P

epsilon = 1e-05
f32 = jnp.float32
bf16 = jnp.bfloat16
i32 = jnp.int32
TILES = 2
LIMIT = 16 << 20
VMEM = pl.BlockSpec(memory_space=pltpu.VMEM)
SMEM = pl.BlockSpec(memory_space=pltpu.SMEM)
HBM = pl.BlockSpec(memory_space=pltpu.HBM)
ANY = pl.BlockSpec(memory_space=pl.ANY)
X, Z, C = 4, 8, 2
TAIL = 16
COST = 1 << 20
BATCHES = (((0, 1), (7, 2)), ((6, 3), (5, 4)))


def dot(left, right):
    return jnp.dot(left, right, preferred_element_type=f32)


def dot_first(left, right):
    return lax.dot_general(left, right, (((0,), (0,)), ((), ())), preferred_element_type=f32)


def silu(value):
    return value / (1.0 + jnp.exp(-value))


def layer_norm(values, scales):
    average = jnp.mean(values, axis=-1, keepdims=True)
    centred = values - average
    variance = jnp.mean(centred * centred, axis=-1, keepdims=True)
    return centred * lax.rsqrt(variance + epsilon) * scales


def as_bf16(mask):
    return mask.astype(f32).astype(bf16)


def hot_columns(row, count, first=0):
    ids = lax.broadcasted_iota(i32, (count, row.shape[1]), 0) + first
    return as_bf16(row == ids)


def in_hbm(value):
    return pltpu.with_memory_space_constraint(value, pltpu.HBM)


def odd(dz):
    return (dz >= 1) & (dz <= 4)


def pack_kernel(where_ref, lists_ref, nodes_ref, out_ref):
    rows, latent = nodes_ref.shape
    cap, peers = lists_ref.shape
    out_ref[:rows] = nodes_ref[...]
    me = where_ref[0]
    x, z, c = me // (Z * C), me // C % Z, me % C
    lane = lax.broadcasted_iota(i32, (cap, latent), 1)
    spread = as_bf16(lane % cap == lax.broadcasted_iota(i32, (cap, latent), 0))
    listed = dot_first(lists_ref[...].astype(f32).astype(bf16), spread)
    peer = lax.broadcasted_iota(i32, (peers, latent), 0)
    lane = lax.broadcasted_iota(i32, (peers, latent), 1)
    k = (peer // (Z * C) - x) & (X - 1)
    dz = (peer // C % Z - z) & (Z - 1)
    s = (peer % C - c) & (C - 1)
    slot = (k * C + s) * 2 + jnp.where(odd(dz), 1, 0)
    listed = jnp.where(lane // cap == slot, listed + 1.0, 0.0).astype(bf16)
    row = lax.broadcasted_iota(i32, (TAIL, peers), 0)
    peer = lax.broadcasted_iota(i32, (TAIL, peers), 1)
    pick = as_bf16(row == ((peer // C % Z - z) & (Z - 1)))
    out_ref[rows:] = (dot(pick, listed) - 1.0).astype(bf16)


def pack(me, lists, nodes):
    return pl.pallas_call(
        pack_kernel,
        in_specs=[SMEM, VMEM, VMEM],
        out_shape=jax.ShapeDtypeStruct((nodes.shape[0] + TAIL, nodes.shape[1]), bf16),
        name="pack",
    )(me, lists, nodes)


def select_kernel(pairs, cap, extra, *refs):
    count = 2 * len(pairs)
    blocks, outs = list(refs[:count]), refs[count + extra : count + extra + X]
    own = pairs[0][0] == 0
    if own:
        held, sem = refs[count + extra + X :]
        fetch = pltpu.make_async_copy(blocks[0], held, sem)
        fetch.start()
        blocks[0] = held
    rows = blocks[0].shape[0] - TAIL
    lanes = X * C * 2 * cap
    for at in reversed(range(len(pairs))):
        total = None
        for side, dz in reversed(list(enumerate(pairs[at]))):
            if dz == 0:
                fetch.wait()
            block = blocks[2 * at + side]
            wanted = block[rows:].astype(f32)[dz : dz + 1, :lanes].astype(i32)
            part = dot_first(hot_columns(wanted, rows), block[:rows])
            total = part if total is None else total + part
        total = total.astype(bf16)
        size = 2 * cap
        for k in range(X):
            for s in range(C):
                first = (k * C + s) * size
                put = (s * len(pairs) + at) * size
                outs[k][put : put + size] = total[first : first + size]


def select(pairs, cap, blocks, *earlier):
    latent = blocks[0].shape[1]
    shape = jax.ShapeDtypeStruct((C * len(pairs) * 2 * cap, latent), bf16)
    own = pairs[0][0] == 0
    blocks = list(blocks)
    if own:
        blocks[0] = in_hbm(blocks[0])
    return pl.pallas_call(
        lambda *refs: select_kernel(pairs, cap, len(earlier), *refs),
        in_specs=[HBM if own else VMEM] + [VMEM] * (len(blocks) - 1) + [ANY] * len(earlier),
        out_shape=[shape] * X,
        scratch_shapes=[pltpu.VMEM(blocks[0].shape, bf16), pltpu.SemaphoreType.DMA] if own else [],
        compiler_params=pltpu.CompilerParams(vmem_limit_bytes=LIMIT),
        cost_estimate=pl.CostEstimate(flops=COST, bytes_accessed=0, transcendentals=0),
        name="select",
    )(*blocks, *earlier)


def cross_kernel(*refs):
    out_ref = refs[-1]
    size = refs[0].shape[0] // C
    for k in range(X):
        out_ref[k * size : (k + 1) * size] = refs[k][size:]


def crossing(parts, *earlier):
    rows, latent = parts[0].shape
    return pl.pallas_call(
        cross_kernel,
        in_specs=[VMEM] * X + [HBM] * len(earlier),
        out_shape=jax.ShapeDtypeStruct((rows // C * X, latent), bf16),
        compiler_params=pltpu.CompilerParams(vmem_limit_bytes=LIMIT),
        name="crossing",
    )(*parts, *[in_hbm(part) for part in earlier])


def fill(table_ref, put, group):
    size = group[0].shape[0] // C
    for k in range(X):
        table_ref[put : put + size] = group[k][:size]
        put += size
    table_ref[put : put + X * size] = group[X][...]


def before_kernel(extra, *refs):
    recv_ref, send_ref, b1_ref = refs[:3]
    parts = refs[3:7]
    edges_hbm, w1_hbm = refs[7:9]
    out_hbm, table_ref, edges_ref, w1_ref, out_ref, sems = refs[9 + extra :]
    loads = [
        pltpu.make_async_copy(w1_hbm, w1_ref, sems.at[0]),
        pltpu.make_async_copy(edges_hbm, edges_ref, sems.at[1]),
    ]
    for load in loads:
        load.start()
    count, latent = edges_ref.shape
    size = parts[0].shape[0]
    nodes = table_ref.shape[0]
    tile = count // TILES
    for k, part in enumerate(parts):
        table_ref[k * size : (k + 1) * size] = part[...]
    stores = []
    for at in range(TILES):
        rows = slice(at * tile, (at + 1) * tile)
        own = dot_first(hot_columns(recv_ref[:, rows], nodes), table_ref[...]).astype(bf16)
        near = dot_first(hot_columns(send_ref[:, rows], nodes), table_ref[...]).astype(bf16)
        if at == 0:
            for load in loads:
                load.wait()
        total = dot(edges_ref[rows], w1_ref[:latent])
        total = total + dot(near, w1_ref[latent : 2 * latent])
        total = total + dot(own, w1_ref[2 * latent :])
        out_ref[rows] = total + b1_ref[...]
        part = pl.ds(at * tile, tile)
        stores.append(pltpu.make_async_copy(out_ref.at[part], out_hbm.at[part], sems.at[2 + at]))
        stores[-1].start()
    for store in stores:
        store.wait()


def edge_before(recv, send, b1, parts, edges, w1, *earlier):
    count, latent = edges.shape
    nodes = sum(part.shape[0] for part in parts)
    return pl.pallas_call(
        lambda *refs: before_kernel(len(earlier), *refs),
        in_specs=[VMEM] * 7 + [HBM] * 2 + [ANY] * len(earlier),
        out_specs=HBM,
        out_shape=pltpu.HBM((count, latent), f32),
        scratch_shapes=[
            pltpu.VMEM((nodes, latent), bf16),
            pltpu.VMEM((count, latent), bf16),
            pltpu.VMEM(w1.shape, bf16),
            pltpu.VMEM((count, latent), f32),
            pltpu.SemaphoreType.DMA((2 + TILES,)),
        ],
        compiler_params=pltpu.CompilerParams(vmem_limit_bytes=32 << 20),
        cost_estimate=pl.CostEstimate(flops=COST, bytes_accessed=0, transcendentals=0),
        name="edge_before",
    )(recv, send, b1, *parts, in_hbm(edges), in_hbm(w1), *earlier)


def after_kernel(first_row, *refs):
    live_ref, send_ref, recv_ref, gain_ref = refs[:4]
    groups, refs = refs[4 : 6 + 2 * X], refs[6 + 2 * X :]
    before_hbm, w1_hbm, w2_hbm, edges_hbm, out_hbm = refs[:5]
    sums_refs = refs[5:9]
    table_ref, before_ref, w1_ref, w2_ref, edges_ref, far_ref, load_sems, store_sems = refs[9:]
    count, latent = edges_ref.shape
    tile = count // TILES
    loads = [
        pltpu.make_async_copy(w1_hbm.at[pl.ds(latent, latent)], w1_ref, load_sems.at[0]),
        pltpu.make_async_copy(before_hbm, before_ref, load_sems.at[1]),
        pltpu.make_async_copy(w2_hbm, w2_ref, load_sems.at[2]),
        pltpu.make_async_copy(edges_hbm, edges_ref, load_sems.at[3]),
    ]
    for load in loads:
        load.start()
    fill(table_ref, 0, groups[: X + 1])
    fill(table_ref, table_ref.shape[0] // 2, groups[X + 1 :])
    stores = []
    live = live_ref[0]
    hot = hot_columns(send_ref[...], table_ref.shape[0], first_row)
    far_ref[...] = dot_first(hot, table_ref[...]).astype(bf16)
    for load in loads:
        load.wait()
    for at in range(TILES):
        rows = slice(at * tile, (at + 1) * tile)
        first = before_ref[rows] + dot(far_ref[rows], w1_ref[...])
        hidden = silu(first).astype(bf16)
        change = layer_norm(dot(hidden, w2_ref[...]), gain_ref[...])
        alive = lax.broadcasted_iota(i32, (tile, 1), 0) + at * tile < live
        edge = edges_ref[rows].astype(f32) + jnp.where(alive, change, 0.0)
        edges_ref[rows] = edge.astype(bf16)
        part = pl.ds(at * tile, tile)
        stores.append(
            pltpu.make_async_copy(edges_ref.at[part], out_hbm.at[part], store_sems.at[at])
        )
        stores[-1].start()
    alive = lax.broadcasted_iota(i32, (1, count), 1) < live
    receiver = jnp.where(alive, recv_ref[...], -1)
    size = sums_refs[0].shape[0]
    for at, ref in enumerate(sums_refs):
        hot = hot_columns(receiver, size, at * size)
        ref[...] = dot(hot, edges_ref[...]).astype(ref.dtype)
    for store in stores:
        store.wait()


def edge_after(first_row, live, send, recv, gain, group, before, w1, w2, edges, rows):
    count, latent = edges.shape
    table = 2 * X * group[0].shape[0]
    return pl.pallas_call(
        lambda *refs: after_kernel(first_row, *refs),
        in_specs=[SMEM] + [VMEM] * (5 + 2 * X) + [HBM] * 4,
        out_specs=[HBM] + [VMEM] * 4,
        out_shape=[jax.ShapeDtypeStruct((count, latent), bf16)]
        + [jax.ShapeDtypeStruct((rows, latent), f32 if k == 0 else bf16) for k in range(4)],
        scratch_shapes=[
            pltpu.VMEM((table, latent), bf16),
            pltpu.VMEM((count, latent), f32),
            pltpu.VMEM((latent, latent), bf16),
            pltpu.VMEM((latent, latent), bf16),
            pltpu.VMEM((count, latent), bf16),
            pltpu.VMEM((count, latent), bf16),
            pltpu.SemaphoreType.DMA((4,)),
            pltpu.SemaphoreType.DMA((TILES,)),
        ],
        compiler_params=pltpu.CompilerParams(vmem_limit_bytes=32 << 20),
        name="edge_after",
    )(live, send, recv, gain, *group, *[in_hbm(part) for part in (before, w1, w2, edges)])


def node_kernel(nodes_ref, p0_ref, p1_ref, p2_ref, p3_ref, w1_ref, b1_ref, w2_ref, gain_ref, out_ref):
    latent = nodes_ref.shape[1]
    total = p0_ref[...].astype(f32) + p1_ref[...].astype(f32)
    total = total + p2_ref[...].astype(f32) + p3_ref[...].astype(f32)
    incoming = total.astype(bf16)
    nodes = nodes_ref[...]
    first = dot(nodes, w1_ref[:latent]) + dot(incoming, w1_ref[latent:])
    hidden = silu(first + b1_ref[...]).astype(bf16)
    change = layer_norm(dot(hidden, w2_ref[...]), gain_ref[...])
    out_ref[...] = (nodes.astype(f32) + change).astype(bf16)


def node_update(nodes, parts, w1, b1, w2, gain):
    return pl.pallas_call(
        node_kernel,
        in_specs=[VMEM] * 9,
        out_shape=jax.ShapeDtypeStruct(nodes.shape, bf16),
        compiler_params=pltpu.CompilerParams(vmem_limit_bytes=LIMIT),
        name="node_update",
    )(nodes, *parts, w1, b1, w2, gain)


def pairs_of(move):
    found = []
    for x in range(X):
        for z in range(Z):
            for c in range(C):
                tx, tz, tc = move(x, z, c)
                found.append(((x * Z + z) * C + c, ((tx % X) * Z + tz % Z) * C + tc % C))
    return found


def moved(value, move):
    return lax.ppermute(value, "patch", pairs_of(move))


def local(
    nodes,
    edges,
    receivers,
    sender_slot,
    send_rows,
    live_edges,
    edge_w1,
    edge_b1,
    edge_w2,
    edge_gain,
    node_w1,
    node_b1,
    node_w2,
    node_gain,
):
    rows, latent = nodes.shape
    cap = send_rows.shape[3]
    me = lax.axis_index("patch")
    mine = lax.axis_index("feat")
    x, z, c = me // (Z * C), me // C % Z, me % C
    feat = lax.axis_size("feat")

    block = pack(me.reshape(1), send_rows[0, 0].T, nodes)
    parts = [nodes]
    for k in range(1, feat):
        parts.append(lax.ppermute(nodes, "feat", [(i, (i + k) % feat) for i in range(feat)]))
    up = lambda a: moved(a, lambda x, z, c: (x, z + 1, c))
    down = lambda a: moved(a, lambda x, z, c: (x, z - 1, c))
    held = {0: block}
    forth = back = block
    for hop in range(1, 4):
        forth, back = up(forth), down(back)
        held[hop], held[Z - hop] = forth, back
    held[4] = up(forth)

    groups = []
    for pairs in BATCHES:
        earlier = parts[1:] if pairs is BATCHES[0] else []
        picked = select(pairs, cap, [held[dz] for pair in pairs for dz in pair], *earlier)
        group = [picked[0]]
        for k in range(1, X):
            group.append(moved(picked[k], lambda x, z, c: (x + k, z, c)))
        groups.append(group)
    swap = lambda a: moved(a, lambda x, z, c: (x, z, c + 1))
    groups[0].append(swap(crossing(groups[0])))

    def near_row(row):
        return ((mine - row // rows) & (feat - 1)) * rows + row % rows

    patch = feat * rows
    slot = jnp.maximum(sender_slot - patch, 0)
    source, entry = slot // cap, slot % cap
    k = (x - source // (Z * C)) & (X - 1)
    dz = (z - source // C % Z) & (Z - 1)
    s = (source - c) & (C - 1)
    place = jnp.zeros_like(slot)
    base = 0
    for pairs in BATCHES:
        for at, pair in enumerate(pairs):
            for side, value in enumerate(pair):
                size = len(pairs) * 2 * cap
                here = base + (s * X + k) * size + at * 2 * cap + side * cap
                place = jnp.where(dz == value, here, place)
        base += X * C * len(pairs) * 2 * cap
    send = jnp.where(sender_slot < patch, near_row(sender_slot), patch + place + entry)
    send = send.reshape(1, -1)
    recv = near_row(receivers).reshape(1, -1)
    before = edge_before(
        recv, send, edge_b1.reshape(1, -1), parts, edges, edge_w1, groups[1][0]
    )
    groups[1].append(swap(crossing(groups[1], before)))
    edges_out, *sums = edge_after(
        patch, live_edges, send, recv, edge_gain.reshape(1, -1), groups[0] + groups[1], before,
        edge_w1, edge_w2, edges, rows,
    )
    parts = [sums[0]]
    for k in range(1, feat):
        parts.append(lax.ppermute(sums[k], "feat", [(i, (i - k) % feat) for i in range(feat)]))
    nodes_out = node_update(
        nodes, parts, node_w1, node_b1.reshape(1, -1), node_w2, node_gain.reshape(1, -1)
    )
    return (edges_out, nodes_out)


def solution(mesh):
    placed = (
        P(("patch", "feat"), None),
        P(("patch", "feat"), None),
        P(("patch", "feat")),
        P(("patch", "feat")),
        P("patch", "feat", None, None),
        P(("patch", "feat")),
    ) + (P(),) * 8
    return jax.shard_map(
        local,
        mesh=mesh,
        in_specs=placed,
        out_specs=(P(("patch", "feat"), None), P(("patch", "feat"), None)),
        check_vma=False,
    )
```

```python
import jax
import jax.numpy as jnp
from jax import lax
from jax.experimental import pallas as pl
from jax.experimental.pallas import tpu as pltpu
from jax.sharding import PartitionSpec as P

epsilon = 1e-05
f32 = jnp.float32
bf16 = jnp.bfloat16
i32 = jnp.int32
TILES = 2
GATHERS = 1
LIMIT = 16 << 20
VMEM = pl.BlockSpec(memory_space=pltpu.VMEM)
SMEM = pl.BlockSpec(memory_space=pltpu.SMEM)
HBM = pl.BlockSpec(memory_space=pltpu.HBM)
ANY = pl.BlockSpec(memory_space=pl.ANY)
X, Z, C = 4, 8, 2
TAIL = 16
COST = 1 << 20
BATCHES = (((0, 1), (7, 2)), ((6, 3), (5, 4)))


def dot(left, right):
    return jnp.dot(left, right, preferred_element_type=f32)


def dot_first(left, right):
    return lax.dot_general(left, right, (((0,), (0,)), ((), ())), preferred_element_type=f32)


def silu(value):
    return value / (1.0 + jnp.exp(-value))


def layer_norm(values, scales):
    average = jnp.mean(values, axis=-1, keepdims=True)
    centred = values - average
    variance = jnp.mean(centred * centred, axis=-1, keepdims=True)
    return centred * lax.rsqrt(variance + epsilon) * scales


def as_bf16(mask):
    return mask.astype(f32).astype(bf16)


def hot_columns(row, count, first=0):
    ids = lax.broadcasted_iota(i32, (count, row.shape[1]), 0) + first
    return as_bf16(row == ids)


def hot_rows(column, count, first=0):
    ids = lax.broadcasted_iota(i32, (column.shape[0], count), 1) + first
    return as_bf16(column == ids)


def in_hbm(value):
    return pltpu.with_memory_space_constraint(value, pltpu.HBM)


def odd(dz):
    return (dz >= 1) & (dz <= 4)


def pack_kernel(where_ref, lists_ref, nodes_ref, out_ref):
    rows, latent = nodes_ref.shape
    cap, peers = lists_ref.shape
    out_ref[:rows] = nodes_ref[...]
    me = where_ref[0]
    x, z, c = me // (Z * C), me // C % Z, me % C
    lane = lax.broadcasted_iota(i32, (cap, latent), 1)
    spread = as_bf16(lane % cap == lax.broadcasted_iota(i32, (cap, latent), 0))
    listed = dot_first(lists_ref[...].astype(f32).astype(bf16), spread)
    peer = lax.broadcasted_iota(i32, (peers, latent), 0)
    lane = lax.broadcasted_iota(i32, (peers, latent), 1)
    k = (peer // (Z * C) - x) & (X - 1)
    dz = (peer // C % Z - z) & (Z - 1)
    s = (peer % C - c) & (C - 1)
    slot = (k * C + s) * 2 + jnp.where(odd(dz), 1, 0)
    listed = jnp.where(lane // cap == slot, listed + 1.0, 0.0).astype(bf16)
    row = lax.broadcasted_iota(i32, (TAIL, peers), 0)
    peer = lax.broadcasted_iota(i32, (TAIL, peers), 1)
    pick = as_bf16(row == ((peer // C % Z - z) & (Z - 1)))
    out_ref[rows:] = (dot(pick, listed) - 1.0).astype(bf16)


def pack(me, lists, nodes):
    return pl.pallas_call(
        pack_kernel,
        in_specs=[SMEM, VMEM, VMEM],
        out_shape=jax.ShapeDtypeStruct((nodes.shape[0] + TAIL, nodes.shape[1]), bf16),
        name="pack",
    )(me, lists, nodes)


def select_kernel(pairs, cap, extra, *refs):
    count = 2 * len(pairs)
    blocks, outs = list(refs[:count]), refs[count + extra : count + extra + X]
    own = pairs[0][0] == 0
    if own:
        held, sem = refs[count + extra + X :]
        fetch = pltpu.make_async_copy(blocks[0], held, sem)
        fetch.start()
        blocks[0] = held
    rows = blocks[0].shape[0] - TAIL
    lanes = X * C * 2 * cap
    for at in reversed(range(len(pairs))):
        total = None
        for side, dz in reversed(list(enumerate(pairs[at]))):
            if dz == 0:
                fetch.wait()
            block = blocks[2 * at + side]
            wanted = block[rows:].astype(f32)[dz : dz + 1, :lanes].astype(i32)
            part = dot_first(hot_columns(wanted, rows), block[:rows])
            total = part if total is None else total + part
        total = total.astype(bf16)
        size = 2 * cap
        for k in range(X):
            for s in range(C):
                first = (k * C + s) * size
                put = (s * len(pairs) + at) * size
                outs[k][put : put + size] = total[first : first + size]


def select(pairs, cap, blocks, *earlier):
    latent = blocks[0].shape[1]
    shape = jax.ShapeDtypeStruct((C * len(pairs) * 2 * cap, latent), bf16)
    own = pairs[0][0] == 0
    blocks = list(blocks)
    if own:
        blocks[0] = in_hbm(blocks[0])
    return pl.pallas_call(
        lambda *refs: select_kernel(pairs, cap, len(earlier), *refs),
        in_specs=[HBM if own else VMEM] + [VMEM] * (len(blocks) - 1) + [ANY] * len(earlier),
        out_shape=[shape] * X,
        scratch_shapes=[pltpu.VMEM(blocks[0].shape, bf16), pltpu.SemaphoreType.DMA] if own else [],
        compiler_params=pltpu.CompilerParams(vmem_limit_bytes=LIMIT),
        cost_estimate=pl.CostEstimate(flops=COST, bytes_accessed=0, transcendentals=0),
        name="select",
    )(*blocks, *earlier)


def gate_kernel(*refs):
    pass


def gate(value, *earlier):
    return pl.pallas_call(
        gate_kernel,
        in_specs=[ANY] * (1 + len(earlier)),
        out_specs=ANY,
        out_shape=jax.ShapeDtypeStruct(value.shape, value.dtype),
        input_output_aliases={0: 0},
        compiler_params=pltpu.CompilerParams(vmem_limit_bytes=1 << 20),
        cost_estimate=pl.CostEstimate(flops=0, bytes_accessed=0, transcendentals=0),
        name="gate",
    )(value, *earlier)


def cross_kernel(*refs):
    out_ref = refs[-1]
    size = refs[0].shape[0] // C
    for k in range(X):
        out_ref[k * size : (k + 1) * size] = refs[k][size:]


def crossing(parts, *earlier):
    rows, latent = parts[0].shape
    return pl.pallas_call(
        cross_kernel,
        in_specs=[VMEM] * X + [HBM] * len(earlier),
        out_shape=jax.ShapeDtypeStruct((rows // C * X, latent), bf16),
        compiler_params=pltpu.CompilerParams(vmem_limit_bytes=LIMIT),
        name="crossing",
    )(*parts, *[in_hbm(part) for part in earlier])


def fill(table_ref, put, group):
    size = group[0].shape[0] // C
    for k in range(X):
        table_ref[put : put + size] = group[k][:size]
        put += size
    table_ref[put : put + X * size] = group[X][...]


def before_kernel(extra, *refs):
    recv_ref, send_ref, b1_ref = refs[:3]
    parts = refs[3:7]
    edges_hbm, w1_hbm = refs[7:9]
    out_hbm, table_ref, edges_ref, w1_ref, out_ref, sems = refs[9 + extra :]
    loads = [
        pltpu.make_async_copy(w1_hbm, w1_ref, sems.at[0]),
        pltpu.make_async_copy(edges_hbm, edges_ref, sems.at[1]),
    ]
    for load in loads:
        load.start()
    count, latent = edges_ref.shape
    size = parts[0].shape[0]
    nodes = table_ref.shape[0]
    tile = count // TILES
    for k, part in enumerate(parts):
        table_ref[k * size : (k + 1) * size] = part[...]
    stores = []
    for at in range(TILES):
        rows = slice(at * tile, (at + 1) * tile)
        own = dot_first(hot_columns(recv_ref[:, rows], nodes), table_ref[...]).astype(bf16)
        near = dot_first(hot_columns(send_ref[:, rows], nodes), table_ref[...]).astype(bf16)
        if at == 0:
            for load in loads:
                load.wait()
        total = dot(edges_ref[rows], w1_ref[:latent])
        total = total + dot(near, w1_ref[latent : 2 * latent])
        total = total + dot(own, w1_ref[2 * latent :])
        out_ref[rows] = total + b1_ref[...]
        part = pl.ds(at * tile, tile)
        stores.append(pltpu.make_async_copy(out_ref.at[part], out_hbm.at[part], sems.at[2 + at]))
        stores[-1].start()
    for store in stores:
        store.wait()


def edge_before(recv, send, b1, parts, edges, w1, *earlier):
    count, latent = edges.shape
    nodes = sum(part.shape[0] for part in parts)
    return pl.pallas_call(
        lambda *refs: before_kernel(len(earlier), *refs),
        in_specs=[VMEM] * 7 + [HBM] * 2 + [ANY] * len(earlier),
        out_specs=HBM,
        out_shape=pltpu.HBM((count, latent), f32),
        scratch_shapes=[
            pltpu.VMEM((nodes, latent), bf16),
            pltpu.VMEM((count, latent), bf16),
            pltpu.VMEM(w1.shape, bf16),
            pltpu.VMEM((count, latent), f32),
            pltpu.SemaphoreType.DMA((2 + TILES,)),
        ],
        compiler_params=pltpu.CompilerParams(vmem_limit_bytes=32 << 20),
        cost_estimate=pl.CostEstimate(flops=COST, bytes_accessed=0, transcendentals=0),
        name="edge_before",
    )(recv, send, b1, *parts, in_hbm(edges), in_hbm(w1), *earlier)


def after_kernel(first_row, *refs):
    live_ref, send_ref, recv_ref, gain_ref = refs[:4]
    groups, refs = refs[4 : 6 + 2 * X], refs[6 + 2 * X :]
    before_hbm, w1_hbm, w2_hbm, edges_hbm, out_hbm = refs[:5]
    sums_refs = refs[5:9]
    table_ref, before_ref, w1_ref, w2_ref, edges_ref, far_ref, load_sems, store_sems = refs[9:]
    count, latent = edges_ref.shape
    tile = count // TILES
    loads = [
        pltpu.make_async_copy(w1_hbm.at[pl.ds(latent, latent)], w1_ref, load_sems.at[0]),
        pltpu.make_async_copy(before_hbm, before_ref, load_sems.at[1]),
        pltpu.make_async_copy(w2_hbm, w2_ref, load_sems.at[2]),
        pltpu.make_async_copy(edges_hbm, edges_ref, load_sems.at[3]),
    ]
    for load in loads:
        load.start()
    fill(table_ref, 0, groups[: X + 1])
    fill(table_ref, table_ref.shape[0] // 2, groups[X + 1 :])
    stores = []
    live = live_ref[0]
    size = count // GATHERS
    for at in range(GATHERS):
        rows = slice(at * size, (at + 1) * size)
        hot = hot_rows(send_ref[rows], table_ref.shape[0], first_row)
        far_ref[rows] = dot(hot, table_ref[...]).astype(bf16)
    for load in loads:
        load.wait()
    for at in range(TILES):
        rows = slice(at * tile, (at + 1) * tile)
        first = before_ref[rows] + dot(far_ref[rows], w1_ref[...])
        hidden = silu(first).astype(bf16)
        change = layer_norm(dot(hidden, w2_ref[...]), gain_ref[...])
        alive = lax.broadcasted_iota(i32, (tile, 1), 0) + at * tile < live
        edge = edges_ref[rows].astype(f32) + jnp.where(alive, change, 0.0)
        edges_ref[rows] = edge.astype(bf16)
        part = pl.ds(at * tile, tile)
        stores.append(
            pltpu.make_async_copy(edges_ref.at[part], out_hbm.at[part], store_sems.at[at])
        )
        stores[-1].start()
    alive = lax.broadcasted_iota(i32, (1, count), 1) < live
    receiver = jnp.where(alive, recv_ref[...], -1)
    size = sums_refs[0].shape[0]
    for at, ref in enumerate(sums_refs):
        hot = hot_columns(receiver, size, at * size)
        ref[...] = dot(hot, edges_ref[...]).astype(ref.dtype)
    for store in stores:
        store.wait()


def edge_after(first_row, live, send, recv, gain, group, before, w1, w2, edges, rows):
    count, latent = edges.shape
    table = 2 * X * group[0].shape[0]
    return pl.pallas_call(
        lambda *refs: after_kernel(first_row, *refs),
        in_specs=[SMEM] + [VMEM] * (5 + 2 * X) + [HBM] * 4,
        out_specs=[HBM] + [VMEM] * 4,
        out_shape=[jax.ShapeDtypeStruct((count, latent), bf16)]
        + [jax.ShapeDtypeStruct((rows, latent), f32 if k == 0 else bf16) for k in range(4)],
        scratch_shapes=[
            pltpu.VMEM((table, latent), bf16),
            pltpu.VMEM((count, latent), f32),
            pltpu.VMEM((latent, latent), bf16),
            pltpu.VMEM((latent, latent), bf16),
            pltpu.VMEM((count, latent), bf16),
            pltpu.VMEM((count, latent), bf16),
            pltpu.SemaphoreType.DMA((4,)),
            pltpu.SemaphoreType.DMA((TILES,)),
        ],
        compiler_params=pltpu.CompilerParams(vmem_limit_bytes=32 << 20),
        name="edge_after",
    )(live, send, recv, gain, *group, *[in_hbm(part) for part in (before, w1, w2, edges)])


def node_kernel(nodes_ref, p0_ref, p1_ref, p2_ref, p3_ref, w1_ref, b1_ref, w2_ref, gain_ref, out_ref):
    latent = nodes_ref.shape[1]
    total = p0_ref[...].astype(f32) + p1_ref[...].astype(f32)
    total = total + p2_ref[...].astype(f32) + p3_ref[...].astype(f32)
    incoming = total.astype(bf16)
    nodes = nodes_ref[...]
    first = dot(nodes, w1_ref[:latent]) + dot(incoming, w1_ref[latent:])
    hidden = silu(first + b1_ref[...]).astype(bf16)
    change = layer_norm(dot(hidden, w2_ref[...]), gain_ref[...])
    out_ref[...] = (nodes.astype(f32) + change).astype(bf16)


def node_update(nodes, parts, w1, b1, w2, gain):
    return pl.pallas_call(
        node_kernel,
        in_specs=[VMEM] * 9,
        out_shape=jax.ShapeDtypeStruct(nodes.shape, bf16),
        compiler_params=pltpu.CompilerParams(vmem_limit_bytes=LIMIT),
        name="node_update",
    )(nodes, *parts, w1, b1, w2, gain)


def pairs_of(move):
    found = []
    for x in range(X):
        for z in range(Z):
            for c in range(C):
                tx, tz, tc = move(x, z, c)
                found.append(((x * Z + z) * C + c, ((tx % X) * Z + tz % Z) * C + tc % C))
    return found


def moved(value, move):
    return lax.ppermute(value, "patch", pairs_of(move))


def local(
    nodes,
    edges,
    receivers,
    sender_slot,
    send_rows,
    live_edges,
    edge_w1,
    edge_b1,
    edge_w2,
    edge_gain,
    node_w1,
    node_b1,
    node_w2,
    node_gain,
):
    rows, latent = nodes.shape
    cap = send_rows.shape[3]
    me = lax.axis_index("patch")
    mine = lax.axis_index("feat")
    x, z, c = me // (Z * C), me // C % Z, me % C
    feat = lax.axis_size("feat")

    block = pack(me.reshape(1), send_rows[0, 0].T, nodes)
    parts = [nodes]
    for k in range(1, feat):
        parts.append(lax.ppermute(nodes, "feat", [(i, (i + k) % feat) for i in range(feat)]))
    up = lambda a: moved(a, lambda x, z, c: (x, z + 1, c))
    down = lambda a: moved(a, lambda x, z, c: (x, z - 1, c))
    held = {0: block}
    forth = back = block
    for hop in range(1, 4):
        forth, back = up(forth), down(back)
        if hop == 2:
            forth = gate(forth, *parts[1:])
        held[hop], held[Z - hop] = forth, back
    held[4] = up(forth)

    groups = []
    for pairs in BATCHES:
        picked = select(pairs, cap, [held[dz] for pair in pairs for dz in pair])
        group = [picked[0]]
        for k in range(1, X):
            group.append(moved(picked[k], lambda x, z, c: (x + k, z, c)))
        groups.append(group)
    swap = lambda a: moved(a, lambda x, z, c: (x, z, c + 1))

    def near_row(row):
        return ((mine - row // rows) & (feat - 1)) * rows + row % rows

    patch = feat * rows
    slot = jnp.maximum(sender_slot - patch, 0)
    source, entry = slot // cap, slot % cap
    k = (x - source // (Z * C)) & (X - 1)
    dz = (z - source // C % Z) & (Z - 1)
    s = (source - c) & (C - 1)
    place = jnp.zeros_like(slot)
    base = 0
    for pairs in BATCHES:
        for at, pair in enumerate(pairs):
            for side, value in enumerate(pair):
                size = len(pairs) * 2 * cap
                here = base + (s * X + k) * size + at * 2 * cap + side * cap
                place = jnp.where(dz == value, here, place)
        base += X * C * len(pairs) * 2 * cap
    send = jnp.where(sender_slot < patch, near_row(sender_slot), patch + place + entry)
    recv = near_row(receivers).reshape(1, -1)
    before = edge_before(
        recv, send.reshape(1, -1), edge_b1.reshape(1, -1), parts, edges, edge_w1, groups[1][0]
    )
    groups = [group + [swap(crossing(group, before))] for group in groups]
    edges_out, *sums = edge_after(
        patch, live_edges, send.reshape(-1, 1), recv, edge_gain.reshape(1, -1), groups[0] + groups[1], before,
        edge_w1, edge_w2, edges, rows,
    )
    parts = [sums[0]]
    for k in range(1, feat):
        parts.append(lax.ppermute(sums[k], "feat", [(i, (i - k) % feat) for i in range(feat)]))
    nodes_out = node_update(
        nodes, parts, node_w1, node_b1.reshape(1, -1), node_w2, node_gain.reshape(1, -1)
    )
    return (edges_out, nodes_out)


def solution(mesh):
    placed = (
        P(("patch", "feat"), None),
        P(("patch", "feat"), None),
        P(("patch", "feat")),
        P(("patch", "feat")),
        P("patch", "feat", None, None),
        P(("patch", "feat")),
    ) + (P(),) * 8
    return jax.shard_map(
        local,
        mesh=mesh,
        in_specs=placed,
        out_specs=(P(("patch", "feat"), None), P(("patch", "feat"), None)),
        check_vma=False,
    )
```

```python
import jax
import jax.numpy as jnp
from jax import lax
from jax.experimental import pallas as pl
from jax.experimental.pallas import tpu as pltpu
from jax.sharding import PartitionSpec as P

epsilon = 1e-05
f32 = jnp.float32
bf16 = jnp.bfloat16
i32 = jnp.int32
TILES = 2
GATHERS = 1
LIMIT = 16 << 20
VMEM = pl.BlockSpec(memory_space=pltpu.VMEM)
SMEM = pl.BlockSpec(memory_space=pltpu.SMEM)
HBM = pl.BlockSpec(memory_space=pltpu.HBM)
ANY = pl.BlockSpec(memory_space=pl.ANY)
X, Z, C = 4, 8, 2
TAIL = 16
COST = 1 << 20
NEAR = (1, 3, 2)
BATCHES = (((0, 1), (7, 2)), ((6, 3), (5, 4)))


def dot(left, right):
    return jnp.dot(left, right, preferred_element_type=f32)


def dot_first(left, right):
    return lax.dot_general(left, right, (((0,), (0,)), ((), ())), preferred_element_type=f32)


def silu(value):
    return value / (1.0 + jnp.exp(-value))


def layer_norm(values, scales):
    average = jnp.mean(values, axis=-1, keepdims=True)
    centred = values - average
    variance = jnp.mean(centred * centred, axis=-1, keepdims=True)
    return centred * lax.rsqrt(variance + epsilon) * scales


def as_bf16(mask):
    return mask.astype(f32).astype(bf16)


def hot_columns(row, count, first=0):
    ids = lax.broadcasted_iota(i32, (count, row.shape[1]), 0) + first
    return as_bf16(row == ids)


def hot_rows(column, count, first=0):
    ids = lax.broadcasted_iota(i32, (column.shape[0], count), 1) + first
    return as_bf16(column == ids)


def in_hbm(value):
    return pltpu.with_memory_space_constraint(value, pltpu.HBM)


def odd(dz):
    return (dz >= 1) & (dz <= 4)


def pack_kernel(where_ref, lists_ref, nodes_ref, out_ref):
    rows, latent = nodes_ref.shape
    cap, peers = lists_ref.shape
    out_ref[:rows] = nodes_ref[...]
    me = where_ref[0]
    x, z, c = me // (Z * C), me // C % Z, me % C
    lane = lax.broadcasted_iota(i32, (cap, latent), 1)
    spread = as_bf16(lane % cap == lax.broadcasted_iota(i32, (cap, latent), 0))
    listed = dot_first(lists_ref[...].astype(f32).astype(bf16), spread)
    peer = lax.broadcasted_iota(i32, (peers, latent), 0)
    lane = lax.broadcasted_iota(i32, (peers, latent), 1)
    k = (peer // (Z * C) - x) & (X - 1)
    dz = (peer // C % Z - z) & (Z - 1)
    s = (peer % C - c) & (C - 1)
    slot = (k * C + s) * 2 + jnp.where(odd(dz), 1, 0)
    listed = jnp.where(lane // cap == slot, listed + 1.0, 0.0).astype(bf16)
    row = lax.broadcasted_iota(i32, (TAIL, peers), 0)
    peer = lax.broadcasted_iota(i32, (TAIL, peers), 1)
    pick = as_bf16(row == ((peer // C % Z - z) & (Z - 1)))
    out_ref[rows:] = (dot(pick, listed) - 1.0).astype(bf16)


def pack(me, lists, nodes):
    return pl.pallas_call(
        pack_kernel,
        in_specs=[SMEM, VMEM, VMEM],
        out_shape=jax.ShapeDtypeStruct((nodes.shape[0] + TAIL, nodes.shape[1]), bf16),
        name="pack",
    )(me, lists, nodes)


def select_kernel(pairs, cap, extra, *refs):
    count = 2 * len(pairs)
    blocks, outs = list(refs[:count]), refs[count + extra : count + extra + X]
    own = pairs[0][0] == 0
    if own:
        held, sem = refs[count + extra + X :]
        fetch = pltpu.make_async_copy(blocks[0], held, sem)
        fetch.start()
        blocks[0] = held
    rows = blocks[0].shape[0] - TAIL
    lanes = X * C * 2 * cap
    for at in reversed(range(len(pairs))):
        total = None
        for side, dz in reversed(list(enumerate(pairs[at]))):
            if dz == 0:
                fetch.wait()
            block = blocks[2 * at + side]
            wanted = block[rows:].astype(f32)[dz : dz + 1, :lanes].astype(i32)
            part = dot_first(hot_columns(wanted, rows), block[:rows])
            total = part if total is None else total + part
        total = total.astype(bf16)
        size = 2 * cap
        for k in range(X):
            for s in range(C):
                first = (k * C + s) * size
                put = (s * len(pairs) + at) * size
                outs[k][put : put + size] = total[first : first + size]


def select(pairs, cap, blocks, *earlier):
    latent = blocks[0].shape[1]
    shape = jax.ShapeDtypeStruct((C * len(pairs) * 2 * cap, latent), bf16)
    own = pairs[0][0] == 0
    blocks = list(blocks)
    if own:
        blocks[0] = in_hbm(blocks[0])
    return pl.pallas_call(
        lambda *refs: select_kernel(pairs, cap, len(earlier), *refs),
        in_specs=[HBM if own else VMEM] + [VMEM] * (len(blocks) - 1) + [ANY] * len(earlier),
        out_shape=[shape] * X,
        scratch_shapes=[pltpu.VMEM(blocks[0].shape, bf16), pltpu.SemaphoreType.DMA] if own else [],
        compiler_params=pltpu.CompilerParams(vmem_limit_bytes=LIMIT),
        cost_estimate=pl.CostEstimate(flops=COST, bytes_accessed=0, transcendentals=0),
        name="select",
    )(*blocks, *earlier)


def gate_kernel(*refs):
    pass


def gate(value, *earlier):
    return pl.pallas_call(
        gate_kernel,
        in_specs=[ANY] * (1 + len(earlier)),
        out_specs=ANY,
        out_shape=jax.ShapeDtypeStruct(value.shape, value.dtype),
        input_output_aliases={0: 0},
        compiler_params=pltpu.CompilerParams(vmem_limit_bytes=1 << 20),
        cost_estimate=pl.CostEstimate(flops=0, bytes_accessed=0, transcendentals=0),
        name="gate",
    )(value, *earlier)


def cross_kernel(*refs):
    out_ref = refs[-1]
    put = 0
    for ref in refs[: X * len(BATCHES)]:
        size = ref.shape[0] // C
        out_ref[put : put + size] = ref[size:]
        put += size


def crossing(parts, *earlier):
    rows = sum(part.shape[0] for part in parts) // C
    return pl.pallas_call(
        cross_kernel,
        in_specs=[VMEM] * len(parts) + [HBM] * len(earlier),
        out_shape=jax.ShapeDtypeStruct((rows, parts[0].shape[1]), bf16),
        compiler_params=pltpu.CompilerParams(vmem_limit_bytes=LIMIT),
        name="crossing",
    )(*parts, *[in_hbm(part) for part in earlier])


def fill(table_ref, parts, crossed):
    put, taken = 0, 0
    for at in range(len(BATCHES)):
        group = parts[at * X : (at + 1) * X]
        size = group[0].shape[0] // C
        for part in group:
            table_ref[put : put + size] = part[:size]
            put += size
        table_ref[put : put + X * size] = crossed[taken : taken + X * size]
        put, taken = put + X * size, taken + X * size


def before_kernel(extra, *refs):
    recv_ref, send_ref, b1_ref = refs[:3]
    parts = refs[3:7]
    edges_hbm, w1_hbm = refs[7:9]
    out_hbm, table_ref, edges_ref, w1_ref, out_ref, sems = refs[9 + extra :]
    loads = [
        pltpu.make_async_copy(w1_hbm, w1_ref, sems.at[0]),
        pltpu.make_async_copy(edges_hbm, edges_ref, sems.at[1]),
    ]
    for load in loads:
        load.start()
    count, latent = edges_ref.shape
    size = parts[0].shape[0]
    nodes = table_ref.shape[0]
    tile = count // TILES
    for k, part in enumerate(parts):
        table_ref[k * size : (k + 1) * size] = part[...]
    stores = []
    for at in range(TILES):
        rows = slice(at * tile, (at + 1) * tile)
        own = dot_first(hot_columns(recv_ref[:, rows], nodes), table_ref[...]).astype(bf16)
        near = dot_first(hot_columns(send_ref[:, rows], nodes), table_ref[...]).astype(bf16)
        if at == 0:
            for load in loads:
                load.wait()
        total = dot(edges_ref[rows], w1_ref[:latent])
        total = total + dot(near, w1_ref[latent : 2 * latent])
        total = total + dot(own, w1_ref[2 * latent :])
        out_ref[rows] = total + b1_ref[...]
        part = pl.ds(at * tile, tile)
        stores.append(pltpu.make_async_copy(out_ref.at[part], out_hbm.at[part], sems.at[2 + at]))
        stores[-1].start()
    for store in stores:
        store.wait()


def edge_before(recv, send, b1, parts, edges, w1, *earlier):
    count, latent = edges.shape
    nodes = sum(part.shape[0] for part in parts)
    return pl.pallas_call(
        lambda *refs: before_kernel(len(earlier), *refs),
        in_specs=[VMEM] * 7 + [HBM] * 2 + [ANY] * len(earlier),
        out_specs=HBM,
        out_shape=pltpu.HBM((count, latent), f32),
        scratch_shapes=[
            pltpu.VMEM((nodes, latent), bf16),
            pltpu.VMEM((count, latent), bf16),
            pltpu.VMEM(w1.shape, bf16),
            pltpu.VMEM((count, latent), f32),
            pltpu.SemaphoreType.DMA((2 + TILES,)),
        ],
        compiler_params=pltpu.CompilerParams(vmem_limit_bytes=32 << 20),
        cost_estimate=pl.CostEstimate(flops=COST, bytes_accessed=0, transcendentals=0),
        name="edge_before",
    )(recv, send, b1, *parts, in_hbm(edges), in_hbm(w1), *earlier)


def after_kernel(first_row, *refs):
    live_ref, send_ref, recv_ref, gain_ref = refs[:4]
    count = X * len(BATCHES)
    parts, crossed, refs = refs[4 : 4 + count], refs[4 + count], refs[5 + count :]
    before_hbm, w1_hbm, w2_hbm, edges_hbm, out_hbm = refs[:5]
    sums_refs = refs[5:9]
    table_ref, before_ref, w1_ref, w2_ref, edges_ref, far_ref, load_sems, store_sems = refs[9:]
    count, latent = edges_ref.shape
    tile = count // TILES
    loads = [
        pltpu.make_async_copy(w1_hbm.at[pl.ds(latent, latent)], w1_ref, load_sems.at[0]),
        pltpu.make_async_copy(before_hbm, before_ref, load_sems.at[1]),
        pltpu.make_async_copy(w2_hbm, w2_ref, load_sems.at[2]),
        pltpu.make_async_copy(edges_hbm, edges_ref, load_sems.at[3]),
    ]
    for load in loads:
        load.start()
    fill(table_ref, parts, crossed)
    stores = []
    live = live_ref[0]
    size = count // GATHERS
    for at in range(GATHERS):
        rows = slice(at * size, (at + 1) * size)
        hot = hot_rows(send_ref[rows], table_ref.shape[0], first_row)
        far_ref[rows] = dot(hot, table_ref[...]).astype(bf16)
    for load in loads:
        load.wait()
    for at in range(TILES):
        rows = slice(at * tile, (at + 1) * tile)
        first = before_ref[rows] + dot(far_ref[rows], w1_ref[...])
        hidden = silu(first).astype(bf16)
        change = layer_norm(dot(hidden, w2_ref[...]), gain_ref[...])
        alive = lax.broadcasted_iota(i32, (tile, 1), 0) + at * tile < live
        edge = edges_ref[rows].astype(f32) + jnp.where(alive, change, 0.0)
        edges_ref[rows] = edge.astype(bf16)
        part = pl.ds(at * tile, tile)
        stores.append(
            pltpu.make_async_copy(edges_ref.at[part], out_hbm.at[part], store_sems.at[at])
        )
        stores[-1].start()
    alive = lax.broadcasted_iota(i32, (1, count), 1) < live
    receiver = jnp.where(alive, recv_ref[...], -1)
    size = sums_refs[0].shape[0]
    for at, ref in enumerate(sums_refs):
        hot = hot_columns(receiver, size, at * size)
        ref[...] = dot(hot, edges_ref[...]).astype(ref.dtype)
    for store in stores:
        store.wait()


def edge_after(first_row, live, send, recv, gain, parts, before, w1, w2, edges, rows):
    count, latent = edges.shape
    table = sum(part.shape[0] for part in parts[:-1]) // C + parts[-1].shape[0]
    return pl.pallas_call(
        lambda *refs: after_kernel(first_row, *refs),
        in_specs=[SMEM] + [VMEM] * (3 + len(parts)) + [HBM] * 4,
        out_specs=[HBM] + [VMEM] * 4,
        out_shape=[jax.ShapeDtypeStruct((count, latent), bf16)]
        + [jax.ShapeDtypeStruct((rows, latent), f32 if k == 0 else bf16) for k in range(4)],
        scratch_shapes=[
            pltpu.VMEM((table, latent), bf16),
            pltpu.VMEM((count, latent), f32),
            pltpu.VMEM((latent, latent), bf16),
            pltpu.VMEM((latent, latent), bf16),
            pltpu.VMEM((count, latent), bf16),
            pltpu.VMEM((count, latent), bf16),
            pltpu.SemaphoreType.DMA((4,)),
            pltpu.SemaphoreType.DMA((TILES,)),
        ],
        compiler_params=pltpu.CompilerParams(vmem_limit_bytes=32 << 20),
        name="edge_after",
    )(live, send, recv, gain, *parts, *[in_hbm(part) for part in (before, w1, w2, edges)])


def node_kernel(nodes_ref, p0_ref, p1_ref, p2_ref, p3_ref, w1_ref, b1_ref, w2_ref, gain_ref, out_ref):
    latent = nodes_ref.shape[1]
    total = p0_ref[...].astype(f32) + p1_ref[...].astype(f32)
    total = total + p2_ref[...].astype(f32) + p3_ref[...].astype(f32)
    incoming = total.astype(bf16)
    nodes = nodes_ref[...]
    first = dot(nodes, w1_ref[:latent]) + dot(incoming, w1_ref[latent:])
    hidden = silu(first + b1_ref[...]).astype(bf16)
    change = layer_norm(dot(hidden, w2_ref[...]), gain_ref[...])
    out_ref[...] = (nodes.astype(f32) + change).astype(bf16)


def node_update(nodes, parts, w1, b1, w2, gain):
    return pl.pallas_call(
        node_kernel,
        in_specs=[VMEM] * 9,
        out_shape=jax.ShapeDtypeStruct(nodes.shape, bf16),
        compiler_params=pltpu.CompilerParams(vmem_limit_bytes=LIMIT),
        name="node_update",
    )(nodes, *parts, w1, b1, w2, gain)


def pairs_of(move):
    found = []
    for x in range(X):
        for z in range(Z):
            for c in range(C):
                tx, tz, tc = move(x, z, c)
                found.append(((x * Z + z) * C + c, ((tx % X) * Z + tz % Z) * C + tc % C))
    return found


def moved(value, move):
    return lax.ppermute(value, "patch", pairs_of(move))


def local(
    nodes,
    edges,
    receivers,
    sender_slot,
    send_rows,
    live_edges,
    edge_w1,
    edge_b1,
    edge_w2,
    edge_gain,
    node_w1,
    node_b1,
    node_w2,
    node_gain,
):
    rows, latent = nodes.shape
    cap = send_rows.shape[3]
    me = lax.axis_index("patch")
    mine = lax.axis_index("feat")
    x, z, c = me // (Z * C), me // C % Z, me % C
    feat = lax.axis_size("feat")

    block = pack(me.reshape(1), send_rows[0, 0].T, nodes)
    parts = [nodes]
    for k in range(1, feat):
        parts.append(lax.ppermute(nodes, "feat", [(i, (i + k) % feat) for i in range(feat)]))
    up = lambda a: moved(a, lambda x, z, c: (x, z + 1, c))
    down = lambda a: moved(a, lambda x, z, c: (x, z - 1, c))
    held = {0: block}
    forth = back = block
    for hop in range(1, 4):
        forth, back = up(forth), down(back)
        forth = gate(forth, parts[NEAR[hop - 1]])
        held[hop], held[Z - hop] = forth, back
    held[4] = up(forth)

    groups = []
    for pairs in BATCHES:
        picked = select(pairs, cap, [held[dz] for pair in pairs for dz in pair])
        group = [picked[0]]
        for k in range(1, X):
            group.append(moved(picked[k], lambda x, z, c: (x + k, z, c)))
        groups.append(group)
    swap = lambda a: moved(a, lambda x, z, c: (x, z, c + 1))

    def near_row(row):
        return ((mine - row // rows) & (feat - 1)) * rows + row % rows

    patch = feat * rows
    slot = jnp.maximum(sender_slot - patch, 0)
    source, entry = slot // cap, slot % cap
    k = (x - source // (Z * C)) & (X - 1)
    dz = (z - source // C % Z) & (Z - 1)
    s = (source - c) & (C - 1)
    place = jnp.zeros_like(slot)
    base = 0
    for pairs in BATCHES:
        for at, pair in enumerate(pairs):
            for side, value in enumerate(pair):
                size = len(pairs) * 2 * cap
                here = base + (s * X + k) * size + at * 2 * cap + side * cap
                place = jnp.where(dz == value, here, place)
        base += X * C * len(pairs) * 2 * cap
    send = jnp.where(sender_slot < patch, near_row(sender_slot), patch + place + entry)
    recv = near_row(receivers).reshape(1, -1)
    before = edge_before(
        recv, send.reshape(1, -1), edge_b1.reshape(1, -1), parts, edges, edge_w1, groups[1][0]
    )
    arrived = groups[0] + groups[1]
    arrived = arrived + [swap(crossing(arrived, before))]
    edges_out, *sums = edge_after(
        patch, live_edges, send.reshape(-1, 1), recv, edge_gain.reshape(1, -1), arrived, before,
        edge_w1, edge_w2, edges, rows,
    )
    parts = [sums[0]]
    for k in range(1, feat):
        parts.append(lax.ppermute(sums[k], "feat", [(i, (i - k) % feat) for i in range(feat)]))
    nodes_out = node_update(
        nodes, parts, node_w1, node_b1.reshape(1, -1), node_w2, node_gain.reshape(1, -1)
    )
    return (edges_out, nodes_out)


def solution(mesh):
    placed = (
        P(("patch", "feat"), None),
        P(("patch", "feat"), None),
        P(("patch", "feat")),
        P(("patch", "feat")),
        P("patch", "feat", None, None),
        P(("patch", "feat")),
    ) + (P(),) * 8
    return jax.shard_map(
        local,
        mesh=mesh,
        in_specs=placed,
        out_specs=(P(("patch", "feat"), None), P(("patch", "feat"), None)),
        check_vma=False,
    )
```

```python
import jax
import jax.numpy as jnp
from jax import lax
from jax.experimental import pallas as pl
from jax.experimental.pallas import tpu as pltpu
from jax.sharding import PartitionSpec as P

epsilon = 1e-05
f32 = jnp.float32
bf16 = jnp.bfloat16
i32 = jnp.int32
TILES = 2
GATHERS = 1
LIMIT = 16 << 20
VMEM = pl.BlockSpec(memory_space=pltpu.VMEM)
SMEM = pl.BlockSpec(memory_space=pltpu.SMEM)
HBM = pl.BlockSpec(memory_space=pltpu.HBM)
ANY = pl.BlockSpec(memory_space=pl.ANY)
X, Z, C = 4, 8, 2
TAIL = 16
COST = 1 << 20
NEAR = (1, 3, 2)
BATCHES = (((0, 1), (7, 2)), ((6, 3), (5, 4)))


def dot(left, right):
    return jnp.dot(left, right, preferred_element_type=f32)


def dot_first(left, right):
    return lax.dot_general(left, right, (((0,), (0,)), ((), ())), preferred_element_type=f32)


def silu(value):
    return value / (1.0 + jnp.exp(-value))


def layer_norm(values, scales):
    average = jnp.mean(values, axis=-1, keepdims=True)
    centred = values - average
    variance = jnp.mean(centred * centred, axis=-1, keepdims=True)
    return centred * lax.rsqrt(variance + epsilon) * scales


def as_bf16(mask):
    return mask.astype(f32).astype(bf16)


def hot_columns(row, count, first=0):
    ids = lax.broadcasted_iota(i32, (count, row.shape[1]), 0) + first
    return as_bf16(row == ids)


def hot_rows(column, count, first=0):
    ids = lax.broadcasted_iota(i32, (column.shape[0], count), 1) + first
    return as_bf16(column == ids)


def in_hbm(value):
    return pltpu.with_memory_space_constraint(value, pltpu.HBM)


def odd(dz):
    return (dz >= 1) & (dz <= 4)


def pack_kernel(where_ref, lists_ref, nodes_hbm, out_hbm, tail_ref, sems):
    rows, latent = nodes_hbm.shape
    cap, peers = lists_ref.shape
    body = pltpu.make_async_copy(nodes_hbm, out_hbm.at[pl.ds(0, rows)], sems.at[0])
    body.start()
    me = where_ref[0]
    x, z, c = me // (Z * C), me // C % Z, me % C
    lane = lax.broadcasted_iota(i32, (cap, latent), 1)
    spread = as_bf16(lane % cap == lax.broadcasted_iota(i32, (cap, latent), 0))
    listed = dot_first(lists_ref[...].astype(f32).astype(bf16), spread)
    peer = lax.broadcasted_iota(i32, (peers, latent), 0)
    lane = lax.broadcasted_iota(i32, (peers, latent), 1)
    k = (peer // (Z * C) - x) & (X - 1)
    dz = (peer // C % Z - z) & (Z - 1)
    s = (peer % C - c) & (C - 1)
    slot = (k * C + s) * 2 + jnp.where(odd(dz), 1, 0)
    listed = jnp.where(lane // cap == slot, listed + 1.0, 0.0).astype(bf16)
    row = lax.broadcasted_iota(i32, (TAIL, peers), 0)
    peer = lax.broadcasted_iota(i32, (TAIL, peers), 1)
    pick = as_bf16(row == ((peer // C % Z - z) & (Z - 1)))
    tail_ref[...] = (dot(pick, listed) - 1.0).astype(bf16)
    tail = pltpu.make_async_copy(tail_ref, out_hbm.at[pl.ds(rows, TAIL)], sems.at[1])
    tail.start()
    tail.wait()
    body.wait()


def pack(me, lists, nodes):
    return pl.pallas_call(
        pack_kernel,
        in_specs=[SMEM, VMEM, HBM],
        out_specs=HBM,
        out_shape=pltpu.HBM((nodes.shape[0] + TAIL, nodes.shape[1]), bf16),
        scratch_shapes=[pltpu.VMEM((TAIL, nodes.shape[1]), bf16), pltpu.SemaphoreType.DMA((2,))],
        name="pack",
    )(me, lists, in_hbm(nodes))


def select_kernel(pairs, cap, extra, *refs):
    count = 2 * len(pairs)
    blocks, outs = list(refs[:count]), refs[count + extra : count + extra + X]
    own = pairs[0][0] == 0
    if own:
        held, sem = refs[count + extra + X :]
        fetch = pltpu.make_async_copy(blocks[0], held, sem)
        fetch.start()
        blocks[0] = held
    rows = blocks[0].shape[0] - TAIL
    lanes = X * C * 2 * cap
    for at in reversed(range(len(pairs))):
        total = None
        for side, dz in reversed(list(enumerate(pairs[at]))):
            if dz == 0:
                fetch.wait()
            block = blocks[2 * at + side]
            wanted = block[rows:].astype(f32)[dz : dz + 1, :lanes].astype(i32)
            part = dot_first(hot_columns(wanted, rows), block[:rows])
            total = part if total is None else total + part
        total = total.astype(bf16)
        size = 2 * cap
        for k in range(X):
            for s in range(C):
                first = (k * C + s) * size
                put = (s * len(pairs) + at) * size
                outs[k][put : put + size] = total[first : first + size]


def select(pairs, cap, blocks, *earlier):
    latent = blocks[0].shape[1]
    shape = jax.ShapeDtypeStruct((C * len(pairs) * 2 * cap, latent), bf16)
    own = pairs[0][0] == 0
    blocks = list(blocks)
    if own:
        blocks[0] = in_hbm(blocks[0])
    return pl.pallas_call(
        lambda *refs: select_kernel(pairs, cap, len(earlier), *refs),
        in_specs=[HBM if own else VMEM] + [VMEM] * (len(blocks) - 1) + [ANY] * len(earlier),
        out_shape=[shape] * X,
        scratch_shapes=[pltpu.VMEM(blocks[0].shape, bf16), pltpu.SemaphoreType.DMA] if own else [],
        compiler_params=pltpu.CompilerParams(vmem_limit_bytes=LIMIT),
        cost_estimate=pl.CostEstimate(flops=COST, bytes_accessed=0, transcendentals=0),
        name="select",
    )(*blocks, *earlier)


def gate_kernel(*refs):
    pass


def gate(value, *earlier):
    return pl.pallas_call(
        gate_kernel,
        in_specs=[ANY] * (1 + len(earlier)),
        out_specs=ANY,
        out_shape=jax.ShapeDtypeStruct(value.shape, value.dtype),
        input_output_aliases={0: 0},
        compiler_params=pltpu.CompilerParams(vmem_limit_bytes=1 << 20),
        cost_estimate=pl.CostEstimate(flops=0, bytes_accessed=0, transcendentals=0),
        name="gate",
    )(value, *earlier)


def cross_kernel(*refs):
    out_ref = refs[-1]
    put = 0
    for ref in refs[: X * len(BATCHES)]:
        size = ref.shape[0] // C
        out_ref[put : put + size] = ref[size:]
        put += size


def crossing(parts, *earlier):
    rows = sum(part.shape[0] for part in parts) // C
    return pl.pallas_call(
        cross_kernel,
        in_specs=[VMEM] * len(parts) + [HBM] * len(earlier),
        out_shape=jax.ShapeDtypeStruct((rows, parts[0].shape[1]), bf16),
        compiler_params=pltpu.CompilerParams(vmem_limit_bytes=LIMIT),
        name="crossing",
    )(*parts, *[in_hbm(part) for part in earlier])


def fill(table_ref, parts, crossed):
    put, taken = 0, 0
    for at in range(len(BATCHES)):
        group = parts[at * X : (at + 1) * X]
        size = group[0].shape[0] // C
        for part in group:
            table_ref[put : put + size] = part[:size]
            put += size
        table_ref[put : put + X * size] = crossed[taken : taken + X * size]
        put, taken = put + X * size, taken + X * size


def before_kernel(extra, *refs):
    recv_ref, send_ref, b1_ref = refs[:3]
    parts = refs[3:7]
    edges_hbm, w1_hbm = refs[7:9]
    out_hbm, table_ref, edges_ref, w1_ref, out_ref, sems = refs[9 + extra :]
    loads = [
        pltpu.make_async_copy(w1_hbm, w1_ref, sems.at[0]),
        pltpu.make_async_copy(edges_hbm, edges_ref, sems.at[1]),
    ]
    for load in loads:
        load.start()
    count, latent = edges_ref.shape
    size = parts[0].shape[0]
    nodes = table_ref.shape[0]
    tile = count // TILES
    for k, part in enumerate(parts):
        table_ref[k * size : (k + 1) * size] = part[...]
    stores = []
    for at in range(TILES):
        rows = slice(at * tile, (at + 1) * tile)
        own = dot_first(hot_columns(recv_ref[:, rows], nodes), table_ref[...]).astype(bf16)
        near = dot_first(hot_columns(send_ref[:, rows], nodes), table_ref[...]).astype(bf16)
        if at == 0:
            for load in loads:
                load.wait()
        total = dot(edges_ref[rows], w1_ref[:latent])
        total = total + dot(near, w1_ref[latent : 2 * latent])
        total = total + dot(own, w1_ref[2 * latent :])
        out_ref[rows] = total + b1_ref[...]
        part = pl.ds(at * tile, tile)
        stores.append(pltpu.make_async_copy(out_ref.at[part], out_hbm.at[part], sems.at[2 + at]))
        stores[-1].start()
    for store in stores:
        store.wait()


def edge_before(recv, send, b1, parts, edges, w1, *earlier):
    count, latent = edges.shape
    nodes = sum(part.shape[0] for part in parts)
    return pl.pallas_call(
        lambda *refs: before_kernel(len(earlier), *refs),
        in_specs=[VMEM] * 7 + [HBM] * 2 + [ANY] * len(earlier),
        out_specs=HBM,
        out_shape=pltpu.HBM((count, latent), f32),
        scratch_shapes=[
            pltpu.VMEM((nodes, latent), bf16),
            pltpu.VMEM((count, latent), bf16),
            pltpu.VMEM(w1.shape, bf16),
            pltpu.VMEM((count, latent), f32),
            pltpu.SemaphoreType.DMA((2 + TILES,)),
        ],
        compiler_params=pltpu.CompilerParams(vmem_limit_bytes=32 << 20),
        cost_estimate=pl.CostEstimate(flops=COST, bytes_accessed=0, transcendentals=0),
        name="edge_before",
    )(recv, send, b1, *parts, in_hbm(edges), in_hbm(w1), *earlier)


def after_kernel(first_row, *refs):
    live_ref, send_ref, recv_ref, gain_ref = refs[:4]
    count = X * len(BATCHES)
    parts, crossed, refs = refs[4 : 4 + count], refs[4 + count], refs[5 + count :]
    before_hbm, w1_hbm, w2_hbm, edges_hbm, out_hbm = refs[:5]
    sums_refs = refs[5:9]
    table_ref, before_ref, w1_ref, w2_ref, edges_ref, far_ref, load_sems, store_sems = refs[9:]
    count, latent = edges_ref.shape
    tile = count // TILES
    loads = [
        pltpu.make_async_copy(w1_hbm.at[pl.ds(latent, latent)], w1_ref, load_sems.at[0]),
        pltpu.make_async_copy(before_hbm, before_ref, load_sems.at[1]),
        pltpu.make_async_copy(w2_hbm, w2_ref, load_sems.at[2]),
        pltpu.make_async_copy(edges_hbm, edges_ref, load_sems.at[3]),
    ]
    for load in loads:
        load.start()
    fill(table_ref, parts, crossed)
    stores = []
    live = live_ref[0]
    size = count // GATHERS
    for at in range(GATHERS):
        rows = slice(at * size, (at + 1) * size)
        hot = hot_rows(send_ref[rows], table_ref.shape[0], first_row)
        far_ref[rows] = dot(hot, table_ref[...]).astype(bf16)
    for load in loads:
        load.wait()
    for at in range(TILES):
        rows = slice(at * tile, (at + 1) * tile)
        first = before_ref[rows] + dot(far_ref[rows], w1_ref[...])
        hidden = silu(first).astype(bf16)
        change = layer_norm(dot(hidden, w2_ref[...]), gain_ref[...])
        alive = lax.broadcasted_iota(i32, (tile, 1), 0) + at * tile < live
        edge = edges_ref[rows].astype(f32) + jnp.where(alive, change, 0.0)
        edges_ref[rows] = edge.astype(bf16)
        part = pl.ds(at * tile, tile)
        stores.append(
            pltpu.make_async_copy(edges_ref.at[part], out_hbm.at[part], store_sems.at[at])
        )
        stores[-1].start()
    alive = lax.broadcasted_iota(i32, (1, count), 1) < live
    receiver = jnp.where(alive, recv_ref[...], -1)
    size = sums_refs[0].shape[0]
    for at, ref in enumerate(sums_refs):
        hot = hot_columns(receiver, size, at * size)
        ref[...] = dot(hot, edges_ref[...]).astype(ref.dtype)
    for store in stores:
        store.wait()


def edge_after(first_row, live, send, recv, gain, parts, before, w1, w2, edges, rows):
    count, latent = edges.shape
    table = sum(part.shape[0] for part in parts[:-1]) // C + parts[-1].shape[0]
    return pl.pallas_call(
        lambda *refs: after_kernel(first_row, *refs),
        in_specs=[SMEM] + [VMEM] * (3 + len(parts)) + [HBM] * 4,
        out_specs=[HBM] + [VMEM] * 4,
        out_shape=[jax.ShapeDtypeStruct((count, latent), bf16)]
        + [jax.ShapeDtypeStruct((rows, latent), f32 if k == 0 else bf16) for k in range(4)],
        scratch_shapes=[
            pltpu.VMEM((table, latent), bf16),
            pltpu.VMEM((count, latent), f32),
            pltpu.VMEM((latent, latent), bf16),
            pltpu.VMEM((latent, latent), bf16),
            pltpu.VMEM((count, latent), bf16),
            pltpu.VMEM((count, latent), bf16),
            pltpu.SemaphoreType.DMA((4,)),
            pltpu.SemaphoreType.DMA((TILES,)),
        ],
        compiler_params=pltpu.CompilerParams(vmem_limit_bytes=32 << 20),
        name="edge_after",
    )(live, send, recv, gain, *parts, *[in_hbm(part) for part in (before, w1, w2, edges)])


def node_kernel(nodes_ref, p0_ref, p1_ref, p2_ref, p3_ref, w1_ref, b1_ref, w2_ref, gain_ref, out_ref):
    latent = nodes_ref.shape[1]
    total = p0_ref[...].astype(f32) + p1_ref[...].astype(f32)
    total = total + p2_ref[...].astype(f32) + p3_ref[...].astype(f32)
    incoming = total.astype(bf16)
    nodes = nodes_ref[...]
    first = dot(nodes, w1_ref[:latent]) + dot(incoming, w1_ref[latent:])
    hidden = silu(first + b1_ref[...]).astype(bf16)
    change = layer_norm(dot(hidden, w2_ref[...]), gain_ref[...])
    out_ref[...] = (nodes.astype(f32) + change).astype(bf16)


def node_update(nodes, parts, w1, b1, w2, gain):
    return pl.pallas_call(
        node_kernel,
        in_specs=[VMEM] * 9,
        out_shape=jax.ShapeDtypeStruct(nodes.shape, bf16),
        compiler_params=pltpu.CompilerParams(vmem_limit_bytes=LIMIT),
        name="node_update",
    )(nodes, *parts, w1, b1, w2, gain)


def pairs_of(move):
    found = []
    for x in range(X):
        for z in range(Z):
            for c in range(C):
                tx, tz, tc = move(x, z, c)
                found.append(((x * Z + z) * C + c, ((tx % X) * Z + tz % Z) * C + tc % C))
    return found


def moved(value, move):
    return lax.ppermute(value, "patch", pairs_of(move))


def local(
    nodes,
    edges,
    receivers,
    sender_slot,
    send_rows,
    live_edges,
    edge_w1,
    edge_b1,
    edge_w2,
    edge_gain,
    node_w1,
    node_b1,
    node_w2,
    node_gain,
):
    rows, latent = nodes.shape
    cap = send_rows.shape[3]
    me = lax.axis_index("patch")
    mine = lax.axis_index("feat")
    x, z, c = me // (Z * C), me // C % Z, me % C
    feat = lax.axis_size("feat")

    block = pack(me.reshape(1), send_rows[0, 0].T, nodes)
    def around(value, k):
        return lax.ppermute(value, "feat", [(i, (i + k) % feat) for i in range(feat)])

    after_one = around(nodes, 1)
    parts = [nodes, after_one, around(after_one, 1), around(nodes, feat - 1)]
    up = lambda a: moved(a, lambda x, z, c: (x, z + 1, c))
    down = lambda a: moved(a, lambda x, z, c: (x, z - 1, c))
    held = {0: block}
    forth = back = block
    for hop in range(1, 4):
        forth, back = up(forth), down(back)
        forth = gate(forth, parts[NEAR[hop - 1]])
        held[hop], held[Z - hop] = forth, back
    held[4] = up(forth)

    groups = []
    for pairs in BATCHES:
        picked = select(pairs, cap, [held[dz] for pair in pairs for dz in pair])
        group = [picked[0]]
        for k in range(1, X):
            group.append(moved(picked[k], lambda x, z, c: (x + k, z, c)))
        groups.append(group)
    swap = lambda a: moved(a, lambda x, z, c: (x, z, c + 1))

    def near_row(row):
        return ((mine - row // rows) & (feat - 1)) * rows + row % rows

    patch = feat * rows
    slot = jnp.maximum(sender_slot - patch, 0)
    source, entry = slot // cap, slot % cap
    k = (x - source // (Z * C)) & (X - 1)
    dz = (z - source // C % Z) & (Z - 1)
    s = (source - c) & (C - 1)
    place = jnp.zeros_like(slot)
    base = 0
    for pairs in BATCHES:
        for at, pair in enumerate(pairs):
            for side, value in enumerate(pair):
                size = len(pairs) * 2 * cap
                here = base + (s * X + k) * size + at * 2 * cap + side * cap
                place = jnp.where(dz == value, here, place)
        base += X * C * len(pairs) * 2 * cap
    send = jnp.where(sender_slot < patch, near_row(sender_slot), patch + place + entry)
    recv = near_row(receivers).reshape(1, -1)
    before = edge_before(
        recv, send.reshape(1, -1), edge_b1.reshape(1, -1), parts, edges, edge_w1, groups[1][0]
    )
    arrived = groups[0] + groups[1]
    arrived = arrived + [swap(crossing(arrived, before))]
    edges_out, *sums = edge_after(
        patch, live_edges, send.reshape(-1, 1), recv, edge_gain.reshape(1, -1), arrived, before,
        edge_w1, edge_w2, edges, rows,
    )
    parts = [sums[0]]
    for k in range(1, feat):
        parts.append(lax.ppermute(sums[k], "feat", [(i, (i - k) % feat) for i in range(feat)]))
    nodes_out = node_update(
        nodes, parts, node_w1, node_b1.reshape(1, -1), node_w2, node_gain.reshape(1, -1)
    )
    return (edges_out, nodes_out)


def solution(mesh):
    placed = (
        P(("patch", "feat"), None),
        P(("patch", "feat"), None),
        P(("patch", "feat")),
        P(("patch", "feat")),
        P("patch", "feat", None, None),
        P(("patch", "feat")),
    ) + (P(),) * 8
    return jax.shard_map(
        local,
        mesh=mesh,
        in_specs=placed,
        out_specs=(P(("patch", "feat"), None), P(("patch", "feat"), None)),
        check_vma=False,
    )
```

```python
import jax
import jax.numpy as jnp
from jax import lax
from jax.experimental import pallas as pl
from jax.experimental.pallas import tpu as pltpu
from jax.sharding import PartitionSpec as P

epsilon = 1e-05
f32 = jnp.float32
bf16 = jnp.bfloat16
i32 = jnp.int32
TILES = 2
GATHERS = 1
LIMIT = 16 << 20
VMEM = pl.BlockSpec(memory_space=pltpu.VMEM)
SMEM = pl.BlockSpec(memory_space=pltpu.SMEM)
HBM = pl.BlockSpec(memory_space=pltpu.HBM)
ANY = pl.BlockSpec(memory_space=pl.ANY)
X, Z, C = 4, 8, 2
TAIL = 16
COST = 1 << 20
NEAR = (1, 3, 2)
FAR_FIRST = (2, 1, 3)
BATCHES = (((0, 1), (7, 2)), ((6, 3), (5, 4)))


def dot(left, right):
    return jnp.dot(left, right, preferred_element_type=f32)


def dot_first(left, right):
    return lax.dot_general(left, right, (((0,), (0,)), ((), ())), preferred_element_type=f32)


def silu(value):
    return value / (1.0 + jnp.exp(-value))


def layer_norm(values, scales):
    average = jnp.mean(values, axis=-1, keepdims=True)
    centred = values - average
    variance = jnp.mean(centred * centred, axis=-1, keepdims=True)
    return centred * lax.rsqrt(variance + epsilon) * scales


def as_bf16(mask):
    return mask.astype(f32).astype(bf16)


def hot_columns(row, count, first=0):
    ids = lax.broadcasted_iota(i32, (count, row.shape[1]), 0) + first
    return as_bf16(row == ids)


def hot_rows(column, count, first=0):
    ids = lax.broadcasted_iota(i32, (column.shape[0], count), 1) + first
    return as_bf16(column == ids)


def in_hbm(value):
    return pltpu.with_memory_space_constraint(value, pltpu.HBM)


def odd(dz):
    return (dz >= 1) & (dz <= 4)


def pack_kernel(where_ref, lists_ref, nodes_hbm, out_hbm, block_ref, sems):
    rows, latent = nodes_hbm.shape
    cap, peers = lists_ref.shape
    body = pltpu.make_async_copy(nodes_hbm, block_ref.at[pl.ds(0, rows)], sems.at[0])
    body.start()
    me = where_ref[0]
    x, z, c = me // (Z * C), me // C % Z, me % C
    lane = lax.broadcasted_iota(i32, (cap, latent), 1)
    spread = as_bf16(lane % cap == lax.broadcasted_iota(i32, (cap, latent), 0))
    listed = dot_first(lists_ref[...].astype(f32).astype(bf16), spread)
    peer = lax.broadcasted_iota(i32, (peers, latent), 0)
    lane = lax.broadcasted_iota(i32, (peers, latent), 1)
    k = (peer // (Z * C) - x) & (X - 1)
    dz = (peer // C % Z - z) & (Z - 1)
    s = (peer % C - c) & (C - 1)
    slot = (k * C + s) * 2 + jnp.where(odd(dz), 1, 0)
    listed = jnp.where(lane // cap == slot, listed + 1.0, 0.0).astype(bf16)
    row = lax.broadcasted_iota(i32, (TAIL, peers), 0)
    peer = lax.broadcasted_iota(i32, (TAIL, peers), 1)
    pick = as_bf16(row == ((peer // C % Z - z) & (Z - 1)))
    block_ref[rows:] = (dot(pick, listed) - 1.0).astype(bf16)
    body.wait()
    store = pltpu.make_async_copy(block_ref, out_hbm, sems.at[1])
    store.start()
    store.wait()


def pack(me, lists, nodes):
    return pl.pallas_call(
        pack_kernel,
        in_specs=[SMEM, VMEM, HBM],
        out_specs=HBM,
        out_shape=pltpu.HBM((nodes.shape[0] + TAIL, nodes.shape[1]), bf16),
        scratch_shapes=[
            pltpu.VMEM((nodes.shape[0] + TAIL, nodes.shape[1]), bf16),
            pltpu.SemaphoreType.DMA((2,)),
        ],
        name="pack",
    )(me, lists, in_hbm(nodes))


def select_kernel(pairs, cap, extra, *refs):
    count = 2 * len(pairs)
    blocks, outs = list(refs[:count]), refs[count + extra : count + extra + X]
    own = pairs[0][0] == 0
    if own:
        held, sem = refs[count + extra + X :]
        fetch = pltpu.make_async_copy(blocks[0], held, sem)
        fetch.start()
        blocks[0] = held
    rows = blocks[0].shape[0] - TAIL
    lanes = X * C * 2 * cap
    for at in reversed(range(len(pairs))):
        total = None
        for side, dz in reversed(list(enumerate(pairs[at]))):
            if dz == 0:
                fetch.wait()
            block = blocks[2 * at + side]
            wanted = block[rows:].astype(f32)[dz : dz + 1, :lanes].astype(i32)
            part = dot_first(hot_columns(wanted, rows), block[:rows])
            total = part if total is None else total + part
        total = total.astype(bf16)
        size = 2 * cap
        for k in range(X):
            for s in range(C):
                first = (k * C + s) * size
                put = (s * len(pairs) + at) * size
                outs[k][put : put + size] = total[first : first + size]


def select(pairs, cap, blocks, *earlier):
    latent = blocks[0].shape[1]
    shape = jax.ShapeDtypeStruct((C * len(pairs) * 2 * cap, latent), bf16)
    own = pairs[0][0] == 0
    blocks = list(blocks)
    if own:
        blocks[0] = in_hbm(blocks[0])
    return pl.pallas_call(
        lambda *refs: select_kernel(pairs, cap, len(earlier), *refs),
        in_specs=[HBM if own else VMEM] + [VMEM] * (len(blocks) - 1) + [ANY] * len(earlier),
        out_shape=[shape] * X,
        scratch_shapes=[pltpu.VMEM(blocks[0].shape, bf16), pltpu.SemaphoreType.DMA] if own else [],
        compiler_params=pltpu.CompilerParams(vmem_limit_bytes=LIMIT),
        cost_estimate=pl.CostEstimate(flops=COST, bytes_accessed=0, transcendentals=0),
        name="select",
    )(*blocks, *earlier)


def gate_kernel(*refs):
    pass


def gate(value, *earlier):
    return pl.pallas_call(
        gate_kernel,
        in_specs=[ANY] * (1 + len(earlier)),
        out_specs=ANY,
        out_shape=jax.ShapeDtypeStruct(value.shape, value.dtype),
        input_output_aliases={0: 0},
        compiler_params=pltpu.CompilerParams(vmem_limit_bytes=1 << 20),
        cost_estimate=pl.CostEstimate(flops=0, bytes_accessed=0, transcendentals=0),
        name="gate",
    )(value, *earlier)


def cross_kernel(*refs):
    out_ref = refs[-1]
    put = 0
    for ref in refs[:X]:
        size = ref.shape[0] // C
        out_ref[put : put + size] = ref[size:]
        put += size


def crossing(parts, *earlier):
    rows = sum(part.shape[0] for part in parts) // C
    return pl.pallas_call(
        cross_kernel,
        in_specs=[VMEM] * len(parts) + [HBM] * len(earlier),
        out_shape=jax.ShapeDtypeStruct((rows, parts[0].shape[1]), bf16),
        compiler_params=pltpu.CompilerParams(vmem_limit_bytes=LIMIT),
        name="crossing",
    )(*parts, *[in_hbm(part) for part in earlier])


def fill(table_ref, groups):
    put = 0
    for at in range(0, len(groups), X + 1):
        size = groups[at].shape[0] // C
        for part in groups[at : at + X]:
            table_ref[put : put + size] = part[:size]
            put += size
        table_ref[put : put + X * size] = groups[at + X][...]
        put += X * size


def before_kernel(extra, *refs):
    recv_ref, send_ref, b1_ref = refs[:3]
    parts = refs[3:7]
    edges_hbm, w1_hbm = refs[7:9]
    out_hbm, table_ref, edges_ref, w1_ref, out_ref, sems = refs[9 + extra :]
    loads = [
        pltpu.make_async_copy(w1_hbm, w1_ref, sems.at[0]),
        pltpu.make_async_copy(edges_hbm, edges_ref, sems.at[1]),
    ]
    for load in loads:
        load.start()
    count, latent = edges_ref.shape
    size = parts[0].shape[0]
    nodes = table_ref.shape[0]
    tile = count // TILES
    for k, part in enumerate(parts):
        table_ref[k * size : (k + 1) * size] = part[...]
    stores = []
    for at in range(TILES):
        rows = slice(at * tile, (at + 1) * tile)
        own = dot_first(hot_columns(recv_ref[:, rows], nodes), table_ref[...]).astype(bf16)
        near = dot_first(hot_columns(send_ref[:, rows], nodes), table_ref[...]).astype(bf16)
        if at == 0:
            for load in loads:
                load.wait()
        total = dot(edges_ref[rows], w1_ref[:latent])
        total = total + dot(near, w1_ref[latent : 2 * latent])
        total = total + dot(own, w1_ref[2 * latent :])
        out_ref[rows] = total + b1_ref[...]
        part = pl.ds(at * tile, tile)
        stores.append(pltpu.make_async_copy(out_ref.at[part], out_hbm.at[part], sems.at[2 + at]))
        stores[-1].start()
    for store in stores:
        store.wait()


def edge_before(recv, send, b1, parts, edges, w1, *earlier):
    count, latent = edges.shape
    nodes = sum(part.shape[0] for part in parts)
    return pl.pallas_call(
        lambda *refs: before_kernel(len(earlier), *refs),
        in_specs=[VMEM] * 7 + [HBM] * 2 + [ANY] * len(earlier),
        out_specs=HBM,
        out_shape=pltpu.HBM((count, latent), f32),
        scratch_shapes=[
            pltpu.VMEM((nodes, latent), bf16),
            pltpu.VMEM((count, latent), bf16),
            pltpu.VMEM(w1.shape, bf16),
            pltpu.VMEM((count, latent), f32),
            pltpu.SemaphoreType.DMA((2 + TILES,)),
        ],
        compiler_params=pltpu.CompilerParams(vmem_limit_bytes=32 << 20),
        cost_estimate=pl.CostEstimate(flops=COST, bytes_accessed=0, transcendentals=0),
        name="edge_before",
    )(recv, send, b1, *parts, in_hbm(edges), in_hbm(w1), *earlier)


def after_kernel(first_row, *refs):
    live_ref, send_ref, recv_ref, gain_ref = refs[:4]
    count = (X + 1) * len(BATCHES)
    groups, refs = refs[4 : 4 + count], refs[4 + count :]
    before_hbm, w1_hbm, w2_hbm, edges_hbm, out_hbm = refs[:5]
    sums_refs = refs[5:9]
    table_ref, before_ref, w1_ref, w2_ref, edges_ref, far_ref, load_sems, store_sems = refs[9:]
    count, latent = edges_ref.shape
    tile = count // TILES
    loads = [
        pltpu.make_async_copy(w1_hbm.at[pl.ds(latent, latent)], w1_ref, load_sems.at[0]),
        pltpu.make_async_copy(before_hbm, before_ref, load_sems.at[1]),
        pltpu.make_async_copy(w2_hbm, w2_ref, load_sems.at[2]),
        pltpu.make_async_copy(edges_hbm, edges_ref, load_sems.at[3]),
    ]
    for load in loads:
        load.start()
    fill(table_ref, groups)
    stores = []
    live = live_ref[0]
    size = count // GATHERS
    for at in range(GATHERS):
        rows = slice(at * size, (at + 1) * size)
        hot = hot_rows(send_ref[rows], table_ref.shape[0], first_row)
        far_ref[rows] = dot(hot, table_ref[...]).astype(bf16)
    for load in loads:
        load.wait()
    for at in range(TILES):
        rows = slice(at * tile, (at + 1) * tile)
        first = before_ref[rows] + dot(far_ref[rows], w1_ref[...])
        hidden = silu(first).astype(bf16)
        change = layer_norm(dot(hidden, w2_ref[...]), gain_ref[...])
        alive = lax.broadcasted_iota(i32, (tile, 1), 0) + at * tile < live
        edge = edges_ref[rows].astype(f32) + jnp.where(alive, change, 0.0)
        edges_ref[rows] = edge.astype(bf16)
        part = pl.ds(at * tile, tile)
        stores.append(
            pltpu.make_async_copy(edges_ref.at[part], out_hbm.at[part], store_sems.at[at])
        )
        stores[-1].start()
    alive = lax.broadcasted_iota(i32, (1, count), 1) < live
    receiver = jnp.where(alive, recv_ref[...], -1)
    size = sums_refs[0].shape[0]
    for at, ref in enumerate(sums_refs):
        hot = hot_columns(receiver, size, at * size)
        ref[...] = dot(hot, edges_ref[...]).astype(ref.dtype)
    for store in stores:
        store.wait()


def edge_after(cap, first_row, live, send, recv, gain, parts, before, w1, w2, edges, rows):
    count, latent = edges.shape
    table = X * Z * C * cap
    return pl.pallas_call(
        lambda *refs: after_kernel(first_row, *refs),
        in_specs=[SMEM] + [VMEM] * (3 + len(parts)) + [HBM] * 4,
        out_specs=[HBM] + [VMEM] * 4,
        out_shape=[jax.ShapeDtypeStruct((count, latent), bf16)]
        + [jax.ShapeDtypeStruct((rows, latent), f32 if k == 0 else bf16) for k in range(4)],
        scratch_shapes=[
            pltpu.VMEM((table, latent), bf16),
            pltpu.VMEM((count, latent), f32),
            pltpu.VMEM((latent, latent), bf16),
            pltpu.VMEM((latent, latent), bf16),
            pltpu.VMEM((count, latent), bf16),
            pltpu.VMEM((count, latent), bf16),
            pltpu.SemaphoreType.DMA((4,)),
            pltpu.SemaphoreType.DMA((TILES,)),
        ],
        compiler_params=pltpu.CompilerParams(vmem_limit_bytes=32 << 20),
        name="edge_after",
    )(live, send, recv, gain, *parts, *[in_hbm(part) for part in (before, w1, w2, edges)])


def node_kernel(nodes_ref, p0_ref, p1_ref, p2_ref, p3_ref, w1_ref, b1_ref, w2_ref, gain_ref, out_ref):
    latent = nodes_ref.shape[1]
    total = p0_ref[...].astype(f32) + p1_ref[...].astype(f32)
    total = total + p2_ref[...].astype(f32) + p3_ref[...].astype(f32)
    incoming = total.astype(bf16)
    nodes = nodes_ref[...]
    first = dot(nodes, w1_ref[:latent]) + dot(incoming, w1_ref[latent:])
    hidden = silu(first + b1_ref[...]).astype(bf16)
    change = layer_norm(dot(hidden, w2_ref[...]), gain_ref[...])
    out_ref[...] = (nodes.astype(f32) + change).astype(bf16)


def node_update(nodes, parts, w1, b1, w2, gain):
    return pl.pallas_call(
        node_kernel,
        in_specs=[VMEM] * 9,
        out_shape=jax.ShapeDtypeStruct(nodes.shape, bf16),
        compiler_params=pltpu.CompilerParams(vmem_limit_bytes=LIMIT),
        name="node_update",
    )(nodes, *parts, w1, b1, w2, gain)


def pairs_of(move):
    found = []
    for x in range(X):
        for z in range(Z):
            for c in range(C):
                tx, tz, tc = move(x, z, c)
                found.append(((x * Z + z) * C + c, ((tx % X) * Z + tz % Z) * C + tc % C))
    return found


def moved(value, move):
    return lax.ppermute(value, "patch", pairs_of(move))


def local(
    nodes,
    edges,
    receivers,
    sender_slot,
    send_rows,
    live_edges,
    edge_w1,
    edge_b1,
    edge_w2,
    edge_gain,
    node_w1,
    node_b1,
    node_w2,
    node_gain,
):
    rows, latent = nodes.shape
    cap = send_rows.shape[3]
    me = lax.axis_index("patch")
    mine = lax.axis_index("feat")
    x, z, c = me // (Z * C), me // C % Z, me % C
    feat = lax.axis_size("feat")

    block = pack(me.reshape(1), send_rows[0, 0].T, nodes)
    def around(value, k):
        return lax.ppermute(value, "feat", [(i, (i + k) % feat) for i in range(feat)])

    after_one = around(nodes, 1)
    parts = [nodes, after_one, around(after_one, 1), around(nodes, feat - 1)]
    up = lambda a: moved(a, lambda x, z, c: (x, z + 1, c))
    down = lambda a: moved(a, lambda x, z, c: (x, z - 1, c))
    held = {0: block}
    forth = back = block
    for hop in range(1, 4):
        forth, back = up(forth), down(back)
        forth = gate(forth, parts[NEAR[hop - 1]])
        held[hop], held[Z - hop] = forth, back
    held[4] = up(forth)

    groups = []
    for pairs in BATCHES:
        picked = select(pairs, cap, [held[dz] for pair in pairs for dz in pair])
        arrived = {0: picked[0]}
        for k in FAR_FIRST:
            arrived[k] = moved(picked[k], lambda x, z, c: (x + k, z, c))
        groups.append([arrived[k] for k in range(X)])
    swap = lambda a: moved(a, lambda x, z, c: (x, z, c + 1))

    def near_row(row):
        return ((mine - row // rows) & (feat - 1)) * rows + row % rows

    patch = feat * rows
    slot = jnp.maximum(sender_slot - patch, 0)
    source, entry = slot // cap, slot % cap
    k = (x - source // (Z * C)) & (X - 1)
    dz = (z - source // C % Z) & (Z - 1)
    s = (source - c) & (C - 1)
    place = jnp.zeros_like(slot)
    base = 0
    for pairs in BATCHES:
        for at, pair in enumerate(pairs):
            for side, value in enumerate(pair):
                size = len(pairs) * 2 * cap
                here = base + (s * X + k) * size + at * 2 * cap + side * cap
                place = jnp.where(dz == value, here, place)
        base += X * C * len(pairs) * 2 * cap
    send = jnp.where(sender_slot < patch, near_row(sender_slot), patch + place + entry)
    recv = near_row(receivers).reshape(1, -1)
    before = edge_before(
        recv, send.reshape(1, -1), edge_b1.reshape(1, -1), parts, edges, edge_w1, groups[1][0]
    )
    early = groups[0] + [swap(crossing(groups[0], before))]
    late = groups[1] + [swap(crossing(groups[1], before))]
    edges_out, *sums = edge_after(
        cap, patch, live_edges, send.reshape(-1, 1), recv, edge_gain.reshape(1, -1), early + late, before,
        edge_w1, edge_w2, edges, rows,
    )
    arrived = {0: sums[0]}
    for k in FAR_FIRST:
        arrived[k] = around(sums[k], feat - k)
    parts = [arrived[k] for k in range(feat)]
    nodes_out = node_update(
        nodes, parts, node_w1, node_b1.reshape(1, -1), node_w2, node_gain.reshape(1, -1)
    )
    return (edges_out, nodes_out)


def solution(mesh):
    placed = (
        P(("patch", "feat"), None),
        P(("patch", "feat"), None),
        P(("patch", "feat")),
        P(("patch", "feat")),
        P("patch", "feat", None, None),
        P(("patch", "feat")),
    ) + (P(),) * 8
    return jax.shard_map(
        local,
        mesh=mesh,
        in_specs=placed,
        out_specs=(P(("patch", "feat"), None), P(("patch", "feat"), None)),
        check_vma=False,
    )
```

```python
import jax
import jax.numpy as jnp
from jax import lax
from jax.experimental import pallas as pl
from jax.experimental.pallas import tpu as pltpu
from jax.sharding import PartitionSpec as P

epsilon = 1e-05
f32 = jnp.float32
bf16 = jnp.bfloat16
i32 = jnp.int32
TILES = 2
GATHERS = 1
LIMIT = 16 << 20
VMEM = pl.BlockSpec(memory_space=pltpu.VMEM)
SMEM = pl.BlockSpec(memory_space=pltpu.SMEM)
HBM = pl.BlockSpec(memory_space=pltpu.HBM)
ANY = pl.BlockSpec(memory_space=pl.ANY)
X, Z, C = 4, 8, 2
TAIL = 16
COST = 1 << 20
NEAR = (1, 3)
BATCHES = (((0, 1), (7, 2)), ((6, 3), (5, 4)))


def dot(left, right):
    return jnp.dot(left, right, preferred_element_type=f32)


def dot_first(left, right):
    return lax.dot_general(left, right, (((0,), (0,)), ((), ())), preferred_element_type=f32)


def silu(value):
    return value / (1.0 + jnp.exp(-value))


def layer_norm(values, scales):
    average = jnp.mean(values, axis=-1, keepdims=True)
    centred = values - average
    variance = jnp.mean(centred * centred, axis=-1, keepdims=True)
    return centred * lax.rsqrt(variance + epsilon) * scales


def as_bf16(mask):
    return mask.astype(f32).astype(bf16)


def hot_columns(row, count, first=0):
    ids = lax.broadcasted_iota(i32, (count, row.shape[1]), 0) + first
    return as_bf16(row == ids)


def hot_rows(column, count, first=0):
    ids = lax.broadcasted_iota(i32, (column.shape[0], count), 1) + first
    return as_bf16(column == ids)


def in_hbm(value):
    return pltpu.with_memory_space_constraint(value, pltpu.HBM)


def odd(dz):
    return (dz >= 1) & (dz <= 4)


def pack_kernel(where_ref, lists_ref, nodes_ref, out_ref):
    rows, latent = nodes_ref.shape
    cap, peers = lists_ref.shape
    out_ref[:rows] = nodes_ref[...]
    me = where_ref[0]
    x, z, c = me // (Z * C), me // C % Z, me % C
    lane = lax.broadcasted_iota(i32, (cap, latent), 1)
    spread = as_bf16(lane % cap == lax.broadcasted_iota(i32, (cap, latent), 0))
    listed = dot_first(lists_ref[...].astype(f32).astype(bf16), spread)
    peer = lax.broadcasted_iota(i32, (peers, latent), 0)
    lane = lax.broadcasted_iota(i32, (peers, latent), 1)
    k = (peer // (Z * C) - x) & (X - 1)
    dz = (peer // C % Z - z) & (Z - 1)
    s = (peer % C - c) & (C - 1)
    slot = (k * C + s) * 2 + jnp.where(odd(dz), 1, 0)
    listed = jnp.where(lane // cap == slot, listed + 1.0, 0.0).astype(bf16)
    row = lax.broadcasted_iota(i32, (TAIL, peers), 0)
    peer = lax.broadcasted_iota(i32, (TAIL, peers), 1)
    pick = as_bf16(row == ((peer // C % Z - z) & (Z - 1)))
    out_ref[rows:] = (dot(pick, listed) - 1.0).astype(bf16)


def pack(me, lists, nodes):
    return pl.pallas_call(
        pack_kernel,
        in_specs=[SMEM, VMEM, VMEM],
        out_shape=jax.ShapeDtypeStruct((nodes.shape[0] + TAIL, nodes.shape[1]), bf16),
        name="pack",
    )(me, lists, nodes)


def select_kernel(pairs, cap, extra, *refs):
    count = 2 * len(pairs)
    blocks, outs = list(refs[:count]), refs[count + extra : count + extra + X]
    own = pairs[0][0] == 0
    if own:
        held, sem = refs[count + extra + X :]
        fetch = pltpu.make_async_copy(blocks[0], held, sem)
        fetch.start()
        blocks[0] = held
    rows = blocks[0].shape[0] - TAIL
    lanes = X * C * 2 * cap
    for at in reversed(range(len(pairs))):
        total = None
        for side, dz in reversed(list(enumerate(pairs[at]))):
            if dz == 0:
                fetch.wait()
            block = blocks[2 * at + side]
            wanted = block[rows:].astype(f32)[dz : dz + 1, :lanes].astype(i32)
            part = dot_first(hot_columns(wanted, rows), block[:rows])
            total = part if total is None else total + part
        total = total.astype(bf16)
        size = 2 * cap
        for k in range(X):
            for s in range(C):
                first = (k * C + s) * size
                put = (s * len(pairs) + at) * size
                outs[k][put : put + size] = total[first : first + size]


def select(pairs, cap, blocks, *earlier):
    latent = blocks[0].shape[1]
    shape = jax.ShapeDtypeStruct((C * len(pairs) * 2 * cap, latent), bf16)
    own = pairs[0][0] == 0
    blocks = list(blocks)
    if own:
        blocks[0] = in_hbm(blocks[0])
    return pl.pallas_call(
        lambda *refs: select_kernel(pairs, cap, len(earlier), *refs),
        in_specs=[HBM if own else VMEM] + [VMEM] * (len(blocks) - 1) + [ANY] * len(earlier),
        out_shape=[shape] * X,
        scratch_shapes=[pltpu.VMEM(blocks[0].shape, bf16), pltpu.SemaphoreType.DMA] if own else [],
        compiler_params=pltpu.CompilerParams(vmem_limit_bytes=LIMIT),
        cost_estimate=pl.CostEstimate(flops=COST, bytes_accessed=0, transcendentals=0),
        name="select",
    )(*blocks, *earlier)


def gate_kernel(*refs):
    pass


def gate(value, *earlier):
    return pl.pallas_call(
        gate_kernel,
        in_specs=[ANY] * (1 + len(earlier)),
        out_specs=ANY,
        out_shape=jax.ShapeDtypeStruct(value.shape, value.dtype),
        input_output_aliases={0: 0},
        compiler_params=pltpu.CompilerParams(vmem_limit_bytes=1 << 20),
        cost_estimate=pl.CostEstimate(flops=0, bytes_accessed=0, transcendentals=0),
        name="gate",
    )(value, *earlier)


def cross_kernel(*refs):
    out_ref = refs[-1]
    put = 0
    for ref in refs[:X]:
        size = ref.shape[0] // C
        out_ref[put : put + size] = ref[size:]
        put += size


def crossing(parts, *earlier):
    rows = sum(part.shape[0] for part in parts) // C
    return pl.pallas_call(
        cross_kernel,
        in_specs=[VMEM] * len(parts) + [ANY] * len(earlier),
        out_shape=jax.ShapeDtypeStruct((rows, parts[0].shape[1]), bf16),
        compiler_params=pltpu.CompilerParams(vmem_limit_bytes=LIMIT),
        name="crossing",
    )(*parts, *earlier)


def fill(table_ref, groups):
    put = 0
    for at in range(0, len(groups), X + 1):
        size = groups[at].shape[0] // C
        for part in groups[at : at + X]:
            table_ref[put : put + size] = part[:size]
            put += size
        table_ref[put : put + X * size] = groups[at + X][...]
        put += X * size


def before_kernel(extra, *refs):
    recv_ref, send_ref, b1_ref = refs[:3]
    parts = refs[3:7]
    edges_hbm, w1_hbm = refs[7:9]
    out_hbm, table_ref, edges_ref, w1_ref, out_ref, sems = refs[9 + extra :]
    loads = [
        pltpu.make_async_copy(w1_hbm, w1_ref, sems.at[0]),
        pltpu.make_async_copy(edges_hbm, edges_ref, sems.at[1]),
    ]
    for load in loads:
        load.start()
    count, latent = edges_ref.shape
    size = parts[0].shape[0]
    nodes = table_ref.shape[0]
    tile = count // TILES
    for k, part in enumerate(parts):
        table_ref[k * size : (k + 1) * size] = part[...]
    stores = []
    for at in range(TILES):
        rows = slice(at * tile, (at + 1) * tile)
        own = dot_first(hot_columns(recv_ref[:, rows], nodes), table_ref[...]).astype(bf16)
        near = dot_first(hot_columns(send_ref[:, rows], nodes), table_ref[...]).astype(bf16)
        if at == 0:
            for load in loads:
                load.wait()
        total = dot(edges_ref[rows], w1_ref[:latent])
        total = total + dot(near, w1_ref[latent : 2 * latent])
        total = total + dot(own, w1_ref[2 * latent :])
        out_ref[rows] = total + b1_ref[...]
        part = pl.ds(at * tile, tile)
        stores.append(pltpu.make_async_copy(out_ref.at[part], out_hbm.at[part], sems.at[2 + at]))
        stores[-1].start()
    for store in stores:
        store.wait()


def edge_before(recv, send, b1, parts, edges, w1, *earlier):
    count, latent = edges.shape
    nodes = sum(part.shape[0] for part in parts)
    return pl.pallas_call(
        lambda *refs: before_kernel(len(earlier), *refs),
        in_specs=[VMEM] * 7 + [HBM] * 2 + [ANY] * len(earlier),
        out_specs=HBM,
        out_shape=pltpu.HBM((count, latent), f32),
        scratch_shapes=[
            pltpu.VMEM((nodes, latent), bf16),
            pltpu.VMEM((count, latent), bf16),
            pltpu.VMEM(w1.shape, bf16),
            pltpu.VMEM((count, latent), f32),
            pltpu.SemaphoreType.DMA((2 + TILES,)),
        ],
        compiler_params=pltpu.CompilerParams(vmem_limit_bytes=32 << 20),
        cost_estimate=pl.CostEstimate(flops=COST, bytes_accessed=0, transcendentals=0),
        name="edge_before",
    )(recv, send, b1, *parts, in_hbm(edges), in_hbm(w1), *earlier)


def after_kernel(first_row, *refs):
    live_ref, send_ref, recv_ref, gain_ref = refs[:4]
    count = (X + 1) * len(BATCHES)
    groups, refs = refs[4 : 4 + count], refs[4 + count :]
    before_hbm, w1_hbm, w2_hbm, edges_hbm, out_hbm = refs[:5]
    sums_refs = refs[5:9]
    table_ref, before_ref, w1_ref, w2_ref, edges_ref, far_ref, load_sems, store_sems = refs[9:]
    count, latent = edges_ref.shape
    tile = count // TILES
    loads = [
        pltpu.make_async_copy(w1_hbm.at[pl.ds(latent, latent)], w1_ref, load_sems.at[0]),
        pltpu.make_async_copy(before_hbm, before_ref, load_sems.at[1]),
        pltpu.make_async_copy(w2_hbm, w2_ref, load_sems.at[2]),
        pltpu.make_async_copy(edges_hbm, edges_ref, load_sems.at[3]),
    ]
    for load in loads:
        load.start()
    fill(table_ref, groups)
    stores = []
    live = live_ref[0]
    size = count // GATHERS
    for at in range(GATHERS):
        rows = slice(at * size, (at + 1) * size)
        hot = hot_rows(send_ref[rows], table_ref.shape[0], first_row)
        far_ref[rows] = dot(hot, table_ref[...]).astype(bf16)
    for load in loads:
        load.wait()
    for at in range(TILES):
        rows = slice(at * tile, (at + 1) * tile)
        first = before_ref[rows] + dot(far_ref[rows], w1_ref[...])
        hidden = silu(first).astype(bf16)
        change = layer_norm(dot(hidden, w2_ref[...]), gain_ref[...])
        alive = lax.broadcasted_iota(i32, (tile, 1), 0) + at * tile < live
        edge = edges_ref[rows].astype(f32) + jnp.where(alive, change, 0.0)
        edges_ref[rows] = edge.astype(bf16)
        part = pl.ds(at * tile, tile)
        stores.append(
            pltpu.make_async_copy(edges_ref.at[part], out_hbm.at[part], store_sems.at[at])
        )
        stores[-1].start()
    alive = lax.broadcasted_iota(i32, (1, count), 1) < live
    receiver = jnp.where(alive, recv_ref[...], -1)
    size = sums_refs[0].shape[0]
    for at, ref in enumerate(sums_refs):
        hot = hot_columns(receiver, size, at * size)
        ref[...] = dot(hot, edges_ref[...]).astype(ref.dtype)
    for store in stores:
        store.wait()


def edge_after(cap, first_row, live, send, recv, gain, parts, before, w1, w2, edges, rows):
    count, latent = edges.shape
    table = X * Z * C * cap
    return pl.pallas_call(
        lambda *refs: after_kernel(first_row, *refs),
        in_specs=[SMEM] + [VMEM] * (3 + len(parts)) + [HBM] * 4,
        out_specs=[HBM] + [VMEM] * 4,
        out_shape=[jax.ShapeDtypeStruct((count, latent), bf16)]
        + [jax.ShapeDtypeStruct((rows, latent), f32 if k == 0 else bf16) for k in range(4)],
        scratch_shapes=[
            pltpu.VMEM((table, latent), bf16),
            pltpu.VMEM((count, latent), f32),
            pltpu.VMEM((latent, latent), bf16),
            pltpu.VMEM((latent, latent), bf16),
            pltpu.VMEM((count, latent), bf16),
            pltpu.VMEM((count, latent), bf16),
            pltpu.SemaphoreType.DMA((4,)),
            pltpu.SemaphoreType.DMA((TILES,)),
        ],
        compiler_params=pltpu.CompilerParams(vmem_limit_bytes=32 << 20),
        name="edge_after",
    )(live, send, recv, gain, *parts, *[in_hbm(part) for part in (before, w1, w2, edges)])


def node_kernel(nodes_ref, p0_ref, p1_ref, p2_ref, p3_ref, w1_ref, b1_ref, w2_ref, gain_ref, out_ref):
    latent = nodes_ref.shape[1]
    total = p0_ref[...].astype(f32) + p1_ref[...].astype(f32)
    total = total + p2_ref[...].astype(f32) + p3_ref[...].astype(f32)
    incoming = total.astype(bf16)
    nodes = nodes_ref[...]
    first = dot(nodes, w1_ref[:latent]) + dot(incoming, w1_ref[latent:])
    hidden = silu(first + b1_ref[...]).astype(bf16)
    change = layer_norm(dot(hidden, w2_ref[...]), gain_ref[...])
    out_ref[...] = (nodes.astype(f32) + change).astype(bf16)


def node_update(nodes, parts, w1, b1, w2, gain):
    return pl.pallas_call(
        node_kernel,
        in_specs=[VMEM] * 9,
        out_shape=jax.ShapeDtypeStruct(nodes.shape, bf16),
        compiler_params=pltpu.CompilerParams(vmem_limit_bytes=LIMIT),
        name="node_update",
    )(nodes, *parts, w1, b1, w2, gain)


def pairs_of(move):
    found = []
    for x in range(X):
        for z in range(Z):
            for c in range(C):
                tx, tz, tc = move(x, z, c)
                found.append(((x * Z + z) * C + c, ((tx % X) * Z + tz % Z) * C + tc % C))
    return found


def moved(value, move):
    return lax.ppermute(value, "patch", pairs_of(move))


def local(
    nodes,
    edges,
    receivers,
    sender_slot,
    send_rows,
    live_edges,
    edge_w1,
    edge_b1,
    edge_w2,
    edge_gain,
    node_w1,
    node_b1,
    node_w2,
    node_gain,
):
    rows, latent = nodes.shape
    cap = send_rows.shape[3]
    me = lax.axis_index("patch")
    mine = lax.axis_index("feat")
    x, z, c = me // (Z * C), me // C % Z, me % C
    feat = lax.axis_size("feat")

    block = pack(me.reshape(1), send_rows[0, 0].T, nodes)
    def around(value, k):
        return lax.ppermute(value, "feat", [(i, (i + k) % feat) for i in range(feat)])

    after_one = around(nodes, 1)
    parts = [nodes, after_one, around(after_one, 1), around(nodes, feat - 1)]
    up = lambda a: moved(a, lambda x, z, c: (x, z + 1, c))
    down = lambda a: moved(a, lambda x, z, c: (x, z - 1, c))
    held = {0: block}
    forth = back = block
    for hop in range(1, 4):
        forth, back = up(forth), down(back)
        if hop < 3:
            forth = gate(forth, parts[NEAR[hop - 1]])
        held[hop], held[Z - hop] = forth, back
    held[4] = up(forth)

    groups = []
    for pairs in BATCHES:
        earlier = [parts[2]] if pairs is BATCHES[1] else []
        picked = select(pairs, cap, [held[dz] for pair in pairs for dz in pair], *earlier)
        arrived = {0: picked[0]}
        for k in range(1, X):
            arrived[k] = moved(picked[k], lambda x, z, c: (x + k, z, c))
        groups.append([arrived[k] for k in range(X)])
    swap = lambda a: moved(a, lambda x, z, c: (x, z, c + 1))

    def near_row(row):
        return ((mine - row // rows) & (feat - 1)) * rows + row % rows

    patch = feat * rows
    slot = jnp.maximum(sender_slot - patch, 0)
    source, entry = slot // cap, slot % cap
    k = (x - source // (Z * C)) & (X - 1)
    dz = (z - source // C % Z) & (Z - 1)
    s = (source - c) & (C - 1)
    place = jnp.zeros_like(slot)
    base = 0
    for pairs in BATCHES:
        for at, pair in enumerate(pairs):
            for side, value in enumerate(pair):
                size = len(pairs) * 2 * cap
                here = base + (s * X + k) * size + at * 2 * cap + side * cap
                place = jnp.where(dz == value, here, place)
        base += X * C * len(pairs) * 2 * cap
    send = jnp.where(sender_slot < patch, near_row(sender_slot), patch + place + entry)
    recv = near_row(receivers).reshape(1, -1)
    crossed = crossing(groups[0], groups[1][0])
    before = edge_before(
        recv, send.reshape(1, -1), edge_b1.reshape(1, -1), parts, edges, edge_w1, crossed
    )
    early = groups[0] + [swap(crossed)]
    late = groups[1] + [swap(crossing(groups[1], in_hbm(before)))]
    edges_out, *sums = edge_after(
        cap, patch, live_edges, send.reshape(-1, 1), recv, edge_gain.reshape(1, -1), early + late, before,
        edge_w1, edge_w2, edges, rows,
    )
    arrived = {0: sums[0]}
    for k in range(1, feat):
        arrived[k] = around(sums[k], feat - k)
    parts = [arrived[k] for k in range(feat)]
    nodes_out = node_update(
        nodes, parts, node_w1, node_b1.reshape(1, -1), node_w2, node_gain.reshape(1, -1)
    )
    return (edges_out, nodes_out)


def solution(mesh):
    placed = (
        P(("patch", "feat"), None),
        P(("patch", "feat"), None),
        P(("patch", "feat")),
        P(("patch", "feat")),
        P("patch", "feat", None, None),
        P(("patch", "feat")),
    ) + (P(),) * 8
    return jax.shard_map(
        local,
        mesh=mesh,
        in_specs=placed,
        out_specs=(P(("patch", "feat"), None), P(("patch", "feat"), None)),
        check_vma=False,
    )
```

```python
import jax
import jax.numpy as jnp
from jax import lax
from jax.experimental import pallas as pl
from jax.experimental.pallas import tpu as pltpu
from jax.sharding import PartitionSpec as P

epsilon = 1e-05
f32 = jnp.float32
bf16 = jnp.bfloat16
i32 = jnp.int32
TILES = 2
BEFORE_TILES = 2
GATHERS = 1
LIMIT = 16 << 20
VMEM = pl.BlockSpec(memory_space=pltpu.VMEM)
SMEM = pl.BlockSpec(memory_space=pltpu.SMEM)
HBM = pl.BlockSpec(memory_space=pltpu.HBM)
ANY = pl.BlockSpec(memory_space=pl.ANY)
X, Z, C = 4, 8, 2
TAIL = 16
COST = 1 << 20
NEAR = (1, 3)
BATCHES = (((0, 1), (7, 2)), ((6, 3), (5, 4)))


def dot(left, right):
    return jnp.dot(left, right, preferred_element_type=f32)


def dot_first(left, right):
    return lax.dot_general(left, right, (((0,), (0,)), ((), ())), preferred_element_type=f32)


def silu(value):
    return value / (1.0 + jnp.exp(-value))


def layer_norm(values, scales):
    average = jnp.mean(values, axis=-1, keepdims=True)
    centred = values - average
    variance = jnp.mean(centred * centred, axis=-1, keepdims=True)
    return centred * lax.rsqrt(variance + epsilon) * scales


def as_bf16(mask):
    return mask.astype(f32).astype(bf16)


def hot_columns(row, count, first=0):
    ids = lax.broadcasted_iota(i32, (count, row.shape[1]), 0) + first
    return as_bf16(row == ids)


def hot_rows(column, count, first=0):
    ids = lax.broadcasted_iota(i32, (column.shape[0], count), 1) + first
    return as_bf16(column == ids)


def in_hbm(value):
    return pltpu.with_memory_space_constraint(value, pltpu.HBM)


def odd(dz):
    return (dz >= 1) & (dz <= 4)


def pack_kernel(where_ref, lists_ref, nodes_ref, out_ref):
    rows, latent = nodes_ref.shape
    cap, peers = lists_ref.shape
    out_ref[:rows] = nodes_ref[...]
    me = where_ref[0]
    x, z, c = me // (Z * C), me // C % Z, me % C
    lane = lax.broadcasted_iota(i32, (cap, latent), 1)
    spread = as_bf16(lane % cap == lax.broadcasted_iota(i32, (cap, latent), 0))
    listed = dot_first(lists_ref[...].astype(f32).astype(bf16), spread)
    peer = lax.broadcasted_iota(i32, (peers, latent), 0)
    lane = lax.broadcasted_iota(i32, (peers, latent), 1)
    k = (peer // (Z * C) - x) & (X - 1)
    dz = (peer // C % Z - z) & (Z - 1)
    s = (peer % C - c) & (C - 1)
    slot = (k * C + s) * 2 + jnp.where(odd(dz), 1, 0)
    listed = jnp.where(lane // cap == slot, listed + 1.0, 0.0).astype(bf16)
    row = lax.broadcasted_iota(i32, (TAIL, peers), 0)
    peer = lax.broadcasted_iota(i32, (TAIL, peers), 1)
    pick = as_bf16(row == ((peer // C % Z - z) & (Z - 1)))
    out_ref[rows:] = (dot(pick, listed) - 1.0).astype(bf16)


def pack(me, lists, nodes):
    return pl.pallas_call(
        pack_kernel,
        in_specs=[SMEM, VMEM, VMEM],
        out_shape=jax.ShapeDtypeStruct((nodes.shape[0] + TAIL, nodes.shape[1]), bf16),
        name="pack",
    )(me, lists, nodes)


def select_kernel(pairs, cap, extra, *refs):
    count = 2 * len(pairs)
    blocks, outs = list(refs[:count]), refs[count + extra : count + extra + X]
    own = pairs[0][0] == 0
    if own:
        held, sem = refs[count + extra + X :]
        fetch = pltpu.make_async_copy(blocks[0], held, sem)
        fetch.start()
        blocks[0] = held
    rows = blocks[0].shape[0] - TAIL
    lanes = X * C * 2 * cap
    for at in reversed(range(len(pairs))):
        total = None
        for side, dz in reversed(list(enumerate(pairs[at]))):
            if dz == 0:
                fetch.wait()
            block = blocks[2 * at + side]
            wanted = block[rows:].astype(f32)[dz : dz + 1, :lanes].astype(i32)
            part = dot_first(hot_columns(wanted, rows), block[:rows])
            total = part if total is None else total + part
        total = total.astype(bf16)
        size = 2 * cap
        for k in range(X):
            for s in range(C):
                first = (k * C + s) * size
                put = (s * len(pairs) + at) * size
                outs[k][put : put + size] = total[first : first + size]


def select(pairs, cap, blocks, *earlier):
    latent = blocks[0].shape[1]
    shape = jax.ShapeDtypeStruct((C * len(pairs) * 2 * cap, latent), bf16)
    own = pairs[0][0] == 0
    blocks = list(blocks)
    if own:
        blocks[0] = in_hbm(blocks[0])
    return pl.pallas_call(
        lambda *refs: select_kernel(pairs, cap, len(earlier), *refs),
        in_specs=[HBM if own else VMEM] + [VMEM] * (len(blocks) - 1) + [ANY] * len(earlier),
        out_shape=[shape] * X,
        scratch_shapes=[pltpu.VMEM(blocks[0].shape, bf16), pltpu.SemaphoreType.DMA] if own else [],
        compiler_params=pltpu.CompilerParams(vmem_limit_bytes=LIMIT),
        cost_estimate=pl.CostEstimate(flops=COST, bytes_accessed=0, transcendentals=0),
        name="select",
    )(*blocks, *earlier)


def gate_kernel(*refs):
    pass


def gate(value, *earlier):
    return pl.pallas_call(
        gate_kernel,
        in_specs=[ANY] * (1 + len(earlier)),
        out_specs=ANY,
        out_shape=jax.ShapeDtypeStruct(value.shape, value.dtype),
        input_output_aliases={0: 0},
        compiler_params=pltpu.CompilerParams(vmem_limit_bytes=1 << 20),
        cost_estimate=pl.CostEstimate(flops=0, bytes_accessed=0, transcendentals=0),
        name="gate",
    )(value, *earlier)


def cross_kernel(*refs):
    out_ref = refs[-1]
    put = 0
    for ref in refs[:X]:
        size = ref.shape[0] // C
        out_ref[put : put + size] = ref[size:]
        put += size


def crossing(parts, *earlier):
    rows = sum(part.shape[0] for part in parts) // C
    return pl.pallas_call(
        cross_kernel,
        in_specs=[VMEM] * len(parts) + [HBM] * len(earlier),
        out_shape=jax.ShapeDtypeStruct((rows, parts[0].shape[1]), bf16),
        compiler_params=pltpu.CompilerParams(vmem_limit_bytes=LIMIT),
        name="crossing",
    )(*parts, *earlier)


def fill(table_ref, groups):
    put = 0
    for at in range(0, len(groups), X + 1):
        size = groups[at].shape[0] // C
        for part in groups[at : at + X]:
            table_ref[put : put + size] = part[:size]
            put += size
        table_ref[put : put + X * size] = groups[at + X][...]
        put += X * size


def before_kernel(extra, *refs):
    recv_ref, send_ref, b1_ref = refs[:3]
    parts = refs[3:7]
    edges_hbm, w1_hbm = refs[7:9]
    out_hbm, table_ref, edges_ref, w1_ref, out_ref, sems = refs[9 + extra :]
    count, latent = edges_ref.shape
    size = parts[0].shape[0]
    nodes = table_ref.shape[0]
    tile = count // BEFORE_TILES
    loads = [pltpu.make_async_copy(w1_hbm, w1_ref, sems.at[0])]
    for at in range(BEFORE_TILES):
        part = pl.ds(at * tile, tile)
        loads.append(
            pltpu.make_async_copy(edges_hbm.at[part], edges_ref.at[part], sems.at[1 + at])
        )
    for load in loads:
        load.start()
    for k, part in enumerate(parts):
        table_ref[k * size : (k + 1) * size] = part[...]
    stores = []
    for at in range(BEFORE_TILES):
        rows = slice(at * tile, (at + 1) * tile)
        own = dot_first(hot_columns(recv_ref[:, rows], nodes), table_ref[...]).astype(bf16)
        near = dot_first(hot_columns(send_ref[:, rows], nodes), table_ref[...]).astype(bf16)
        if at == 0:
            loads[0].wait()
        loads[1 + at].wait()
        total = dot(edges_ref[rows], w1_ref[:latent])
        total = total + dot(near, w1_ref[latent : 2 * latent])
        total = total + dot(own, w1_ref[2 * latent :])
        out_ref[rows] = total + b1_ref[...]
        part = pl.ds(at * tile, tile)
        stores.append(pltpu.make_async_copy(out_ref.at[part], out_hbm.at[part], sems.at[1 + BEFORE_TILES + at]))
        stores[-1].start()
    for store in stores:
        store.wait()


def edge_before(recv, send, b1, parts, edges, w1, *earlier):
    count, latent = edges.shape
    nodes = sum(part.shape[0] for part in parts)
    return pl.pallas_call(
        lambda *refs: before_kernel(len(earlier), *refs),
        in_specs=[VMEM] * 7 + [HBM] * 2 + [ANY] * len(earlier),
        out_specs=HBM,
        out_shape=pltpu.HBM((count, latent), f32),
        scratch_shapes=[
            pltpu.VMEM((nodes, latent), bf16),
            pltpu.VMEM((count, latent), bf16),
            pltpu.VMEM(w1.shape, bf16),
            pltpu.VMEM((count, latent), f32),
            pltpu.SemaphoreType.DMA((1 + 2 * BEFORE_TILES,)),
        ],
        compiler_params=pltpu.CompilerParams(vmem_limit_bytes=32 << 20),
        cost_estimate=pl.CostEstimate(flops=COST, bytes_accessed=0, transcendentals=0),
        name="edge_before",
    )(recv, send, b1, *parts, in_hbm(edges), in_hbm(w1), *earlier)


def after_kernel(first_row, *refs):
    live_ref, send_ref, recv_ref, gain_ref = refs[:4]
    count = (X + 1) * len(BATCHES)
    groups, refs = refs[4 : 4 + count], refs[4 + count :]
    before_hbm, w1_hbm, w2_hbm, edges_hbm, out_hbm = refs[:5]
    sums_refs = refs[5:9]
    table_ref, before_ref, w1_ref, w2_ref, edges_ref, far_ref, load_sems, store_sems = refs[9:]
    count, latent = edges_ref.shape
    tile = count // TILES
    loads = [
        pltpu.make_async_copy(w1_hbm.at[pl.ds(latent, latent)], w1_ref, load_sems.at[0]),
        pltpu.make_async_copy(before_hbm, before_ref, load_sems.at[1]),
        pltpu.make_async_copy(w2_hbm, w2_ref, load_sems.at[2]),
        pltpu.make_async_copy(edges_hbm, edges_ref, load_sems.at[3]),
    ]
    for load in loads:
        load.start()
    fill(table_ref, groups)
    stores = []
    live = live_ref[0]
    size = count // GATHERS
    for at in range(GATHERS):
        rows = slice(at * size, (at + 1) * size)
        hot = hot_rows(send_ref[rows], table_ref.shape[0], first_row)
        far_ref[rows] = dot(hot, table_ref[...]).astype(bf16)
    for load in loads:
        load.wait()
    for at in range(TILES):
        rows = slice(at * tile, (at + 1) * tile)
        first = before_ref[rows] + dot(far_ref[rows], w1_ref[...])
        hidden = silu(first).astype(bf16)
        change = layer_norm(dot(hidden, w2_ref[...]), gain_ref[...])
        alive = lax.broadcasted_iota(i32, (tile, 1), 0) + at * tile < live
        edge = edges_ref[rows].astype(f32) + jnp.where(alive, change, 0.0)
        edges_ref[rows] = edge.astype(bf16)
        part = pl.ds(at * tile, tile)
        stores.append(
            pltpu.make_async_copy(edges_ref.at[part], out_hbm.at[part], store_sems.at[at])
        )
        stores[-1].start()
    alive = lax.broadcasted_iota(i32, (1, count), 1) < live
    receiver = jnp.where(alive, recv_ref[...], -1)
    size = sums_refs[0].shape[0]
    for at, ref in enumerate(sums_refs):
        hot = hot_columns(receiver, size, at * size)
        ref[...] = dot(hot, edges_ref[...]).astype(ref.dtype)
    for store in stores:
        store.wait()


def edge_after(cap, first_row, live, send, recv, gain, parts, before, w1, w2, edges, rows):
    count, latent = edges.shape
    table = X * Z * C * cap
    return pl.pallas_call(
        lambda *refs: after_kernel(first_row, *refs),
        in_specs=[SMEM] + [VMEM] * (3 + len(parts)) + [HBM] * 4,
        out_specs=[HBM] + [VMEM] * 4,
        out_shape=[jax.ShapeDtypeStruct((count, latent), bf16)]
        + [jax.ShapeDtypeStruct((rows, latent), f32 if k == 0 else bf16) for k in range(4)],
        scratch_shapes=[
            pltpu.VMEM((table, latent), bf16),
            pltpu.VMEM((count, latent), f32),
            pltpu.VMEM((latent, latent), bf16),
            pltpu.VMEM((latent, latent), bf16),
            pltpu.VMEM((count, latent), bf16),
            pltpu.VMEM((count, latent), bf16),
            pltpu.SemaphoreType.DMA((4,)),
            pltpu.SemaphoreType.DMA((TILES,)),
        ],
        compiler_params=pltpu.CompilerParams(vmem_limit_bytes=32 << 20),
        name="edge_after",
    )(live, send, recv, gain, *parts, *[in_hbm(part) for part in (before, w1, w2, edges)])


def node_kernel(nodes_ref, p0_ref, p1_ref, p2_ref, p3_ref, w1_ref, b1_ref, w2_ref, gain_ref, out_ref):
    latent = nodes_ref.shape[1]
    total = p0_ref[...].astype(f32) + p1_ref[...].astype(f32)
    total = total + p2_ref[...].astype(f32) + p3_ref[...].astype(f32)
    incoming = total.astype(bf16)
    nodes = nodes_ref[...]
    first = dot(nodes, w1_ref[:latent]) + dot(incoming, w1_ref[latent:])
    hidden = silu(first + b1_ref[...]).astype(bf16)
    change = layer_norm(dot(hidden, w2_ref[...]), gain_ref[...])
    out_ref[...] = (nodes.astype(f32) + change).astype(bf16)


def node_update(nodes, parts, w1, b1, w2, gain):
    return pl.pallas_call(
        node_kernel,
        in_specs=[VMEM] * 9,
        out_shape=jax.ShapeDtypeStruct(nodes.shape, bf16),
        compiler_params=pltpu.CompilerParams(vmem_limit_bytes=LIMIT),
        name="node_update",
    )(nodes, *parts, w1, b1, w2, gain)


def pairs_of(move):
    found = []
    for x in range(X):
        for z in range(Z):
            for c in range(C):
                tx, tz, tc = move(x, z, c)
                found.append(((x * Z + z) * C + c, ((tx % X) * Z + tz % Z) * C + tc % C))
    return found


def moved(value, move):
    return lax.ppermute(value, "patch", pairs_of(move))


def local(
    nodes,
    edges,
    receivers,
    sender_slot,
    send_rows,
    live_edges,
    edge_w1,
    edge_b1,
    edge_w2,
    edge_gain,
    node_w1,
    node_b1,
    node_w2,
    node_gain,
):
    rows, latent = nodes.shape
    cap = send_rows.shape[3]
    me = lax.axis_index("patch")
    mine = lax.axis_index("feat")
    x, z, c = me // (Z * C), me // C % Z, me % C
    feat = lax.axis_size("feat")

    block = pack(me.reshape(1), send_rows[0, 0].T, nodes)
    def around(value, k):
        return lax.ppermute(value, "feat", [(i, (i + k) % feat) for i in range(feat)])

    after_one = around(nodes, 1)
    parts = [nodes, after_one, around(after_one, 1), around(nodes, feat - 1)]
    up = lambda a: moved(a, lambda x, z, c: (x, z + 1, c))
    down = lambda a: moved(a, lambda x, z, c: (x, z - 1, c))
    held = {0: block}
    forth = back = block
    for hop in range(1, 4):
        forth, back = up(forth), down(back)
        if hop < 3:
            forth = gate(forth, parts[NEAR[hop - 1]])
        held[hop], held[Z - hop] = forth, back
    held[4] = up(forth)

    groups = []
    for pairs in BATCHES:
        earlier = [parts[2]] if pairs is BATCHES[1] else []
        picked = select(pairs, cap, [held[dz] for pair in pairs for dz in pair], *earlier)
        arrived = {0: picked[0]}
        for k in range(1, X):
            arrived[k] = moved(picked[k], lambda x, z, c: (x + k, z, c))
        groups.append([arrived[k] for k in range(X)])
    swap = lambda a: moved(a, lambda x, z, c: (x, z, c + 1))

    def near_row(row):
        return ((mine - row // rows) & (feat - 1)) * rows + row % rows

    patch = feat * rows
    slot = jnp.maximum(sender_slot - patch, 0)
    source, entry = slot // cap, slot % cap
    k = (x - source // (Z * C)) & (X - 1)
    dz = (z - source // C % Z) & (Z - 1)
    s = (source - c) & (C - 1)
    place = jnp.zeros_like(slot)
    base = 0
    for pairs in BATCHES:
        for at, pair in enumerate(pairs):
            for side, value in enumerate(pair):
                size = len(pairs) * 2 * cap
                here = base + (s * X + k) * size + at * 2 * cap + side * cap
                place = jnp.where(dz == value, here, place)
        base += X * C * len(pairs) * 2 * cap
    send = jnp.where(sender_slot < patch, near_row(sender_slot), patch + place + entry)
    recv = near_row(receivers).reshape(1, -1)
    before = edge_before(
        recv, send.reshape(1, -1), edge_b1.reshape(1, -1), parts, edges, edge_w1, groups[1][0]
    )
    early = groups[0] + [swap(crossing(groups[0], in_hbm(before)))]
    late = groups[1] + [swap(crossing(groups[1], in_hbm(before)))]
    edges_out, *sums = edge_after(
        cap, patch, live_edges, send.reshape(-1, 1), recv, edge_gain.reshape(1, -1), early + late, before,
        edge_w1, edge_w2, edges, rows,
    )
    arrived = {0: sums[0]}
    for k in range(1, feat):
        arrived[k] = around(sums[k], feat - k)
    parts = [arrived[k] for k in range(feat)]
    nodes_out = node_update(
        nodes, parts, node_w1, node_b1.reshape(1, -1), node_w2, node_gain.reshape(1, -1)
    )
    return (edges_out, nodes_out)


def solution(mesh):
    placed = (
        P(("patch", "feat"), None),
        P(("patch", "feat"), None),
        P(("patch", "feat")),
        P(("patch", "feat")),
        P("patch", "feat", None, None),
        P(("patch", "feat")),
    ) + (P(),) * 8
    return jax.shard_map(
        local,
        mesh=mesh,
        in_specs=placed,
        out_specs=(P(("patch", "feat"), None), P(("patch", "feat"), None)),
        check_vma=False,
    )
```

```python
import jax
import jax.numpy as jnp
from jax import lax
from jax.experimental import pallas as pl
from jax.experimental.pallas import tpu as pltpu
from jax.sharding import PartitionSpec as P

epsilon = 1e-05
f32 = jnp.float32
bf16 = jnp.bfloat16
i32 = jnp.int32
TILES = 2
BEFORE_TILES = 2
GATHERS = 1
LIMIT = 16 << 20
VMEM = pl.BlockSpec(memory_space=pltpu.VMEM)
SMEM = pl.BlockSpec(memory_space=pltpu.SMEM)
HBM = pl.BlockSpec(memory_space=pltpu.HBM)
ANY = pl.BlockSpec(memory_space=pl.ANY)
X, Z, C = 4, 8, 2
TAIL = 16
COST = 1 << 20
NEAR = (1, 3)
BATCHES = (((0, 1), (7, 2)), ((6, 3), (5, 4)))


def dot(left, right):
    return jnp.dot(left, right, preferred_element_type=f32)


def dot_first(left, right):
    return lax.dot_general(left, right, (((0,), (0,)), ((), ())), preferred_element_type=f32)


def silu(value):
    return value / (1.0 + jnp.exp(-value))


def layer_norm(values, scales):
    average = jnp.mean(values, axis=-1, keepdims=True)
    centred = values - average
    variance = jnp.mean(centred * centred, axis=-1, keepdims=True)
    return centred * lax.rsqrt(variance + epsilon) * scales


def as_bf16(mask):
    return mask.astype(f32).astype(bf16)


def hot_columns(row, count, first=0):
    ids = lax.broadcasted_iota(i32, (count, row.shape[1]), 0) + first
    return as_bf16(row == ids)


def hot_rows(column, count, first=0):
    ids = lax.broadcasted_iota(i32, (column.shape[0], count), 1) + first
    return as_bf16(column == ids)


def in_hbm(value):
    return pltpu.with_memory_space_constraint(value, pltpu.HBM)


def odd(dz):
    return (dz >= 1) & (dz <= 4)


def pack_kernel(where_ref, lists_hbm, nodes_hbm, out_ref, lists_ref, sems):
    rows, latent = nodes_hbm.shape
    cap, peers = lists_ref.shape
    body = pltpu.make_async_copy(nodes_hbm, out_ref.at[pl.ds(0, rows)], sems.at[0])
    body.start()
    load = pltpu.make_async_copy(lists_hbm, lists_ref, sems.at[1])
    load.start()
    load.wait()
    me = where_ref[0]
    x, z, c = me // (Z * C), me // C % Z, me % C
    lane = lax.broadcasted_iota(i32, (cap, latent), 1)
    spread = as_bf16(lane % cap == lax.broadcasted_iota(i32, (cap, latent), 0))
    listed = dot_first(lists_ref[...].astype(f32).astype(bf16), spread)
    peer = lax.broadcasted_iota(i32, (peers, latent), 0)
    lane = lax.broadcasted_iota(i32, (peers, latent), 1)
    k = (peer // (Z * C) - x) & (X - 1)
    dz = (peer // C % Z - z) & (Z - 1)
    s = (peer % C - c) & (C - 1)
    slot = (k * C + s) * 2 + jnp.where(odd(dz), 1, 0)
    listed = jnp.where(lane // cap == slot, listed + 1.0, 0.0).astype(bf16)
    row = lax.broadcasted_iota(i32, (TAIL, peers), 0)
    peer = lax.broadcasted_iota(i32, (TAIL, peers), 1)
    pick = as_bf16(row == ((peer // C % Z - z) & (Z - 1)))
    out_ref[rows:] = (dot(pick, listed) - 1.0).astype(bf16)
    body.wait()


def pack(me, lists, nodes):
    return pl.pallas_call(
        pack_kernel,
        in_specs=[SMEM, HBM, HBM],
        out_specs=VMEM,
        out_shape=jax.ShapeDtypeStruct((nodes.shape[0] + TAIL, nodes.shape[1]), bf16),
        scratch_shapes=[pltpu.VMEM(lists.shape, i32), pltpu.SemaphoreType.DMA((2,))],
        compiler_params=pltpu.CompilerParams(vmem_limit_bytes=4 << 20),
        name="pack",
    )(me, in_hbm(lists), in_hbm(nodes))


def select_kernel(pairs, cap, extra, *refs):
    count = 2 * len(pairs)
    blocks, outs = list(refs[:count]), refs[count + extra : count + extra + X]
    rows = blocks[0].shape[0] - TAIL
    lanes = X * C * 2 * cap
    for at in range(len(pairs)):
        total = None
        for side, dz in enumerate(pairs[at]):
            block = blocks[2 * at + side]
            wanted = block[rows:].astype(f32)[dz : dz + 1, :lanes].astype(i32)
            part = dot_first(hot_columns(wanted, rows), block[:rows])
            total = part if total is None else total + part
        total = total.astype(bf16)
        size = 2 * cap
        for k in range(X):
            for s in range(C):
                first = (k * C + s) * size
                put = (s * len(pairs) + at) * size
                outs[k][put : put + size] = total[first : first + size]


def select(pairs, cap, blocks, *earlier):
    latent = blocks[0].shape[1]
    shape = jax.ShapeDtypeStruct((C * len(pairs) * 2 * cap, latent), bf16)
    return pl.pallas_call(
        lambda *refs: select_kernel(pairs, cap, len(earlier), *refs),
        in_specs=[VMEM] * len(blocks) + [ANY] * len(earlier),
        out_shape=[shape] * X,
        compiler_params=pltpu.CompilerParams(vmem_limit_bytes=LIMIT),
        cost_estimate=pl.CostEstimate(flops=COST, bytes_accessed=0, transcendentals=0),
        name="select",
    )(*blocks, *earlier)


def gate_kernel(*refs):
    pass


def gate(value, *earlier):
    return pl.pallas_call(
        gate_kernel,
        in_specs=[ANY] * (1 + len(earlier)),
        out_specs=ANY,
        out_shape=jax.ShapeDtypeStruct(value.shape, value.dtype),
        input_output_aliases={0: 0},
        compiler_params=pltpu.CompilerParams(vmem_limit_bytes=1 << 20),
        cost_estimate=pl.CostEstimate(flops=0, bytes_accessed=0, transcendentals=0),
        name="gate",
    )(value, *earlier)


def cross_kernel(*refs):
    out_ref = refs[-1]
    put = 0
    for ref in refs[:X]:
        size = ref.shape[0] // C
        out_ref[put : put + size] = ref[size:]
        put += size


def crossing(parts, *earlier):
    rows = sum(part.shape[0] for part in parts) // C
    return pl.pallas_call(
        cross_kernel,
        in_specs=[VMEM] * len(parts) + [HBM] * len(earlier),
        out_shape=jax.ShapeDtypeStruct((rows, parts[0].shape[1]), bf16),
        compiler_params=pltpu.CompilerParams(vmem_limit_bytes=LIMIT),
        name="crossing",
    )(*parts, *earlier)


def fill(table_ref, groups):
    put = 0
    for at in range(0, len(groups), X + 1):
        size = groups[at].shape[0] // C
        for part in groups[at : at + X]:
            table_ref[put : put + size] = part[:size]
            put += size
        table_ref[put : put + X * size] = groups[at + X][...]
        put += X * size


def before_kernel(extra, *refs):
    recv_ref, send_ref, b1_ref = refs[:3]
    parts = refs[3:7]
    edges_hbm, w1_hbm = refs[7:9]
    out_hbm, table_ref, edges_ref, w1_ref, out_ref, sems = refs[9 + extra :]
    count, latent = edges_ref.shape
    size = parts[0].shape[0]
    nodes = table_ref.shape[0]
    tile = count // BEFORE_TILES
    loads = [pltpu.make_async_copy(w1_hbm, w1_ref, sems.at[0])]
    for at in range(BEFORE_TILES):
        part = pl.ds(at * tile, tile)
        loads.append(
            pltpu.make_async_copy(edges_hbm.at[part], edges_ref.at[part], sems.at[1 + at])
        )
    for load in loads:
        load.start()
    for k, part in enumerate(parts):
        table_ref[k * size : (k + 1) * size] = part[...]
    stores = []
    for at in range(BEFORE_TILES):
        rows = slice(at * tile, (at + 1) * tile)
        own = dot_first(hot_columns(recv_ref[:, rows], nodes), table_ref[...]).astype(bf16)
        near = dot_first(hot_columns(send_ref[:, rows], nodes), table_ref[...]).astype(bf16)
        if at == 0:
            loads[0].wait()
        loads[1 + at].wait()
        total = dot(edges_ref[rows], w1_ref[:latent])
        total = total + dot(near, w1_ref[latent : 2 * latent])
        total = total + dot(own, w1_ref[2 * latent :])
        out_ref[rows] = total + b1_ref[...]
        part = pl.ds(at * tile, tile)
        stores.append(pltpu.make_async_copy(out_ref.at[part], out_hbm.at[part], sems.at[1 + BEFORE_TILES + at]))
        stores[-1].start()
    for store in stores:
        store.wait()


def edge_before(recv, send, b1, parts, edges, w1, *earlier):
    count, latent = edges.shape
    nodes = sum(part.shape[0] for part in parts)
    return pl.pallas_call(
        lambda *refs: before_kernel(len(earlier), *refs),
        in_specs=[VMEM] * 7 + [HBM] * 2 + [ANY] * len(earlier),
        out_specs=HBM,
        out_shape=pltpu.HBM((count, latent), f32),
        scratch_shapes=[
            pltpu.VMEM((nodes, latent), bf16),
            pltpu.VMEM((count, latent), bf16),
            pltpu.VMEM(w1.shape, bf16),
            pltpu.VMEM((count, latent), f32),
            pltpu.SemaphoreType.DMA((1 + 2 * BEFORE_TILES,)),
        ],
        compiler_params=pltpu.CompilerParams(vmem_limit_bytes=32 << 20),
        cost_estimate=pl.CostEstimate(flops=COST, bytes_accessed=0, transcendentals=0),
        name="edge_before",
    )(recv, send, b1, *parts, in_hbm(edges), in_hbm(w1), *earlier)


def after_kernel(first_row, *refs):
    live_ref, send_ref, recv_ref, gain_ref = refs[:4]
    count = (X + 1) * len(BATCHES)
    groups, refs = refs[4 : 4 + count], refs[4 + count :]
    before_hbm, w1_hbm, w2_hbm, edges_hbm, out_hbm = refs[:5]
    sums_refs = refs[5:9]
    table_ref, before_ref, w1_ref, w2_ref, edges_ref, far_ref, load_sems, store_sems = refs[9:]
    count, latent = edges_ref.shape
    tile = count // TILES
    loads = [
        pltpu.make_async_copy(w1_hbm.at[pl.ds(latent, latent)], w1_ref, load_sems.at[0]),
        pltpu.make_async_copy(before_hbm, before_ref, load_sems.at[1]),
        pltpu.make_async_copy(w2_hbm, w2_ref, load_sems.at[2]),
        pltpu.make_async_copy(edges_hbm, edges_ref, load_sems.at[3]),
    ]
    for load in loads:
        load.start()
    fill(table_ref, groups)
    stores = []
    live = live_ref[0]
    size = count // GATHERS
    for at in range(GATHERS):
        rows = slice(at * size, (at + 1) * size)
        hot = hot_rows(send_ref[rows], table_ref.shape[0], first_row)
        far_ref[rows] = dot(hot, table_ref[...]).astype(bf16)
    for load in loads:
        load.wait()
    for at in range(TILES):
        rows = slice(at * tile, (at + 1) * tile)
        first = before_ref[rows] + dot(far_ref[rows], w1_ref[...])
        hidden = silu(first).astype(bf16)
        change = layer_norm(dot(hidden, w2_ref[...]), gain_ref[...])
        alive = lax.broadcasted_iota(i32, (tile, 1), 0) + at * tile < live
        edge = edges_ref[rows].astype(f32) + jnp.where(alive, change, 0.0)
        edges_ref[rows] = edge.astype(bf16)
        part = pl.ds(at * tile, tile)
        stores.append(
            pltpu.make_async_copy(edges_ref.at[part], out_hbm.at[part], store_sems.at[at])
        )
        stores[-1].start()
    alive = lax.broadcasted_iota(i32, (1, count), 1) < live
    receiver = jnp.where(alive, recv_ref[...], -1)
    size = sums_refs[0].shape[0]
    for at, ref in enumerate(sums_refs):
        hot = hot_columns(receiver, size, at * size)
        ref[...] = dot(hot, edges_ref[...]).astype(ref.dtype)
    for store in stores:
        store.wait()


def edge_after(cap, first_row, live, send, recv, gain, parts, before, w1, w2, edges, rows):
    count, latent = edges.shape
    table = X * Z * C * cap
    return pl.pallas_call(
        lambda *refs: after_kernel(first_row, *refs),
        in_specs=[SMEM] + [VMEM] * (3 + len(parts)) + [HBM] * 4,
        out_specs=[HBM] + [VMEM] * 4,
        out_shape=[jax.ShapeDtypeStruct((count, latent), bf16)]
        + [jax.ShapeDtypeStruct((rows, latent), f32 if k == 0 else bf16) for k in range(4)],
        scratch_shapes=[
            pltpu.VMEM((table, latent), bf16),
            pltpu.VMEM((count, latent), f32),
            pltpu.VMEM((latent, latent), bf16),
            pltpu.VMEM((latent, latent), bf16),
            pltpu.VMEM((count, latent), bf16),
            pltpu.VMEM((count, latent), bf16),
            pltpu.SemaphoreType.DMA((4,)),
            pltpu.SemaphoreType.DMA((TILES,)),
        ],
        compiler_params=pltpu.CompilerParams(vmem_limit_bytes=32 << 20),
        name="edge_after",
    )(live, send, recv, gain, *parts, *[in_hbm(part) for part in (before, w1, w2, edges)])


def node_kernel(nodes_ref, p0_ref, p1_ref, p2_ref, p3_ref, w1_ref, b1_ref, w2_ref, gain_ref, out_ref):
    latent = nodes_ref.shape[1]
    total = p0_ref[...].astype(f32) + p1_ref[...].astype(f32)
    total = total + p2_ref[...].astype(f32) + p3_ref[...].astype(f32)
    incoming = total.astype(bf16)
    nodes = nodes_ref[...]
    first = dot(nodes, w1_ref[:latent]) + dot(incoming, w1_ref[latent:])
    hidden = silu(first + b1_ref[...]).astype(bf16)
    change = layer_norm(dot(hidden, w2_ref[...]), gain_ref[...])
    out_ref[...] = (nodes.astype(f32) + change).astype(bf16)


def node_update(nodes, parts, w1, b1, w2, gain):
    return pl.pallas_call(
        node_kernel,
        in_specs=[VMEM] * 9,
        out_shape=jax.ShapeDtypeStruct(nodes.shape, bf16),
        compiler_params=pltpu.CompilerParams(vmem_limit_bytes=LIMIT),
        name="node_update",
    )(nodes, *parts, w1, b1, w2, gain)


def pairs_of(move):
    found = []
    for x in range(X):
        for z in range(Z):
            for c in range(C):
                tx, tz, tc = move(x, z, c)
                found.append(((x * Z + z) * C + c, ((tx % X) * Z + tz % Z) * C + tc % C))
    return found


def moved(value, move):
    return lax.ppermute(value, "patch", pairs_of(move))


def local(
    nodes,
    edges,
    receivers,
    sender_slot,
    send_rows,
    live_edges,
    edge_w1,
    edge_b1,
    edge_w2,
    edge_gain,
    node_w1,
    node_b1,
    node_w2,
    node_gain,
):
    rows, latent = nodes.shape
    cap = send_rows.shape[3]
    me = lax.axis_index("patch")
    mine = lax.axis_index("feat")
    x, z, c = me // (Z * C), me // C % Z, me % C
    feat = lax.axis_size("feat")

    block = pack(me.reshape(1), send_rows[0, 0].T, nodes)
    def around(value, k):
        return lax.ppermute(value, "feat", [(i, (i + k) % feat) for i in range(feat)])

    after_one = around(nodes, 1)
    parts = [nodes, after_one, around(after_one, 1), around(nodes, feat - 1)]
    up = lambda a: moved(a, lambda x, z, c: (x, z + 1, c))
    down = lambda a: moved(a, lambda x, z, c: (x, z - 1, c))
    held = {0: block}
    forth = back = block
    for hop in range(1, 4):
        forth, back = up(forth), down(back)
        if hop < 3:
            forth = gate(forth, parts[NEAR[hop - 1]])
        held[hop], held[Z - hop] = forth, back
    held[4] = up(forth)

    groups = []
    for pairs in BATCHES:
        earlier = [parts[2]] if pairs is BATCHES[1] else []
        picked = select(pairs, cap, [held[dz] for pair in pairs for dz in pair], *earlier)
        arrived = {0: picked[0]}
        for k in range(1, X):
            arrived[k] = moved(picked[k], lambda x, z, c: (x + k, z, c))
        groups.append([arrived[k] for k in range(X)])
    swap = lambda a: moved(a, lambda x, z, c: (x, z, c + 1))

    def near_row(row):
        return ((mine - row // rows) & (feat - 1)) * rows + row % rows

    patch = feat * rows
    slot = jnp.maximum(sender_slot - patch, 0)
    source, entry = slot // cap, slot % cap
    k = (x - source // (Z * C)) & (X - 1)
    dz = (z - source // C % Z) & (Z - 1)
    s = (source - c) & (C - 1)
    place = jnp.zeros_like(slot)
    base = 0
    for pairs in BATCHES:
        for at, pair in enumerate(pairs):
            for side, value in enumerate(pair):
                size = len(pairs) * 2 * cap
                here = base + (s * X + k) * size + at * 2 * cap + side * cap
                place = jnp.where(dz == value, here, place)
        base += X * C * len(pairs) * 2 * cap
    send = jnp.where(sender_slot < patch, near_row(sender_slot), patch + place + entry)
    recv = near_row(receivers).reshape(1, -1)
    before = edge_before(
        recv, send.reshape(1, -1), edge_b1.reshape(1, -1), parts, edges, edge_w1, groups[1][0]
    )
    early = groups[0] + [swap(crossing(groups[0], in_hbm(before)))]
    late = groups[1] + [swap(crossing(groups[1], in_hbm(before)))]
    edges_out, *sums = edge_after(
        cap, patch, live_edges, send.reshape(-1, 1), recv, edge_gain.reshape(1, -1), early + late, before,
        edge_w1, edge_w2, edges, rows,
    )
    arrived = {0: sums[0]}
    for k in range(1, feat):
        arrived[k] = around(sums[k], feat - k)
    parts = [arrived[k] for k in range(feat)]
    nodes_out = node_update(
        nodes, parts, node_w1, node_b1.reshape(1, -1), node_w2, node_gain.reshape(1, -1)
    )
    return (edges_out, nodes_out)


def solution(mesh):
    placed = (
        P(("patch", "feat"), None),
        P(("patch", "feat"), None),
        P(("patch", "feat")),
        P(("patch", "feat")),
        P("patch", "feat", None, None),
        P(("patch", "feat")),
    ) + (P(),) * 8
    return jax.shard_map(
        local,
        mesh=mesh,
        in_specs=placed,
        out_specs=(P(("patch", "feat"), None), P(("patch", "feat"), None)),
        check_vma=False,
    )
```

```python
import jax
import jax.numpy as jnp
from jax import lax
from jax.experimental import pallas as pl
from jax.experimental.pallas import tpu as pltpu
from jax.sharding import PartitionSpec as P

epsilon = 1e-05
f32 = jnp.float32
bf16 = jnp.bfloat16
i32 = jnp.int32
TILES = 2
BEFORE_TILES = 2
GATHERS = 1
LIMIT = 16 << 20
VMEM = pl.BlockSpec(memory_space=pltpu.VMEM)
SMEM = pl.BlockSpec(memory_space=pltpu.SMEM)
HBM = pl.BlockSpec(memory_space=pltpu.HBM)
ANY = pl.BlockSpec(memory_space=pl.ANY)
X, Z, C = 4, 8, 2
TAIL = 16
COST = 1 << 20
NEAR = (1, 3)
BATCHES = (((0, 1), (7, 2)), ((6, 3), (5, 4)))


def dot(left, right):
    return jnp.dot(left, right, preferred_element_type=f32)


def dot_first(left, right):
    return lax.dot_general(left, right, (((0,), (0,)), ((), ())), preferred_element_type=f32)


def silu(value):
    return value / (1.0 + jnp.exp(-value))


def layer_norm(values, scales):
    average = jnp.mean(values, axis=-1, keepdims=True)
    centred = values - average
    variance = jnp.mean(centred * centred, axis=-1, keepdims=True)
    return centred * lax.rsqrt(variance + epsilon) * scales


def as_bf16(mask):
    return mask.astype(f32).astype(bf16)


def hot_columns(row, count, first=0):
    ids = lax.broadcasted_iota(i32, (count, row.shape[1]), 0) + first
    return as_bf16(row == ids)


def hot_rows(column, count, first=0):
    ids = lax.broadcasted_iota(i32, (column.shape[0], count), 1) + first
    return as_bf16(column == ids)


def in_hbm(value):
    return pltpu.with_memory_space_constraint(value, pltpu.HBM)


def odd(dz):
    return (dz >= 1) & (dz <= 4)


def pack_kernel(where_ref, lists_hbm, nodes_hbm, out_ref, lists_ref, sems):
    rows, latent = nodes_hbm.shape
    cap, peers = lists_ref.shape
    body = pltpu.make_async_copy(nodes_hbm, out_ref.at[pl.ds(0, rows)], sems.at[0])
    body.start()
    load = pltpu.make_async_copy(lists_hbm, lists_ref, sems.at[1])
    load.start()
    load.wait()
    me = where_ref[0]
    x, z, c = me // (Z * C), me // C % Z, me % C
    lane = lax.broadcasted_iota(i32, (cap, latent), 1)
    spread = as_bf16(lane % cap == lax.broadcasted_iota(i32, (cap, latent), 0))
    listed = dot_first(lists_ref[...].astype(f32).astype(bf16), spread)
    peer = lax.broadcasted_iota(i32, (peers, latent), 0)
    lane = lax.broadcasted_iota(i32, (peers, latent), 1)
    k = (peer // (Z * C) - x) & (X - 1)
    dz = (peer // C % Z - z) & (Z - 1)
    s = (peer % C - c) & (C - 1)
    slot = (k * C + s) * 2 + jnp.where(odd(dz), 1, 0)
    listed = jnp.where(lane // cap == slot, listed + 1.0, 0.0).astype(bf16)
    row = lax.broadcasted_iota(i32, (TAIL, peers), 0)
    peer = lax.broadcasted_iota(i32, (TAIL, peers), 1)
    pick = as_bf16(row == ((peer // C % Z - z) & (Z - 1)))
    out_ref[rows:] = (dot(pick, listed) - 1.0).astype(bf16)
    body.wait()


def pack(me, lists, nodes):
    return pl.pallas_call(
        pack_kernel,
        in_specs=[SMEM, HBM, HBM],
        out_specs=VMEM,
        out_shape=jax.ShapeDtypeStruct((nodes.shape[0] + TAIL, nodes.shape[1]), bf16),
        scratch_shapes=[pltpu.VMEM(lists.shape, i32), pltpu.SemaphoreType.DMA((2,))],
        compiler_params=pltpu.CompilerParams(vmem_limit_bytes=4 << 20),
        name="pack",
    )(me, in_hbm(lists), in_hbm(nodes))


def select_kernel(pairs, cap, extra, *refs):
    count = 2 * len(pairs)
    blocks, outs = list(refs[:count]), refs[count + extra : count + extra + X]
    rows = blocks[0].shape[0] - TAIL
    lanes = X * C * 2 * cap
    for at in range(len(pairs)):
        total = None
        for side, dz in enumerate(pairs[at]):
            block = blocks[2 * at + side]
            wanted = block[rows:].astype(f32)[dz : dz + 1, :lanes].astype(i32)
            part = dot_first(hot_columns(wanted, rows), block[:rows])
            total = part if total is None else total + part
        total = total.astype(bf16)
        size = 2 * cap
        for k in range(X):
            for s in range(C):
                first = (k * C + s) * size
                put = (s * len(pairs) + at) * size
                outs[k][put : put + size] = total[first : first + size]


def select(pairs, cap, blocks, *earlier):
    latent = blocks[0].shape[1]
    shape = jax.ShapeDtypeStruct((C * len(pairs) * 2 * cap, latent), bf16)
    return pl.pallas_call(
        lambda *refs: select_kernel(pairs, cap, len(earlier), *refs),
        in_specs=[VMEM] * len(blocks) + [ANY] * len(earlier),
        out_shape=[shape] * X,
        compiler_params=pltpu.CompilerParams(vmem_limit_bytes=LIMIT),
        cost_estimate=pl.CostEstimate(flops=COST, bytes_accessed=0, transcendentals=0),
        name="select",
    )(*blocks, *earlier)


def gate_kernel(*refs):
    pass


def gate(value, *earlier):
    return pl.pallas_call(
        gate_kernel,
        in_specs=[ANY] * (1 + len(earlier)),
        out_specs=ANY,
        out_shape=jax.ShapeDtypeStruct(value.shape, value.dtype),
        input_output_aliases={0: 0},
        compiler_params=pltpu.CompilerParams(vmem_limit_bytes=1 << 20),
        cost_estimate=pl.CostEstimate(flops=0, bytes_accessed=0, transcendentals=0),
        name="gate",
    )(value, *earlier)


def cross_kernel(*refs):
    out_ref = refs[-1]
    put = 0
    for ref in refs[:X]:
        size = ref.shape[0] // C
        out_ref[put : put + size] = ref[size:]
        put += size


def crossing(parts, *earlier):
    rows = sum(part.shape[0] for part in parts) // C
    return pl.pallas_call(
        cross_kernel,
        in_specs=[VMEM] * len(parts) + [HBM] * len(earlier),
        out_shape=jax.ShapeDtypeStruct((rows, parts[0].shape[1]), bf16),
        compiler_params=pltpu.CompilerParams(vmem_limit_bytes=LIMIT),
        name="crossing",
    )(*parts, *earlier)


def fill(table_ref, groups):
    put = 0
    for at in range(0, len(groups), X + 1):
        size = groups[at].shape[0] // C
        for part in groups[at : at + X]:
            table_ref[put : put + size] = part[:size]
            put += size
        table_ref[put : put + X * size] = groups[at + X][...]
        put += X * size


def before_kernel(extra, *refs):
    recv_ref, send_ref, b1_ref = refs[:3]
    parts = refs[3:7]
    edges_hbm, w1_hbm = refs[7:9]
    out_hbm, table_ref, edges_ref, w1_ref, out_ref, sems = refs[9 + extra :]
    count, latent = edges_ref.shape
    size = parts[0].shape[0]
    nodes = table_ref.shape[0]
    tile = count // BEFORE_TILES
    loads = [pltpu.make_async_copy(w1_hbm, w1_ref, sems.at[0])]
    for at in range(BEFORE_TILES):
        part = pl.ds(at * tile, tile)
        loads.append(
            pltpu.make_async_copy(edges_hbm.at[part], edges_ref.at[part], sems.at[1 + at])
        )
    for load in loads:
        load.start()
    for k, part in enumerate(parts):
        table_ref[k * size : (k + 1) * size] = part[...]
    stores = []
    for at in range(BEFORE_TILES):
        rows = slice(at * tile, (at + 1) * tile)
        own = dot_first(hot_columns(recv_ref[:, rows], nodes), table_ref[...]).astype(bf16)
        near = dot_first(hot_columns(send_ref[:, rows], nodes), table_ref[...]).astype(bf16)
        if at == 0:
            loads[0].wait()
        loads[1 + at].wait()
        total = dot(edges_ref[rows], w1_ref[:latent])
        total = total + dot(near, w1_ref[latent : 2 * latent])
        total = total + dot(own, w1_ref[2 * latent :])
        out_ref[rows] = total + b1_ref[...]
        part = pl.ds(at * tile, tile)
        stores.append(pltpu.make_async_copy(out_ref.at[part], out_hbm.at[part], sems.at[1 + BEFORE_TILES + at]))
        stores[-1].start()
    for store in stores:
        store.wait()


def edge_before(recv, send, b1, parts, edges, w1, *earlier):
    count, latent = edges.shape
    nodes = sum(part.shape[0] for part in parts)
    return pl.pallas_call(
        lambda *refs: before_kernel(len(earlier), *refs),
        in_specs=[VMEM] * 7 + [HBM] * 2 + [ANY] * len(earlier),
        out_specs=HBM,
        out_shape=pltpu.HBM((count, latent), f32),
        scratch_shapes=[
            pltpu.VMEM((nodes, latent), bf16),
            pltpu.VMEM((count, latent), bf16),
            pltpu.VMEM(w1.shape, bf16),
            pltpu.VMEM((count, latent), f32),
            pltpu.SemaphoreType.DMA((1 + 2 * BEFORE_TILES,)),
        ],
        compiler_params=pltpu.CompilerParams(vmem_limit_bytes=32 << 20),
        cost_estimate=pl.CostEstimate(flops=COST, bytes_accessed=0, transcendentals=0),
        name="edge_before",
    )(recv, send, b1, *parts, in_hbm(edges), in_hbm(w1), *earlier)


def after_kernel(first_row, *refs):
    live_ref, send_ref, recv_ref, gain_ref = refs[:4]
    count = (X + 1) * len(BATCHES)
    groups, refs = refs[4 : 4 + count], refs[4 + count :]
    before_hbm, w1_hbm, w2_hbm, edges_hbm, out_hbm = refs[:5]
    sums_refs = refs[5:9]
    table_ref, before_ref, w1_ref, w2_ref, edges_ref, far_ref, load_sems, store_sems = refs[9:]
    count, latent = edges_ref.shape
    tile = count // TILES
    loads = [
        pltpu.make_async_copy(w1_hbm.at[pl.ds(latent, latent)], w1_ref, load_sems.at[0]),
        pltpu.make_async_copy(before_hbm, before_ref, load_sems.at[1]),
        pltpu.make_async_copy(w2_hbm, w2_ref, load_sems.at[2]),
        pltpu.make_async_copy(edges_hbm, edges_ref, load_sems.at[3]),
    ]
    for load in loads:
        load.start()
    fill(table_ref, groups)
    stores = []
    live = live_ref[0]
    size = count // GATHERS
    for at in range(GATHERS):
        rows = slice(at * size, (at + 1) * size)
        hot = hot_rows(send_ref[rows], table_ref.shape[0], first_row)
        far_ref[rows] = dot(hot, table_ref[...]).astype(bf16)
    for load in loads:
        load.wait()
    for at in range(TILES):
        rows = slice(at * tile, (at + 1) * tile)
        first = before_ref[rows] + dot(far_ref[rows], w1_ref[...])
        hidden = silu(first).astype(bf16)
        change = layer_norm(dot(hidden, w2_ref[...]), gain_ref[...])
        alive = lax.broadcasted_iota(i32, (tile, 1), 0) + at * tile < live
        edge = edges_ref[rows].astype(f32) + jnp.where(alive, change, 0.0)
        edges_ref[rows] = edge.astype(bf16)
        part = pl.ds(at * tile, tile)
        stores.append(
            pltpu.make_async_copy(edges_ref.at[part], out_hbm.at[part], store_sems.at[at])
        )
        stores[-1].start()
    alive = lax.broadcasted_iota(i32, (1, count), 1) < live
    receiver = jnp.where(alive, recv_ref[...], -1)
    size = sums_refs[0].shape[0]
    for at, ref in enumerate(sums_refs):
        hot = hot_columns(receiver, size, at * size)
        ref[...] = dot(hot, edges_ref[...]).astype(ref.dtype)
    for store in stores:
        store.wait()


def edge_after(cap, first_row, live, send, recv, gain, parts, before, w1, w2, edges, rows):
    count, latent = edges.shape
    table = X * Z * C * cap
    return pl.pallas_call(
        lambda *refs: after_kernel(first_row, *refs),
        in_specs=[SMEM] + [VMEM] * (3 + len(parts)) + [HBM] * 4,
        out_specs=[HBM] + [VMEM] * 4,
        out_shape=[jax.ShapeDtypeStruct((count, latent), bf16)]
        + [jax.ShapeDtypeStruct((rows, latent), f32 if k == 0 else bf16) for k in range(4)],
        scratch_shapes=[
            pltpu.VMEM((table, latent), bf16),
            pltpu.VMEM((count, latent), f32),
            pltpu.VMEM((latent, latent), bf16),
            pltpu.VMEM((latent, latent), bf16),
            pltpu.VMEM((count, latent), bf16),
            pltpu.VMEM((count, latent), bf16),
            pltpu.SemaphoreType.DMA((4,)),
            pltpu.SemaphoreType.DMA((TILES,)),
        ],
        compiler_params=pltpu.CompilerParams(vmem_limit_bytes=32 << 20),
        name="edge_after",
    )(live, send, recv, gain, *parts, *[in_hbm(part) for part in (before, w1, w2, edges)])


def node_kernel(nodes_ref, p0_ref, p1_ref, p2_ref, p3_ref, w1_ref, b1_ref, w2_ref, gain_ref, out_ref):
    latent = nodes_ref.shape[1]
    total = p0_ref[...].astype(f32) + p1_ref[...].astype(f32)
    total = total + p2_ref[...].astype(f32) + p3_ref[...].astype(f32)
    incoming = total.astype(bf16)
    nodes = nodes_ref[...]
    first = dot(nodes, w1_ref[:latent]) + dot(incoming, w1_ref[latent:])
    hidden = silu(first + b1_ref[...]).astype(bf16)
    change = layer_norm(dot(hidden, w2_ref[...]), gain_ref[...])
    out_ref[...] = (nodes.astype(f32) + change).astype(bf16)


def node_update(nodes, parts, w1, b1, w2, gain):
    return pl.pallas_call(
        node_kernel,
        in_specs=[VMEM] * 9,
        out_shape=jax.ShapeDtypeStruct(nodes.shape, bf16),
        compiler_params=pltpu.CompilerParams(vmem_limit_bytes=LIMIT),
        name="node_update",
    )(nodes, *parts, w1, b1, w2, gain)


def pairs_of(move):
    found = []
    for x in range(X):
        for z in range(Z):
            for c in range(C):
                tx, tz, tc = move(x, z, c)
                found.append(((x * Z + z) * C + c, ((tx % X) * Z + tz % Z) * C + tc % C))
    return found


def moved(value, move):
    return lax.ppermute(value, "patch", pairs_of(move))


def local(
    nodes,
    edges,
    receivers,
    sender_slot,
    send_rows,
    live_edges,
    edge_w1,
    edge_b1,
    edge_w2,
    edge_gain,
    node_w1,
    node_b1,
    node_w2,
    node_gain,
):
    rows, latent = nodes.shape
    cap = send_rows.shape[3]
    me = lax.axis_index("patch")
    mine = lax.axis_index("feat")
    x, z, c = me // (Z * C), me // C % Z, me % C
    feat = lax.axis_size("feat")

    block = pack(me.reshape(1), send_rows[0, 0].T, nodes)
    def around(value, k):
        return lax.ppermute(value, "feat", [(i, (i + k) % feat) for i in range(feat)])

    after_one = around(nodes, 1)
    parts = [nodes, after_one, around(after_one, 1), around(nodes, feat - 1)]
    up = lambda a: moved(a, lambda x, z, c: (x, z + 1, c))
    down = lambda a: moved(a, lambda x, z, c: (x, z - 1, c))
    held = {0: block}
    forth = back = block
    for hop in range(1, 4):
        forth, back = up(forth), down(back)
        if hop == 1:
            forth = gate(forth, parts[NEAR[0]])
        if hop == 2:
            back = gate(back, parts[NEAR[1]])
        held[hop], held[Z - hop] = forth, back
    held[4] = up(forth)

    groups = []
    for pairs in BATCHES:
        earlier = [parts[2]] if pairs is BATCHES[1] else []
        picked = select(pairs, cap, [held[dz] for pair in pairs for dz in pair], *earlier)
        arrived = {0: picked[0]}
        for k in range(1, X):
            arrived[k] = moved(picked[k], lambda x, z, c: (x + k, z, c))
        groups.append([arrived[k] for k in range(X)])
    swap = lambda a: moved(a, lambda x, z, c: (x, z, c + 1))

    def near_row(row):
        return ((mine - row // rows) & (feat - 1)) * rows + row % rows

    patch = feat * rows
    slot = jnp.maximum(sender_slot - patch, 0)
    source, entry = slot // cap, slot % cap
    k = (x - source // (Z * C)) & (X - 1)
    dz = (z - source // C % Z) & (Z - 1)
    s = (source - c) & (C - 1)
    place = jnp.zeros_like(slot)
    base = 0
    for pairs in BATCHES:
        for at, pair in enumerate(pairs):
            for side, value in enumerate(pair):
                size = len(pairs) * 2 * cap
                here = base + (s * X + k) * size + at * 2 * cap + side * cap
                place = jnp.where(dz == value, here, place)
        base += X * C * len(pairs) * 2 * cap
    send = jnp.where(sender_slot < patch, near_row(sender_slot), patch + place + entry)
    recv = near_row(receivers).reshape(1, -1)
    before = edge_before(
        recv, send.reshape(1, -1), edge_b1.reshape(1, -1), parts, edges, edge_w1, groups[1][0]
    )
    early = groups[0] + [swap(crossing(groups[0], in_hbm(before)))]
    late = groups[1] + [swap(crossing(groups[1], in_hbm(before)))]
    edges_out, *sums = edge_after(
        cap, patch, live_edges, send.reshape(-1, 1), recv, edge_gain.reshape(1, -1), early + late, before,
        edge_w1, edge_w2, edges, rows,
    )
    arrived = {0: sums[0]}
    for k in range(1, feat):
        arrived[k] = around(sums[k], feat - k)
    parts = [arrived[k] for k in range(feat)]
    nodes_out = node_update(
        nodes, parts, node_w1, node_b1.reshape(1, -1), node_w2, node_gain.reshape(1, -1)
    )
    return (edges_out, nodes_out)


def solution(mesh):
    placed = (
        P(("patch", "feat"), None),
        P(("patch", "feat"), None),
        P(("patch", "feat")),
        P(("patch", "feat")),
        P("patch", "feat", None, None),
        P(("patch", "feat")),
    ) + (P(),) * 8
    return jax.shard_map(
        local,
        mesh=mesh,
        in_specs=placed,
        out_specs=(P(("patch", "feat"), None), P(("patch", "feat"), None)),
        check_vma=False,
    )
```
